32 devices in a mesh: axial: 8 (over z, x), azim: 4 (over y, core).
Axes of the slice: x: 2, y: 2, z: 4, core: 2. Of those that a mesh axis runs over, the one named last changes fastest.
Arguments:
- source: float32 [12, 32, 64, 256], P(None, 'axial', 'azim'), may hold values from -24 to 24
- storage: float32 [12, 32, 64, 256], P(None, 'axial', 'azim'), may hold values from 0.5 to 2
- materials: int32 [32, 64, 256], P('axial', 'azim'), may hold values from 0 to 3
- conductance: float32 [12], replicated, may hold values from 0.3 to 2
- mixing: float32 [4, 12, 12], replicated, may hold values from -0.9 to 0.9
- counts: int32 [8, 4], P('axial', 'azim'), may hold values from 30 to 120, as said below
- vis_owner: int32 [8, 4, 120, 4], P('axial', 'azim'), may hold values from 0 to 7, as said below
- vis_slot: int32 [8, 4, 120, 4], P('axial', 'azim'), may hold values from 0 to 119, as said below
- vis_block: int32 [8, 4, 120, 4], P('axial', 'azim'), may hold values from 0 to 7
- radiosity_old: bfloat16 [8, 4, 120, 128], P('axial', 'azim'), may hold values from -6 to 6
- view_blocks: bfloat16 [8, 128, 128], replicated, may hold values from -0.25 to 0.25
- emission: float32 [8, 4, 120, 128], P('axial', 'azim'), may hold values from 0.5 to 1.5
- reflect: float32 [8, 4, 120, 128], P('axial', 'azim'), may hold values from 0.2 to 0.8
Outputs:
- solution: float32 [12, 32, 64, 256], P(None, 'axial', 'azim')
- residual: float32 [12, 32, 64, 256], P(None, 'axial', 'azim')
- radiosity_new: float32 [8, 4, 120, 128], P('axial', 'azim')
The draws below stay inside these ranges and needn't reach their ends.
Inputs may be any that keep to these rules, and one draw needn't show every extreme that they name: Slots 0 to counts - 1 of a device hold its panels; some device has exactly 120. `vis_owner`: owners lie in the same azimuthal column as the panel. Among the entries of the live panels of one device, no owner is named more than 60 times; some device names every owner exactly 60 times, and some owner is named exactly 60 times by every device. `vis_slot`: every entry is below the count of the named owner in the same azimuthal column.
All inputs are finite; a program needn't handle non-finite values.
Results may differ from the reference program's by a relative error of at most 0.0004.
Values may be sent and summed in bfloat16 or wider, within the bound.
No kernel may reach another device: no remote copies, remote signals or barrier semaphores. Data moves between devices by JAX's collectives and lax.ppermute only.
A program may use at most 128 MiB of HBM per device.

```python
import math
import jax
import jax.numpy as jnp
from jax import lax

NF = 12
MATS = 4
VIS = 4
NB = 8
ITERS = 3
CA = 4
CZ = 16
CR = 256
PSLOT = 120
RAD = 128
NA = 32
NZ = 64
CAP = 60
N_AXIAL = 8
N_AZIM = 4


def visibility(base_key):
    seed_key = jax.random.fold_in(base_key, 4242)
    count_key, full_key, owner_key, slot_key, star_key = jax.random.split(seed_key, 5)
    total = VIS * PSLOT
    lowest = PSLOT // 4
    devices = N_AXIAL * N_AZIM
    levels = jax.random.randint(count_key, (devices,), 0, 1000)
    counts_flat = lowest + (PSLOT - lowest) * levels * levels // 1000000
    fullest = jax.random.randint(full_key, (), 0, devices)
    counts_flat = jnp.where(jnp.arange(devices) == fullest, PSLOT, counts_flat).astype(jnp.int32)
    counts = counts_flat.reshape(N_AXIAL, N_AZIM)
    starred = jax.random.randint(star_key, (), 0, N_AXIAL)
    base_owner = (jnp.arange(total) // CAP).astype(jnp.int32)

    def one_device(device_key, live_count):
        first_key, second_key = jax.random.split(device_key)
        order_one = jax.random.permutation(first_key, total)
        pool = base_owner[jnp.argsort(jnp.where(base_owner == starred, order_one - total, order_one))]
        order_two = jax.random.permutation(second_key, total)
        scores = jnp.where(jnp.arange(total) < VIS * live_count, order_two, order_two + total)
        places = jnp.argsort(scores)
        return jnp.zeros((total,), jnp.int32).at[places].set(pool)
    device_keys = jax.random.split(owner_key, devices)
    owners = jax.vmap(one_device)(device_keys, counts_flat).reshape(N_AXIAL, N_AZIM, PSLOT, VIS)
    column = jnp.arange(N_AZIM)[None, :, None, None]
    limits = counts[owners, column]
    slots = jax.random.randint(slot_key, owners.shape, 0, limits).astype(jnp.int32)
    return (counts, owners, slots)


def draw_counts(key, part):
    return visibility(key)[0]


def draw_vis_owner(key, part):
    return visibility(key)[1]


def draw_vis_slot(key, part):
    return visibility(key)[2]


def plant(values, rng, smallest, largest):
    shape = values.shape
    place = [jax.random.randint(jax.random.fold_in(rng, axis), (), 0, shape[axis]) for axis in range(len(shape))]
    values = values.at[tuple(place)].set(smallest)
    longest = shape.index(max(shape))
    place[longest] = (place[longest] + 1) % shape[longest]
    return values.at[tuple(place)].set(largest)


def shard_levels(key, dims, cuts, smallest, largest):
    loudness = 1.0
    for position, blocks in cuts:
        draws = jax.random.uniform(jax.random.fold_in(jax.random.fold_in(key, 6), position), (blocks,), jnp.float32, smallest / len(cuts), largest / len(cuts))
        loudness = loudness * jnp.repeat(jnp.exp(draws), dims[position] // blocks).reshape((-1,) + (1,) * (len(dims) - 1 - position))
    return loudness


def noise(own_key, extent, width, reach, cuts=(), held_as=jnp.bfloat16):
    factor_of = shard_levels(own_key, extent, cuts, -0.22, 0.18) if cuts else 1.0
    drawn = jax.random.normal(own_key, extent, jnp.float32) * width * factor_of
    return jnp.minimum(jnp.maximum(drawn, -reach), reach).astype(held_as)


def setup_inputs(seed: int = 0) -> dict:
    streams_of = jax.random.split(jax.random.key(seed), 14)
    return {
        "source": noise(streams_of[0], (NF, NA, NZ, CR), 4.0, 24.0, ((1, 8), (2, 4)), jnp.float32),
        "storage": jnp.clip(jnp.exp(math.log(2.0) - 1.3862944 * jax.random.uniform(streams_of[1], (NF, NA, NZ, CR), jnp.float32) ** shard_levels(streams_of[1], (NF, NA, NZ, CR), ((1, 8), (2, 4)), -0.2, 0.2)), 0.5, 2.0),
        "materials": plant(jax.random.randint(streams_of[2], (NA, NZ, CR), 0, MATS), jax.random.fold_in(streams_of[2], 1), 0, MATS - 1).astype(jnp.int32),
        "conductance": jnp.clip(jnp.exp(jax.random.uniform(streams_of[3], (NF,), jnp.float32, math.log(0.3), math.log(2.0))), 0.3, 2.0),
        "mixing": noise(streams_of[4], (MATS, NF, NF), 0.15, 0.9, (), jnp.float32),
        "counts": draw_counts(jax.random.fold_in(streams_of[13], 71), 0),
        "vis_owner": draw_vis_owner(jax.random.fold_in(streams_of[13], 71), 0),
        "vis_slot": draw_vis_slot(jax.random.fold_in(streams_of[13], 71), 0),
        "vis_block": plant(jax.random.randint(streams_of[8], (N_AXIAL, N_AZIM, PSLOT, VIS), 0, NB), jax.random.fold_in(streams_of[8], 1), 0, NB - 1).astype(jnp.int32),
        "radiosity_old": noise(streams_of[9], (N_AXIAL, N_AZIM, PSLOT, RAD), 1.0, 6.0, ((0, 8), (1, 4))),
        "view_blocks": noise(streams_of[10], (NB, RAD, RAD), (RAD * VIS) ** -0.5, 0.25),
        "emission": jnp.clip(0.5 + 1.0 * jax.random.uniform(streams_of[11], (N_AXIAL, N_AZIM, PSLOT, RAD), jnp.float32) ** shard_levels(streams_of[11], (N_AXIAL, N_AZIM, PSLOT, RAD), ((0, 8), (1, 4)), -0.2, 0.2), 0.5, 1.5),
        "reflect": jnp.clip(0.2 + 0.6 * jax.random.uniform(streams_of[12], (N_AXIAL, N_AZIM, PSLOT, RAD), jnp.float32) ** shard_levels(streams_of[12], (N_AXIAL, N_AZIM, PSLOT, RAD), ((0, 8), (1, 4)), -0.2, 0.2), 0.2, 0.8),
    }


center_value = 14.2
half_width = 13.8


def operate(field, storage, materials, conductance, mixing):
    axial_pad = jnp.pad(field, ((0, 0), (1, 1), (0, 0), (0, 0)))
    radial_pad = jnp.pad(field, ((0, 0), (0, 0), (0, 0), (1, 1)))
    beside = axial_pad[:, 2:] + axial_pad[:, :-2]
    beside = beside + jnp.roll(field, 1, axis=2) + jnp.roll(field, -1, axis=2)
    beside = beside + radial_pad[..., 2:] + radial_pad[..., :-2]
    mixed = jnp.zeros_like(field)
    for material in range(MATS):
        chosen = (materials == material).astype(jnp.float32)
        mixed = mixed + chosen[None] * jnp.einsum("fg,gazr->fazr", mixing[material], field, precision=lax.Precision.HIGHEST)
    return storage * field + mixed + conductance[:, None, None, None] * (6.0 * field - beside)


def reference(source, storage, materials, conductance, mixing, counts, vis_owner, vis_slot, vis_block, radiosity_old, view_blocks, emission, reflect):
    spread_ratio = center_value / half_width
    ratio_now = 1.0 / spread_ratio
    solution = jnp.zeros_like(source)
    residual = source
    direction = source / center_value
    for iteration in range(ITERS):
        solution = solution + direction
        residual = residual - operate(direction, storage, materials, conductance, mixing)
        ratio_next = 1.0 / (2.0 * spread_ratio - ratio_now)
        direction = (ratio_next * ratio_now) * direction + (2.0 * ratio_next / half_width) * residual
        ratio_now = ratio_next
    column = jnp.arange(N_AZIM, dtype=jnp.int32)[None, :, None, None]
    gathered = radiosity_old[vis_owner, column, vis_slot].astype(jnp.float32)
    live = jnp.arange(PSLOT, dtype=jnp.int32)[None, None, :] < counts[:, :, None]
    block_hot = ((vis_block[..., None] == jnp.arange(NB, dtype=jnp.int32)) & live[..., None, None]).astype(jnp.float32)
    grouped = jnp.einsum("azpkb,azpkr->azbpr", block_hot, gathered, precision=lax.Precision.HIGHEST)
    incoming = jnp.einsum("bij,azbpj->azpi", view_blocks.astype(jnp.float32), grouped, precision=lax.Precision.HIGHEST)
    wall = solution[0, :, :, CR - 1].reshape(N_AXIAL, CA, N_AZIM, CZ).transpose(0, 2, 1, 3).reshape(N_AXIAL, N_AZIM, CA * CZ)
    wall_temp = wall[:, :, jnp.arange(PSLOT, dtype=jnp.int32) % (CA * CZ)]
    radiosity_new = jnp.where(live[..., None], emission * wall_temp[..., None] + reflect * incoming, 0.0)
    return (solution, residual, radiosity_new)
```

```python
import functools
import jax
import jax.numpy as jnp
from jax import lax
from jax.experimental import pallas as pl
from jax.experimental.pallas import tpu as pltpu
from jax.sharding import PartitionSpec as P

center_value = 14.2
half_width = 13.8
sigma = center_value / half_width
ratio_0 = 1.0 / sigma
ratio_1 = 1.0 / (2.0 * sigma - ratio_0)
ratio_2 = 1.0 / (2.0 * sigma - ratio_1)
ALPHA = (None, ratio_1 * ratio_0, ratio_2 * ratio_1)
BETA = (None, 2.0 * ratio_1 / half_width, 2.0 * ratio_2 / half_width)
INV_CENTER = 1.0 / center_value

ROWS = 8
LINK = jnp.float16
f32, bf16 = jnp.float32, jnp.bfloat16

VMEM = pl.BlockSpec(memory_space=pltpu.VMEM)
SMEM = pl.BlockSpec(memory_space=pltpu.SMEM)
PARAMS = pltpu.CompilerParams(vmem_limit_bytes=24 * 1024 * 1024)


def mixed_part(cells, kinds, coef_two, coef_one):
    nf, rows, cr = cells.shape
    flat = cells.reshape(nf * rows, cr)
    high = flat.astype(bf16)
    low = (flat - high.astype(f32)).astype(bf16)
    out = jnp.dot(coef_two, jnp.concatenate([high, high], axis=0), preferred_element_type=f32)
    out = out + jnp.dot(coef_one, low, preferred_element_type=f32)
    mats = out.shape[0] // (nf * rows)
    out = out.reshape(mats, nf, rows, cr)
    picked = out[mats - 1]
    for m in range(mats - 1):
        picked = jnp.where((kinds == m)[None], out[m], picked)
    return picked


def radial_sum(cells):
    cr = cells.shape[-1]
    lane = lax.broadcasted_iota(jnp.int32, cells.shape, cells.ndim - 1)
    inner = jnp.where(lane == 0, 0.0, pltpu.roll(cells, 1, cells.ndim - 1))
    outer = jnp.where(lane == cr - 1, 0.0, pltpu.roll(cells, cr - 1, cells.ndim - 1))
    return inner + outer


def azim_sum(cells):
    rows = cells.shape[1]
    return pltpu.roll(cells, 1, 1) + pltpu.roll(cells, rows - 1, 1)


def apply_local(planes, store, kinds, cond, coef_two, coef_one, tiles, emit):
    ca = len(planes)
    for a in range(ca):
        around = azim_sum(planes[a])
        if a > 0:
            around = around + planes[a - 1]
        if a + 1 < ca:
            around = around + planes[a + 1]
        for t in tiles:
            rows = slice(t * ROWS, (t + 1) * ROWS)
            cells = planes[a][:, rows]
            beside = around[:, rows] + radial_sum(cells)
            image = store(a, t) * cells + mixed_part(cells, kinds(a, t), coef_two, coef_one)
            emit(a, t, image - cond * beside)


def first_kernel(
    even_ref, source_ref, store_ref, kinds_ref, wing_ref, wing_kinds_ref, mix_ref, cond_ref,
    rest_ref, next_ref, edge1_ref, edge0_ref, two_ref, one_ref,
):
    nf, ca, cz, cr = source_ref.shape
    own = cz // ROWS
    mixes = mix_ref[...]
    high = mixes.astype(bf16)
    low = (mixes - high.astype(f32)).astype(bf16)
    wide = mixes.shape[0] * ROWS
    inner = nf * ROWS
    row = lax.broadcasted_iota(jnp.int32, (wide, mixes.shape[0]), 0)
    col = lax.broadcasted_iota(jnp.int32, (wide, mixes.shape[0]), 1)
    down = (row // ROWS == col).astype(bf16)
    row = lax.broadcasted_iota(jnp.int32, (mixes.shape[1], inner), 0)
    col = lax.broadcasted_iota(jnp.int32, (mixes.shape[1], inner), 1)
    across = (col // ROWS == row).astype(bf16)
    row = lax.broadcasted_iota(jnp.int32, (wide, inner), 0)
    col = lax.broadcasted_iota(jnp.int32, (wide, inner), 1)
    same = row % ROWS == col % ROWS

    def spread(part):
        tall = jnp.dot(down, part, preferred_element_type=f32).astype(bf16)
        full = jnp.dot(tall, across, preferred_element_type=f32)
        return jnp.where(same, full, 0.0).astype(bf16)

    coef_one = spread(high)
    coef_two = jnp.concatenate([coef_one, spread(low)], axis=1)
    one_ref[...] = coef_one
    two_ref[...] = coef_two

    cond = cond_ref[...]
    planes = [
        jnp.concatenate([source_ref[:, a] * INV_CENTER, wing_ref[0, :, a]], axis=1)
        for a in range(ca)
    ]

    def store(a, t):
        return store_ref[:, a, t * ROWS : (t + 1) * ROWS] if t < own else wing_ref[1, :, a]

    def kinds(a, t):
        return kinds_ref[a, t * ROWS : (t + 1) * ROWS] if t < own else wing_kinds_ref[a]

    def emit(a, t, image):
        rows = slice(t * ROWS, (t + 1) * ROWS)
        direction = planes[a][:, rows]
        if t < own:
            rest = source_ref[:, a, rows] - image
        else:
            rest = center_value * direction - image
        rest_ref[:, a, rows] = rest
        next_ref[:, a, rows] = ALPHA[1] * direction + BETA[1] * rest

    apply_local(planes, store, kinds, cond, coef_two, coef_one, range(own + 1), emit)

    even = even_ref[0] == 1
    for ref, first in ((edge1_ref, True), (edge0_ref, False)):
        below, above = (0, ca - 1) if first else (ca - 1, 0)
        ref[:, :cz] = jnp.where(even, next_ref[:, below, :cz], next_ref[:, above, :cz])
        ahead = jnp.where(even, next_ref[:, below, cz:], next_ref[:, above, cz:])
        wing = jnp.where(even, wing_ref[0, :, below], wing_ref[0, :, above])
        place = lax.broadcasted_iota(jnp.int32, wing.shape, 1)
        moved = jnp.where(place < 4, pltpu.roll(wing, 2, 1), pltpu.roll(wing, 6, 1))
        ref[:, cz:] = jnp.where((place >= 2) & (place <= 5), moved, ahead)


def second_kernel(
    even_ref, rest_ref, next_ref, halo1_ref, halo0_ref, store_ref, kinds_ref, cond_ref, two_ref, one_ref,
    newrest_ref, dir_ref, newnext_ref, edge1_ref, edge0_ref,
):
    nf, ca, cz, cr = store_ref.shape
    own = cz // ROWS
    even = even_ref[0] == 1
    cond = cond_ref[...]
    wide = jnp.concatenate([cond] * own, axis=1)
    h1, h0 = halo1_ref[...], halo0_ref[...]
    low = wide * jnp.where(even, h1, h0)
    high = wide * jnp.where(even, h0, h1)
    arrived = {0: low, ca - 1: high}
    dir_ref[...] = next_ref[...]
    dir_ref[:, 0, :cz] += BETA[1] * low
    dir_ref[:, ca - 1, :cz] += BETA[1] * high
    planes = [dir_ref[:, a] for a in range(ca)]
    coef_two, coef_one = two_ref[...], one_ref[...]

    def store(a, t):
        return store_ref[:, a, t * ROWS : (t + 1) * ROWS]

    def kinds(a, t):
        return kinds_ref[a, t * ROWS : (t + 1) * ROWS]

    def emit(a, t, image):
        rows = slice(t * ROWS, (t + 1) * ROWS)
        rest = rest_ref[:, a, rows] - image
        if a in arrived:
            rest = rest + arrived[a][:, rows]
        newrest_ref[:, a, rows] = rest
        newnext_ref[:, a, rows] = ALPHA[2] * planes[a][:, rows] + BETA[2] * rest

    apply_local(planes, store, kinds, cond, coef_two, coef_one, range(own), emit)
    edge1_ref[...] = jnp.where(even, newnext_ref[:, 0], newnext_ref[:, ca - 1])
    edge0_ref[...] = jnp.where(even, newnext_ref[:, ca - 1], newnext_ref[:, 0])


def third_kernel(
    even_ref, live_ref, rest_ref, next_ref, halo1_ref, halo0_ref, dir_ref, first_rest_ref, source_ref, store_ref,
    kinds_ref, wing_ref, wing_kinds_ref, cond_ref, two_ref, one_ref, incoming_ref, emission_ref, reflect_ref,
    out_ref, solution_ref, panel_ref,
):
    nf, ca, cz, cr = source_ref.shape
    own = cz // ROWS
    even = even_ref[0] == 1
    cond = cond_ref[...]
    wide = jnp.concatenate([cond] * own, axis=1)
    h1, h0 = halo1_ref[...], halo0_ref[...]
    halo = {0: jnp.where(even, h1, h0), ca - 1: jnp.where(even, h0, h1)}
    coef_two, coef_one = two_ref[...], one_ref[...]

    place = lax.broadcasted_iota(jnp.int32, (nf, cz, cr), 1)
    rests, dirs = {}, {}
    fix = {}
    side = lax.broadcasted_iota(jnp.int32, (nf, ROWS, cr), 1)
    for a in range(ca):
        if a not in halo:
            dirs[a] = next_ref[:, a]
            continue
        old = halo[a][:, cz:]
        moved = jnp.where(side < 4, pltpu.roll(old, ROWS - 2, 1), pltpu.roll(old, 2, 1))
        fix[a] = cond * jnp.where((side <= 1) | (side >= 6), moved, 0.0)
        turned = pltpu.roll(fix[a], 1, 1)
        back = pltpu.roll(fix[a], ROWS - 1, 1)
        ends = [jnp.where(side == 0, turned, 0.0)]
        ends += [jnp.zeros_like(turned)] * (own - 2)
        ends += [jnp.where(side == ROWS - 1, back, 0.0)]
        added = wide * (halo[a][:, :cz] + BETA[1] * jnp.concatenate(ends, axis=1))
        rests[a] = added
        dirs[a] = next_ref[:, a] + BETA[2] * added

    has_partner = {0: even_ref[1] == 1, ca - 1: even_ref[2] == 1}
    second = [dir_ref[:, a] for a in range(ca)]
    for a in fix:
        second[a] = jnp.concatenate([second[a][:, :cz], second[a][:, cz:] + BETA[1] * fix[a]], axis=1)
    planes = [None] * ca

    def wing_store(a, t):
        return wing_ref[1, :, a]

    def wing_kinds(a, t):
        return wing_kinds_ref[a]

    def wing_emit(a, t, image):
        rest = first_rest_ref[:, a, cz:] - image
        if a in fix:
            beyond = halo[a][:, cz:] + BETA[1] * cond * wing_ref[0, :, a]
            rest = rest + fix[a] + jnp.where(has_partner[a], cond * beyond, 0.0)
        ahead = ALPHA[2] * second[a][:, cz:] + BETA[2] * rest
        planes[a] = jnp.concatenate([dirs[a], ahead], axis=1)

    apply_local(second, wing_store, wing_kinds, cond, coef_two, coef_one, (own,), wing_emit)

    def store(a, t):
        return store_ref[:, a, t * ROWS : (t + 1) * ROWS]

    def kinds(a, t):
        return kinds_ref[a, t * ROWS : (t + 1) * ROWS]

    def emit(a, t, image):
        rows = slice(t * ROWS, (t + 1) * ROWS)
        rest = rest_ref[:, a, rows] - image
        if a in rests:
            rest = rest + rests[a][:, rows]
        out_ref[:, a, rows] = rest
        solution_ref[:, a, rows] = (
            source_ref[:, a, rows] * INV_CENTER + dir_ref[:, a, rows] + planes[a][:, rows]
        )

    apply_local(planes, store, kinds, cond, coef_two, coef_one, range(own), emit)

    slots, values = emission_ref.shape
    wall = solution_ref[0].reshape(ca * cz, cr)[:, cr - 1 : cr]
    wall = jnp.broadcast_to(wall, (ca * cz, values))
    wall = jnp.concatenate([wall] * (-(-slots // (ca * cz))), axis=0)[:slots]
    panel = lax.broadcasted_iota(jnp.int32, (slots, values), 0)
    fresh = emission_ref[...] * wall + reflect_ref[...] * incoming_ref[...]
    panel_ref[...] = jnp.where(panel < live_ref[0], fresh, 0.0)


def last_kernel(even_ref, rest_ref, halo1_ref, halo0_ref, cond_ref, out_ref):
    nf, ca, cz, cr = rest_ref.shape
    even = even_ref[0] == 1
    wide = jnp.concatenate([cond_ref[...]] * (cz // ROWS), axis=1)
    h1, h0 = halo1_ref[...], halo0_ref[...]
    for a in range(1, ca - 1):
        out_ref[:, a] = rest_ref[:, a]
    out_ref[:, 0] = rest_ref[:, 0] + wide * jnp.where(even, h1, h0)
    out_ref[:, ca - 1] = rest_ref[:, ca - 1] + wide * jnp.where(even, h0, h1)


def panel_kernel(chunk, index_ref, block_ref, rows_ref, view_ref, out_ref):
    slots, visible = index_ref.shape
    total, values = rows_ref.shape
    index = index_ref[...]
    block = block_ref[...]
    types = view_ref.shape[0]
    lane = lax.broadcasted_iota(jnp.int32, (slots, chunk), 1)

    def gather(start):
        rows = rows_ref[pl.ds(start, chunk), :]
        return tuple(
            jnp.dot(
                (index[:, k : k + 1] == lane + start).astype(f32).astype(bf16),
                rows,
                preferred_element_type=f32,
            )
            for k in range(visible)
        )

    if total == chunk:
        found = gather(0)
    else:
        zero = tuple(jnp.zeros((slots, values), f32) for _ in range(visible))

        def step(i, sums):
            return tuple(s + g for s, g in zip(sums, gather(pl.multiple_of(i * chunk, chunk))))

        found = lax.fori_loop(0, total // chunk, step, zero)
    out = jnp.zeros((slots, values), f32)
    for b in range(types):
        stack = jnp.concatenate(
            [jnp.where(block[:, k : k + 1] == b, found[k], 0.0) for k in range(visible)], axis=0
        ).astype(bf16)
        moved = lax.dot_general(
            stack, view_ref[b], (((1,), (1,)), ((), ())), preferred_element_type=f32
        )
        for k in range(visible):
            out = out + moved[k * slots : (k + 1) * slots]
    out_ref[...] = out


def pairs(count, first, closed):
    swaps = []
    for i in range(first, count if closed and first else count - 1, 2):
        j = (i + 1) % count
        swaps += [(i, j), (j, i)]
    return swaps


def swap(array, axis, first, closed=False):
    return lax.ppermute(array, axis, pairs(lax.axis_size(axis), first, closed))


def body(
    source, storage, materials, conductance, mixing, counts, vis_owner, vis_slot, vis_block,
    radiosity_old, view_blocks, emission, reflect,
):
    nf, ca, cz, cr = source.shape
    mats = mixing.shape[0]
    owners = lax.axis_size("axial")
    me = lax.axis_index("axial")
    is_even = me % 2 == 0
    even = jnp.stack([is_even, me > 0, me + 1 < owners]).astype(jnp.int32)
    azim_even = lax.axis_index("azim") % 2 == 0
    shape = jax.ShapeDtypeStruct
    call = functools.partial(pl.pallas_call, compiler_params=PARAMS)

    half = ROWS // 2
    bundle = jnp.concatenate(
        [source * INV_CENTER, storage, materials[None].astype(f32)], axis=0
    )
    to_right = bundle[:, :, cz - half :].astype(LINK)
    to_left = bundle[:, :, :half].astype(LINK)
    near = jnp.where(azim_even, to_right, to_left)
    far = jnp.where(azim_even, to_left, to_right)
    far_in = swap(far, "azim", 1, True)
    layer_low, layer_high = source[:, 0] * INV_CENTER, source[:, ca - 1] * INV_CENTER
    halo1 = swap(jnp.where(is_even, layer_low, layer_high).astype(LINK), "axial", 1)
    near_in = swap(near, "azim", 0)
    halo0 = swap(jnp.where(is_even, layer_high, layer_low).astype(LINK), "axial", 0)
    from_right = jnp.where(azim_even, near_in, far_in)
    from_left = jnp.where(azim_even, far_in, near_in)
    wings = jnp.concatenate([from_right, from_left], axis=2).astype(f32)
    wing = wings[: 2 * nf].reshape(2, nf, ca, ROWS, cr)
    wing_kinds = wings[2 * nf].astype(jnp.int32)

    cond = jnp.broadcast_to(conductance[:, None, None], (nf, ROWS, cr))
    mixes = mixing + 6.0 * jnp.diag(conductance)
    mixes = jnp.pad(mixes.reshape(mats * nf, nf), ((0, 0), (0, 128 - nf)))
    full = shape((nf, ca, cz + ROWS, cr), f32)
    plain = shape((nf, ca, cz, cr), f32)
    tall = shape((nf, cz + ROWS, cr), f32)
    layer = shape((nf, cz, cr), f32)
    rest, ahead, edge1, edge0, two, one = call(
        first_kernel,
        out_shape=(
            full, full, tall, tall,
            shape((mats * nf * ROWS, 2 * nf * ROWS), bf16), shape((mats * nf * ROWS, nf * ROWS), bf16),
        ),
        in_specs=[SMEM] + [VMEM] * 7,
        out_specs=(VMEM,) * 6,
    )(even, source, storage, materials, wing, wing_kinds, mixes, cond)

    wide = conductance[:, None, None]

    def grown(edge, halo):
        return (edge + jnp.pad(BETA[1] * wide * halo, ((0, 0), (0, ROWS), (0, 0)))).astype(LINK)

    halo1, halo0 = halo1.astype(f32), halo0.astype(f32)
    second1 = swap(grown(edge1, halo1), "axial", 1).astype(f32)
    second0 = swap(grown(edge0, halo0), "axial", 0).astype(f32)

    slots, visible = vis_owner.shape[2:]
    values = radiosity_old.shape[3]
    tile = -(-slots // 16) * 16
    panels = jnp.pad(radiosity_old[0, 0], ((0, tile - slots), (0, 0)))
    if owners & (owners - 1) == 0:
        step = 1
        while step < owners:
            other = lax.ppermute(panels, "axial", [(i, i ^ step) for i in range(owners)])
            panels = jnp.concatenate([panels, other], axis=0)
            step *= 2
        owner = vis_owner[0, 0] ^ me
    else:
        panels = lax.all_gather(panels, "axial", axis=0, tiled=True)
        owner = vis_owner[0, 0]
    live_count = counts[0]
    index = owner * tile + vis_slot[0, 0]
    chunk = tile * 8 if owners % 8 == 0 else tile * owners
    incoming = call(
        functools.partial(panel_kernel, chunk),
        out_shape=shape((slots, values), f32),
        in_specs=[VMEM] * 4,
        out_specs=VMEM,
    )(index, vis_block[0, 0], panels, view_blocks)

    rest2, dir2, ahead2, edge1, edge0 = call(
        second_kernel,
        out_shape=(plain, full, plain, layer, layer),
        in_specs=[SMEM] + [VMEM] * 9,
        out_specs=(VMEM,) * 5,
    )(even, rest, ahead, halo1, halo0, storage, materials, cond, two, one)

    def grown_again(edge, halo):
        old = BETA[1] * wide * halo[:, cz:]
        zero = jnp.zeros((nf, cz - 2, cr), f32)
        ends = jnp.concatenate([old[:, 5:6], zero, old[:, 2:3]], axis=1)
        return (edge + BETA[2] * wide * (halo[:, :cz] + ends)).astype(LINK)

    third1 = swap(grown_again(edge1, second1), "axial", 1).astype(f32)
    third0 = swap(grown_again(edge0, second0), "axial", 0).astype(f32)

    rest3, solution_out, panel_new = call(
        third_kernel,
        out_shape=(plain, plain, shape((slots, values), f32)),
        in_specs=[SMEM] * 2 + [VMEM] * 17,
        out_specs=(VMEM,) * 3,
    )(
        even, live_count, rest2, ahead2, second1, second0, dir2, rest, source, storage, materials,
        wing, wing_kinds, cond, two, one, incoming, emission[0, 0], reflect[0, 0],
    )
    residual = call(
        last_kernel,
        out_shape=plain,
        in_specs=[SMEM] + [VMEM] * 4,
        out_specs=VMEM,
    )(even, rest3, third1, third0, cond)
    return (solution_out, residual, panel_new[None, None])


def solution(mesh):
    return jax.shard_map(
        body,
        mesh=mesh,
        in_specs=(
            P(None, "axial", "azim", None),
            P(None, "axial", "azim", None),
            P("axial", "azim", None),
            P(),
            P(),
            P("axial", "azim"),
            P("axial", "azim", None, None),
            P("axial", "azim", None, None),
            P("axial", "azim", None, None),
            P("axial", "azim", None, None),
            P(),
            P("axial", "azim", None, None),
            P("axial", "azim", None, None),
        ),
        out_specs=(
            P(None, "axial", "azim", None),
            P(None, "axial", "azim", None),
            P("axial", "azim", None, None),
        ),
        check_vma=False,
    )
```

```python
import functools
import jax
import jax.numpy as jnp
from jax import lax
from jax.experimental import pallas as pl
from jax.experimental.pallas import tpu as pltpu
from jax.sharding import PartitionSpec as P

center_value = 14.2
half_width = 13.8
sigma = center_value / half_width
ratio_0 = 1.0 / sigma
ratio_1 = 1.0 / (2.0 * sigma - ratio_0)
ratio_2 = 1.0 / (2.0 * sigma - ratio_1)
ALPHA = (None, ratio_1 * ratio_0, ratio_2 * ratio_1)
BETA = (None, 2.0 * ratio_1 / half_width, 2.0 * ratio_2 / half_width)
INV_CENTER = 1.0 / center_value

ROWS = 8
LINK = jnp.float16
RAD_SCALE = 8192.0
f32, bf16 = jnp.float32, jnp.bfloat16

VMEM = pl.BlockSpec(memory_space=pltpu.VMEM)
SMEM = pl.BlockSpec(memory_space=pltpu.SMEM)
PARAMS = pltpu.CompilerParams(vmem_limit_bytes=16 * 1024 * 1024)


def mixed_part(cells, kinds, coef_two, coef_one):
    nf, rows, cr = cells.shape
    flat = cells.reshape(nf * rows, cr)
    high = flat.astype(bf16)
    low = (flat - high.astype(f32)).astype(bf16)
    out = jnp.dot(coef_two, jnp.concatenate([high, high], axis=0), preferred_element_type=f32)
    out = out + jnp.dot(coef_one, low, preferred_element_type=f32)
    mats = out.shape[0] // (nf * rows)
    out = out.reshape(mats, nf, rows, cr)
    picked = out[mats - 1]
    for m in range(mats - 1):
        picked = jnp.where((kinds == m)[None], out[m], picked)
    return picked


def radial_sum(cells):
    cr = cells.shape[-1]
    lane = lax.broadcasted_iota(jnp.int32, cells.shape, cells.ndim - 1)
    inner = jnp.where(lane == 0, 0.0, pltpu.roll(cells, 1, cells.ndim - 1))
    outer = jnp.where(lane == cr - 1, 0.0, pltpu.roll(cells, cr - 1, cells.ndim - 1))
    return inner + outer


def azim_sum(cells):
    rows = cells.shape[1]
    return pltpu.roll(cells, 1, 1) + pltpu.roll(cells, rows - 1, 1)


def apply_local(planes, store, kinds, cond, coef_two, coef_one, tiles, emit):
    ca = len(planes)
    for a in range(ca):
        around = azim_sum(planes[a])
        if a > 0:
            around = around + planes[a - 1]
        if a + 1 < ca:
            around = around + planes[a + 1]
        for t in tiles:
            rows = slice(t * ROWS, (t + 1) * ROWS)
            cells = planes[a][:, rows]
            beside = around[:, rows] + radial_sum(cells)
            image = store(a, t) * cells + mixed_part(cells, kinds(a, t), coef_two, coef_one)
            emit(a, t, image - cond * beside)


def first_kernel(
    even_ref, source_ref, store_ref, kinds_ref, wing_ref, wing_kinds_ref, mix_ref, cond_ref,
    rest_ref, edge_ref, two_ref, one_ref,
):
    nf, ca, cz, cr = source_ref.shape
    own = cz // ROWS
    mixes = mix_ref[...]
    high = mixes.astype(bf16)
    low = (mixes - high.astype(f32)).astype(bf16)
    wide = mixes.shape[0] * ROWS
    inner = nf * ROWS
    row = lax.broadcasted_iota(jnp.int32, (wide, mixes.shape[0]), 0)
    col = lax.broadcasted_iota(jnp.int32, (wide, mixes.shape[0]), 1)
    down = (row // ROWS == col).astype(bf16)
    row = lax.broadcasted_iota(jnp.int32, (mixes.shape[1], inner), 0)
    col = lax.broadcasted_iota(jnp.int32, (mixes.shape[1], inner), 1)
    across = (col // ROWS == row).astype(bf16)
    row = lax.broadcasted_iota(jnp.int32, (wide, inner), 0)
    col = lax.broadcasted_iota(jnp.int32, (wide, inner), 1)
    same = row % ROWS == col % ROWS

    def spread(part):
        tall = jnp.dot(down, part, preferred_element_type=f32).astype(bf16)
        full = jnp.dot(tall, across, preferred_element_type=f32)
        return jnp.where(same, full, 0.0).astype(bf16)

    coef_one = spread(high)
    coef_two = jnp.concatenate([coef_one, spread(low)], axis=1)
    one_ref[...] = coef_one
    two_ref[...] = coef_two

    cond = cond_ref[...]
    planes = [
        jnp.concatenate([source_ref[:, a] * INV_CENTER, wing_ref[0, :, a]], axis=1)
        for a in range(ca)
    ]

    def store(a, t):
        return store_ref[:, a, t * ROWS : (t + 1) * ROWS] if t < own else wing_ref[1, :, a]

    def kinds(a, t):
        return kinds_ref[a, t * ROWS : (t + 1) * ROWS] if t < own else wing_kinds_ref[a]

    slot = {0: 1 - even_ref[0], ca - 1: even_ref[0]}
    place = lax.broadcasted_iota(jnp.int32, (nf, ROWS, cr), 1)

    def emit(a, t, image):
        rows = slice(t * ROWS, (t + 1) * ROWS)
        direction = planes[a][:, rows]
        if t < own:
            rest = source_ref[:, a, rows] - image
        else:
            rest = center_value * direction - image
        rest_ref[:, a, rows] = rest
        if a in slot:
            ahead = ALPHA[1] * direction + BETA[1] * rest
            if t == own:
                moved = jnp.where(place < 4, pltpu.roll(direction, 2, 1), pltpu.roll(direction, 6, 1))
                ahead = jnp.where((place >= 2) & (place <= 5), moved, ahead)
            edge_ref[slot[a], :, rows] = ahead

    apply_local(planes, store, kinds, cond, coef_two, coef_one, range(own + 1), emit)


def second_kernel(
    even_ref, rest_ref, halo1_ref, halo0_ref, source_ref, store_ref, kinds_ref, wing_ref, cond_ref, two_ref, one_ref,
    newrest_ref, dir_ref, edge_ref,
):
    nf, ca, cz, cr = store_ref.shape
    own = cz // ROWS
    even = even_ref[0] == 1
    cond = cond_ref[...]
    wide = jnp.concatenate([cond] * own, axis=1)
    h1, h0 = halo1_ref[...], halo0_ref[...]
    arrived = {0: wide * jnp.where(even, h1, h0), ca - 1: wide * jnp.where(even, h0, h1)}
    for a in range(ca):
        rest = rest_ref[:, a, :cz]
        if a in arrived:
            rest = rest + arrived[a]
        dir_ref[:, a, :cz] = (ALPHA[1] * INV_CENTER) * source_ref[:, a] + BETA[1] * rest
        dir_ref[:, a, cz:] = ALPHA[1] * wing_ref[0, :, a] + BETA[1] * rest_ref[:, a, cz:]
    planes = [dir_ref[:, a] for a in range(ca)]
    coef_two, coef_one = two_ref[...], one_ref[...]
    slot = {0: 1 - even_ref[0], ca - 1: even_ref[0]}

    def store(a, t):
        return store_ref[:, a, t * ROWS : (t + 1) * ROWS]

    def kinds(a, t):
        return kinds_ref[a, t * ROWS : (t + 1) * ROWS]

    def emit(a, t, image):
        rows = slice(t * ROWS, (t + 1) * ROWS)
        rest = rest_ref[:, a, rows] - image
        if a in arrived:
            rest = rest + arrived[a][:, rows]
        newrest_ref[:, a, rows] = rest
        if a in slot:
            edge_ref[slot[a], :, rows] = ALPHA[2] * planes[a][:, rows] + BETA[2] * rest

    apply_local(planes, store, kinds, cond, coef_two, coef_one, range(own), emit)


def third_kernel(
    even_ref, live_ref, rest_ref, halo1_ref, halo0_ref, dir_ref, first_rest_ref, source_ref, store_ref,
    kinds_ref, wing_ref, wing_kinds_ref, cond_ref, two_ref, one_ref, incoming_ref, emission_ref, reflect_ref,
    out_ref, solution_ref, panel_ref,
):
    nf, ca, cz, cr = source_ref.shape
    own = cz // ROWS
    even = even_ref[0] == 1
    cond = cond_ref[...]
    wide = jnp.concatenate([cond] * own, axis=1)
    h1, h0 = halo1_ref[...], halo0_ref[...]
    halo = {0: jnp.where(even, h1, h0), ca - 1: jnp.where(even, h0, h1)}
    coef_two, coef_one = two_ref[...], one_ref[...]

    place = lax.broadcasted_iota(jnp.int32, (nf, cz, cr), 1)
    rests, dirs = {}, {}
    fix = {}
    side = lax.broadcasted_iota(jnp.int32, (nf, ROWS, cr), 1)
    for a in range(ca):
        ahead = ALPHA[2] * dir_ref[:, a, :cz] + BETA[2] * rest_ref[:, a]
        if a not in halo:
            dirs[a] = ahead
            continue
        old = halo[a][:, cz:]
        moved = jnp.where(side < 4, pltpu.roll(old, ROWS - 2, 1), pltpu.roll(old, 2, 1))
        fix[a] = cond * jnp.where((side <= 1) | (side >= 6), moved, 0.0)
        turned = pltpu.roll(fix[a], 1, 1)
        back = pltpu.roll(fix[a], ROWS - 1, 1)
        ends = [jnp.where(side == 0, turned, 0.0)]
        ends += [jnp.zeros_like(turned)] * (own - 2)
        ends += [jnp.where(side == ROWS - 1, back, 0.0)]
        added = wide * (halo[a][:, :cz] + BETA[1] * jnp.concatenate(ends, axis=1))
        rests[a] = added
        dirs[a] = ahead + BETA[2] * added

    has_partner = {0: even_ref[1] == 1, ca - 1: even_ref[2] == 1}
    second = [dir_ref[:, a] for a in range(ca)]
    for a in fix:
        second[a] = jnp.concatenate([second[a][:, :cz], second[a][:, cz:] + BETA[1] * fix[a]], axis=1)
    planes = [None] * ca

    def wing_store(a, t):
        return wing_ref[1, :, a]

    def wing_kinds(a, t):
        return wing_kinds_ref[a]

    def wing_emit(a, t, image):
        rest = first_rest_ref[:, a, cz:] - image
        if a in fix:
            beyond = halo[a][:, cz:] + BETA[1] * cond * wing_ref[0, :, a]
            rest = rest + fix[a] + jnp.where(has_partner[a], cond * beyond, 0.0)
        beside = ALPHA[2] * second[a][:, cz:] + BETA[2] * rest
        planes[a] = jnp.concatenate([dirs[a], beside], axis=1)

    apply_local(second, wing_store, wing_kinds, cond, coef_two, coef_one, (own,), wing_emit)

    def store(a, t):
        return store_ref[:, a, t * ROWS : (t + 1) * ROWS]

    def kinds(a, t):
        return kinds_ref[a, t * ROWS : (t + 1) * ROWS]

    def emit(a, t, image):
        rows = slice(t * ROWS, (t + 1) * ROWS)
        rest = rest_ref[:, a, rows] - image
        if a in rests:
            rest = rest + rests[a][:, rows]
        out_ref[:, a, rows] = rest
        solution_ref[:, a, rows] = (
            source_ref[:, a, rows] * INV_CENTER + dir_ref[:, a, rows] + planes[a][:, rows]
        )

    apply_local(planes, store, kinds, cond, coef_two, coef_one, range(own), emit)

    slots, values = emission_ref.shape
    wall = solution_ref[0].reshape(ca * cz, cr)[:, cr - 1 : cr]
    wall = jnp.broadcast_to(wall, (ca * cz, values))
    wall = jnp.concatenate([wall] * (-(-slots // (ca * cz))), axis=0)[:slots]
    panel = lax.broadcasted_iota(jnp.int32, (slots, values), 0)
    fresh = emission_ref[...] * wall + reflect_ref[...] * incoming_ref[:slots]
    panel_ref[...] = jnp.where(panel < live_ref[0], fresh, 0.0)


def last_kernel(even_ref, rest_ref, halo1_ref, halo0_ref, cond_ref, out_ref):
    nf, ca, cz, cr = rest_ref.shape
    even = even_ref[0] == 1
    wide = jnp.concatenate([cond_ref[...]] * (cz // ROWS), axis=1)
    h1, h0 = halo1_ref[...], halo0_ref[...]
    for a in range(1, ca - 1):
        out_ref[:, a] = rest_ref[:, a]
    out_ref[:, 0] = rest_ref[:, 0] + wide * jnp.where(even, h1, h0)
    out_ref[:, ca - 1] = rest_ref[:, ca - 1] + wide * jnp.where(even, h0, h1)


def panel_kernel(chunk, visible, index_ref, block_ref, rows_ref, view_ref, out_ref):
    slots = index_ref.shape[1]
    total, values = rows_ref.shape
    index = index_ref[...].T
    block = block_ref[...].T
    types = view_ref.shape[0]
    lane = lax.broadcasted_iota(jnp.int32, (slots, chunk), 1)

    def gather(start):
        rows = rows_ref[pl.ds(start, chunk), :]
        return tuple(
            jnp.dot(
                (index[:, k : k + 1] == lane + start).astype(f32).astype(bf16),
                rows,
                preferred_element_type=f32,
            )
            for k in range(visible)
        )

    if total == chunk:
        found = gather(0)
    else:
        zero = tuple(jnp.zeros((slots, values), f32) for _ in range(visible))

        def step(i, sums):
            return tuple(s + g for s, g in zip(sums, gather(pl.multiple_of(i * chunk, chunk))))

        found = lax.fori_loop(0, total // chunk, step, zero)
    out = jnp.zeros((slots, values), f32)
    for b in range(types):
        stack = jnp.concatenate(
            [jnp.where(block[:, k : k + 1] == b, found[k], 0.0) for k in range(visible)], axis=0
        ).astype(bf16)
        moved = lax.dot_general(
            stack, view_ref[b], (((1,), (1,)), ((), ())), preferred_element_type=f32
        )
        for k in range(visible):
            out = out + moved[k * slots : (k + 1) * slots]
    out_ref[...] = out


def pairs(count, first, closed):
    swaps = []
    for i in range(first, count if closed and first else count - 1, 2):
        j = (i + 1) % count
        swaps += [(i, j), (j, i)]
    return swaps


def swap(array, axis, first, closed=False):
    return lax.ppermute(array, axis, pairs(lax.axis_size(axis), first, closed))


def body(
    source, storage, materials, conductance, mixing, counts, vis_owner, vis_slot, vis_block,
    radiosity_old, view_blocks, emission, reflect,
):
    nf, ca, cz, cr = source.shape
    mats = mixing.shape[0]
    owners = lax.axis_size("axial")
    me = lax.axis_index("axial")
    is_even = me % 2 == 0
    even = jnp.stack([is_even, me > 0, me + 1 < owners]).astype(jnp.int32)
    azim_even = lax.axis_index("azim") % 2 == 0
    near_memory = functools.partial(pltpu.with_memory_space_constraint, memory_space=pltpu.VMEM)
    call = functools.partial(pl.pallas_call, compiler_params=PARAMS)

    half = ROWS // 2

    def columns(right):
        def cut(array):
            return jnp.where(right, array[..., cz - half :, :], array[..., :half, :])

        kinds = cut(materials)[None].astype(f32)
        return jnp.concatenate([cut(source) * INV_CENTER, cut(storage), kinds], axis=0).astype(LINK)

    far_in = swap(columns(~azim_even), "azim", 1, True)
    layer_low, layer_high = source[:, 0] * INV_CENTER, source[:, ca - 1] * INV_CENTER
    halo1 = swap(jnp.where(is_even, layer_low, layer_high).astype(LINK), "axial", 1)
    near_in = swap(columns(azim_even), "azim", 0)

    slots, visible = vis_owner.shape[2:]
    values = radiosity_old.shape[3]
    tile = -(-slots // 16) * 16
    panels = jnp.pad(radiosity_old[0, 0], ((0, tile - slots), (0, 0)))
    fold = cr // values
    folded = panels.astype(f32) * RAD_SCALE
    folded = jnp.concatenate(jnp.split(folded, fold, axis=0), axis=1)
    layer0 = jnp.where(is_even, layer_high, layer_low).reshape(nf * cz, cr)
    message = swap(jnp.concatenate([layer0, folded], axis=0).astype(LINK), "axial", 0)
    halo0 = message[: nf * cz].reshape(nf, cz, cr)
    partner = message[nf * cz :].astype(f32) * (1.0 / RAD_SCALE)
    partner = jnp.concatenate(jnp.split(partner, fold, axis=1), axis=0).astype(bf16)

    from_right = jnp.where(azim_even, near_in, far_in)
    from_left = jnp.where(azim_even, far_in, near_in)
    wings = jnp.concatenate([from_right, from_left], axis=2).astype(f32)
    wing = wings[: 2 * nf].reshape(2, nf, ca, ROWS, cr)
    wing_kinds = wings[2 * nf].astype(jnp.int32)

    cond = jnp.broadcast_to(conductance[:, None, None], (nf, ROWS, cr))
    mixes = mixing + 6.0 * jnp.diag(conductance)
    mixes = jnp.pad(mixes.reshape(mats * nf, nf), ((0, 0), (0, 128 - nf)))
    here = pltpu.VMEM
    rest, edges, two, one = call(
        first_kernel,
        out_shape=(
            here((nf, ca, cz + ROWS, cr), f32), here((2, nf, cz + ROWS, cr), f32),
            here((mats * nf * ROWS, 2 * nf * ROWS), bf16), here((mats * nf * ROWS, nf * ROWS), bf16),
        ),
        in_specs=[SMEM] + [VMEM] * 7,
        out_specs=(VMEM,) * 4,
    )(even, source, storage, materials, wing, wing_kinds, mixes, cond)

    wide = conductance[:, None, None]

    def grown(edge, halo):
        return (edge + jnp.pad(BETA[1] * wide * halo, ((0, 0), (0, ROWS), (0, 0)))).astype(LINK)

    halo1, halo0 = halo1.astype(f32), halo0.astype(f32)
    second1 = swap(grown(edges[0], halo1), "axial", 1).astype(f32)
    second0 = swap(grown(edges[1], halo0), "axial", 0).astype(f32)

    if owners & (owners - 1) == 0:
        panels = jnp.concatenate([panels, partner], axis=0)
        step = 2
        while step < owners:
            other = lax.ppermute(panels, "axial", [(i, i ^ step) for i in range(owners)])
            panels = jnp.concatenate([panels, other], axis=0)
            step *= 2
        owner = vis_owner[0, 0].T ^ me
    else:
        pair = jnp.stack([panels, partner])
        panels = jnp.where(is_even, pair, pair[::-1]).reshape(2 * tile, values)
        groups = [list(range(k, owners, 2)) for k in range(2)]
        panels = lax.all_gather(panels, "axial", axis=0, tiled=True, axis_index_groups=groups)
        owner = vis_owner[0, 0].T
    live_count = counts[0]
    pad = ((0, -visible % ROWS), (0, -slots % 128))
    index = jnp.pad(owner * tile + vis_slot[0, 0].T, pad, constant_values=-1)
    block = jnp.pad(vis_block[0, 0].T, pad)
    chunk = tile * 8 if owners % 8 == 0 else tile * owners
    incoming = call(
        functools.partial(panel_kernel, chunk, visible),
        out_shape=here((index.shape[1], values), f32),
        in_specs=[VMEM] * 4,
        out_specs=VMEM,
    )(index, block, panels, view_blocks)

    rest2, dir2, edges = call(
        second_kernel,
        out_shape=(
            here((nf, ca, cz, cr), f32), here((nf, ca, cz + ROWS, cr), f32), here((2, nf, cz, cr), f32),
        ),
        in_specs=[SMEM] + [VMEM] * 10,
        out_specs=(VMEM,) * 3,
    )(even, rest, halo1, halo0, source, storage, materials, wing, cond, two, one)

    def grown_again(edge, halo):
        old = BETA[1] * wide * halo[:, cz:]
        zero = jnp.zeros((nf, cz - 2, cr), f32)
        ends = jnp.concatenate([old[:, 5:6], zero, old[:, 2:3]], axis=1)
        return (edge + BETA[2] * wide * (halo[:, :cz] + ends)).astype(LINK)

    third1 = swap(grown_again(edges[0], second1), "axial", 1).astype(f32)
    third0 = swap(grown_again(edges[1], second0), "axial", 0).astype(f32)

    plain = jax.ShapeDtypeStruct((nf, ca, cz, cr), f32)
    rest3, solution_out, panel_new = call(
        third_kernel,
        out_shape=(here(plain.shape, f32), plain, jax.ShapeDtypeStruct((slots, values), f32)),
        in_specs=[SMEM] * 2 + [VMEM] * 16,
        out_specs=(VMEM,) * 3,
    )(
        even, live_count, rest2, second1, second0, dir2, rest, source, storage, materials,
        wing, wing_kinds, cond, two, one, incoming, emission[0, 0], reflect[0, 0],
    )
    residual = call(
        last_kernel,
        out_shape=plain,
        in_specs=[SMEM] + [VMEM] * 4,
        out_specs=VMEM,
    )(even, rest3, third1, third0, cond)
    return (solution_out, residual, panel_new[None, None])


def solution(mesh):
    return jax.shard_map(
        body,
        mesh=mesh,
        in_specs=(
            P(None, "axial", "azim", None),
            P(None, "axial", "azim", None),
            P("axial", "azim", None),
            P(),
            P(),
            P("axial", "azim"),
            P("axial", "azim", None, None),
            P("axial", "azim", None, None),
            P("axial", "azim", None, None),
            P("axial", "azim", None, None),
            P(),
            P("axial", "azim", None, None),
            P("axial", "azim", None, None),
        ),
        out_specs=(
            P(None, "axial", "azim", None),
            P(None, "axial", "azim", None),
            P("axial", "azim", None, None),
        ),
        check_vma=False,
    )
```

```python
import functools
import jax
import jax.numpy as jnp
from jax import lax
from jax.experimental import pallas as pl
from jax.experimental.pallas import tpu as pltpu
from jax.sharding import PartitionSpec as P

center_value = 14.2
half_width = 13.8
sigma = center_value / half_width
ratio_0 = 1.0 / sigma
ratio_1 = 1.0 / (2.0 * sigma - ratio_0)
ratio_2 = 1.0 / (2.0 * sigma - ratio_1)
ALPHA = (None, ratio_1 * ratio_0, ratio_2 * ratio_1)
BETA = (None, 2.0 * ratio_1 / half_width, 2.0 * ratio_2 / half_width)
INV_CENTER = 1.0 / center_value

COPIES = 4
ROWS = 8
LINK = jnp.float16
RAD_SCALE = 8192.0
f32, bf16 = jnp.float32, jnp.bfloat16

VMEM = pl.BlockSpec(memory_space=pltpu.VMEM)
HBM = pl.BlockSpec(memory_space=pl.ANY)
PARAMS = pltpu.CompilerParams(vmem_limit_bytes=16 * 1024 * 1024)
CHEAP = pl.CostEstimate(flops=0, bytes_accessed=0, transcendentals=0)


def each_field(count, step):
    for f in range(count):
        step(f)


def tall(tile, height):
    return jnp.concatenate([tile] * (height // ROWS), axis=0)


def mixed_part(cells, kinds, coef, out_ref, a, rows):
    nf, height, cr = cells.shape
    flat = cells.reshape(nf * height, cr)
    high = flat.astype(bf16)
    low = (flat - high.astype(f32)).astype(bf16)
    out = jnp.dot(coef, jnp.concatenate([high, high, low], axis=0), preferred_element_type=f32)
    mats = out.shape[0] // (nf * height)
    out = out.reshape(mats, nf, height, cr)
    is_kind = [kinds == m for m in range(mats - 1)]
    for f in range(nf):
        picked = out[mats - 1, f]
        for m in range(mats - 1):
            picked = jnp.where(is_kind[m], out[m, f], picked)
        out_ref[f, a, rows] = picked


def radial_sum(cells):
    cr = cells.shape[-1]
    lane = lax.broadcasted_iota(jnp.int32, cells.shape, cells.ndim - 1)
    inner = jnp.where(lane == 0, 0.0, pltpu.roll(cells, 1, cells.ndim - 1))
    outer = jnp.where(lane == cr - 1, 0.0, pltpu.roll(cells, cr - 1, cells.ndim - 1))
    return inner + outer


def azim_sum(cells):
    rows = cells.shape[0]
    return pltpu.roll(cells, 1, 0) + pltpu.roll(cells, rows - 1, 0)


def apply_local(dir_ref, store, kinds, cond_ref, coef, mix_ref, span, emit):
    nf, ca = dir_ref.shape[:2]
    start, stop = span
    for a in range(ca):
        for t in range(start // ROWS, stop // ROWS):
            rows = slice(t * ROWS, (t + 1) * ROWS)
            mixed_part(dir_ref[:, a, rows], kinds(a, t), coef, mix_ref, a, rows)

    def step(f):
        cond = tall(cond_ref[f], stop - start)
        planes = [dir_ref[f, a] for a in range(ca)]
        for a in range(ca):
            cells = planes[a][start:stop]
            around = azim_sum(planes[a])[start:stop] + radial_sum(cells)
            if a > 0:
                around = around + planes[a - 1][start:stop]
            if a + 1 < ca:
                around = around + planes[a + 1][start:stop]
            emit(f, a, store(f, a) * cells + mix_ref[f, a, start:stop] - cond * around)

    each_field(nf, step)


def swapped(tile):
    place = lax.broadcasted_iota(jnp.int32, tile.shape, 0)
    return jnp.where((place // 2) % 2 == 0, pltpu.roll(tile, ROWS - 2, 0), pltpu.roll(tile, 2, 0))


def ends_kernel(
    flags_ref, source_hbm, store_hbm, kinds_hbm, source_ref, store_ref, kinds_ref, edge_ref, side_ref, sems
):
    nf, ca, cz, cr = source_ref.shape
    part = nf // COPIES
    pairs_of = [
        (far.at[pl.ds(i * part, part)], near.at[pl.ds(i * part, part)])
        for far, near in ((source_hbm, source_ref), (store_hbm, store_ref))
        for i in range(COPIES)
    ] + [(kinds_hbm, kinds_ref)]
    copies = [pltpu.make_async_copy(far, near, sems.at[i]) for i, (far, near) in enumerate(pairs_of)]
    for copy in copies:
        copy.start()
    even = tall(flags_ref[0], cz) > 0.5
    place = lax.broadcasted_iota(jnp.int32, (ROWS, cr), 0)

    def both(ref, *lead):
        return jnp.where(place < ROWS // 2, ref[(*lead, slice(0, ROWS))], ref[(*lead, slice(cz - ROWS, cz))])

    for copy in copies[:COPIES]:
        copy.wait()
    for f in range(nf):
        low, high = source_ref[f, 0] * INV_CENTER, source_ref[f, ca - 1] * INV_CENTER
        edge_ref[0, f] = jnp.where(even, low, high)
        edge_ref[1, f] = jnp.where(even, high, low)
        for a in range(ca):
            side_ref[f, a] = both(source_ref, f, a) * INV_CENTER
    for copy in copies[COPIES : 2 * COPIES]:
        copy.wait()
    outer = (place < 2) | (place >= ROWS - 2)
    for f in range(nf // 2):
        for a in range(ca):
            side_ref[nf + f, a] = jnp.where(
                outer, both(store_ref, f, a), swapped(both(store_ref, nf // 2 + f, a))
            )
    copies[2 * COPIES].wait()
    for a in range(ca):
        side_ref[nf + nf // 2, a] = both(kinds_ref, a).astype(f32)


def wing_store(wing_ref, f, a):
    nf = wing_ref.shape[0] // 3 * 2
    if f < nf // 2:
        return wing_ref[nf + f, a]
    return swapped(wing_ref[nf // 2 + f, a])


def coef_kernel(mix_ref, coef_ref):
    mixes = mix_ref[...]
    high = mixes.astype(bf16)
    low = (mixes - high.astype(f32)).astype(bf16)
    wide, inner = coef_ref.shape[0], coef_ref.shape[1] // 3
    row = lax.broadcasted_iota(jnp.int32, (wide, mixes.shape[0]), 0)
    col = lax.broadcasted_iota(jnp.int32, (wide, mixes.shape[0]), 1)
    down = (row // ROWS == col).astype(bf16)
    row = lax.broadcasted_iota(jnp.int32, (mixes.shape[1], inner), 0)
    col = lax.broadcasted_iota(jnp.int32, (mixes.shape[1], inner), 1)
    across = (col // ROWS == row).astype(bf16)
    row = lax.broadcasted_iota(jnp.int32, (wide, inner), 0)
    col = lax.broadcasted_iota(jnp.int32, (wide, inner), 1)
    same = row % ROWS == col % ROWS

    def spread(part):
        part = jnp.dot(down, part, preferred_element_type=f32).astype(bf16)
        full = jnp.dot(part, across, preferred_element_type=f32)
        return jnp.where(same, full, 0.0).astype(bf16)

    high = spread(high)
    coef_ref[:, :inner] = high
    coef_ref[:, inner : 2 * inner] = spread(low)
    coef_ref[:, 2 * inner :] = high


def first_kernel(
    source_ref, store_ref, kinds_ref, wing_ref, cond_ref, coef_ref,
    rest_ref, dir_ref, mix_ref,
):
    nf, ca, cz, cr = source_ref.shape
    own = cz // ROWS
    for f in range(nf):
        for a in range(ca):
            dir_ref[f, a, :cz] = source_ref[f, a] * INV_CENTER
            dir_ref[f, a, cz:] = wing_ref[f, a]

    def store(f, a):
        return jnp.concatenate([store_ref[f, a], wing_store(wing_ref, f, a)], axis=0)

    def kinds(a, t):
        return kinds_ref[a, t * ROWS : (t + 1) * ROWS].astype(f32) if t < own else wing_ref[nf + nf // 2, a]

    def emit(f, a, image):
        origin = jnp.concatenate([source_ref[f, a], center_value * wing_ref[f, a]], axis=0)
        rest_ref[f, a] = origin - image

    apply_local(dir_ref, store, kinds, cond_ref, coef_ref[...], mix_ref, (0, cz + ROWS), emit)


def side_kernel(
    first, flags_ref, rest_ref, halo_ref, source_ref, store_ref, kinds_ref, wing_ref, cond_ref, coef_ref,
    message_ref, dir_ref, next_ref, mix_ref,
):
    nf, ca, cz, cr = source_ref.shape
    even = flags_ref[0] > 0.5

    def choose(low, high):
        mask = tall(even, low.shape[0])
        return jnp.where(mask, low, high) if first else jnp.where(mask, high, low)

    place = lax.broadcasted_iota(jnp.int32, (ROWS, cr), 0)
    for f in range(nf):
        rest = choose(rest_ref[f, 0], rest_ref[f, ca - 1])
        wing = choose(wing_ref[f, 0], wing_ref[f, ca - 1])
        own = rest[:cz] + tall(cond_ref[f], cz) * halo_ref[f]
        direction = (ALPHA[1] * INV_CENTER) * choose(source_ref[f, 0], source_ref[f, ca - 1]) + BETA[1] * own
        beside = ALPHA[1] * wing + BETA[1] * rest[cz:]
        next_ref[f] = (ALPHA[1] * INV_CENTER) * choose(source_ref[f, 1], source_ref[f, ca - 2]) + BETA[1] * choose(
            rest_ref[f, 1, :cz], rest_ref[f, ca - 2, :cz]
        )
        dir_ref[f, 0, :cz] = direction
        dir_ref[f, 0, cz:] = beside
        message_ref[f, :cz] = direction
        message_ref[f, cz : 2 * cz] = own
        moved = jnp.where(place < 4, pltpu.roll(wing, 2, 0), pltpu.roll(wing, 6, 0))
        message_ref[f, 2 * cz :] = jnp.where((place >= 2) & (place <= 5), moved, beside)

    def kinds(a, t):
        rows = slice(t * ROWS, (t + 1) * ROWS)
        return choose(kinds_ref[0, rows].astype(f32), kinds_ref[ca - 1, rows].astype(f32))

    def emit(f, a, image):
        rest = message_ref[f, cz : 2 * cz] - image + tall(cond_ref[f], cz) * next_ref[f]
        message_ref[f, cz : 2 * cz] = ALPHA[2] * dir_ref[f, 0, :cz] + BETA[2] * rest

    apply_local(
        dir_ref, lambda f, a: choose(store_ref[f, 0], store_ref[f, ca - 1]), kinds,
        cond_ref, coef_ref[...], mix_ref, (0, cz), emit,
    )


def second_kernel(
    flags_ref, rest_ref, halo1_ref, halo0_ref, source_ref, store_ref, kinds_ref, wing_ref, cond_ref, coef_ref,
    newrest_ref, dir_ref, mix_ref,
):
    nf, ca, cz, cr = store_ref.shape
    even = tall(flags_ref[0], cz) > 0.5
    for f in range(nf):
        cond = tall(cond_ref[f], cz)
        arrived = {
            0: cond * jnp.where(even, halo1_ref[f], halo0_ref[f]),
            ca - 1: cond * jnp.where(even, halo0_ref[f], halo1_ref[f]),
        }
        for a in range(ca):
            rest = rest_ref[f, a, :cz]
            if a in arrived:
                rest = rest + arrived[a]
            newrest_ref[f, a] = rest
            dir_ref[f, a, :cz] = (ALPHA[1] * INV_CENTER) * source_ref[f, a] + BETA[1] * rest
            dir_ref[f, a, cz:] = ALPHA[1] * wing_ref[f, a] + BETA[1] * rest_ref[f, a, cz:]

    def emit(f, a, image):
        newrest_ref[f, a] = newrest_ref[f, a] - image

    apply_local(
        dir_ref, lambda f, a: store_ref[f, a], lambda a, t: kinds_ref[a, t * ROWS : (t + 1) * ROWS].astype(f32),
        cond_ref, coef_ref[...], mix_ref, (0, cz), emit,
    )


def third_kernel(
    flags_ref, rest_ref, halo1_ref, halo0_ref, second_ref, first_rest_ref, source_ref, store_ref,
    kinds_ref, wing_ref, cond_ref, coef_ref, live_ref, incoming_ref, emission_ref, reflect_ref,
    panel_ref, solution_ref, residual_ref,
    total_ref, out_ref, fixed_ref, dir_ref, beside_ref, mix_ref, sems,
):
    nf, ca, cz, cr = source_ref.shape
    own = cz // ROWS
    even = tall(flags_ref[0], 2 * cz + ROWS) > 0.5
    partner = {0: flags_ref[1] > 0.5, ca - 1: flags_ref[2] > 0.5}
    place = lax.broadcasted_iota(jnp.int32, (ROWS, cr), 0)
    outer = (place <= 1) | (place >= 6)

    def inward(beside):
        ends = [jnp.where(place == 0, pltpu.roll(beside, 1, 0), 0.0)]
        ends += [jnp.zeros_like(beside)] * (own - 2)
        ends += [jnp.where(place == ROWS - 1, pltpu.roll(beside, ROWS - 1, 0), 0.0)]
        return jnp.concatenate(ends, axis=0)

    for f in range(nf):
        cond = cond_ref[f]
        wide = tall(cond, cz)
        halo = {
            0: jnp.where(even, halo1_ref[f], halo0_ref[f]),
            ca - 1: jnp.where(even, halo0_ref[f], halo1_ref[f]),
        }
        for a in range(ca):
            rest = rest_ref[f, a]
            wing = second_ref[f, a, cz:]
            beside = first_rest_ref[f, a, cz:]
            direction = second_ref[f, a, :cz]
            if a in halo:
                old = halo[a][2 * cz :]
                moved = jnp.where(place < 4, pltpu.roll(old, ROWS - 2, 0), pltpu.roll(old, 2, 0))
                fix = cond * jnp.where(outer, moved, 0.0)
                rest = rest + wide * (halo[a][:cz] + BETA[1] * inward(fix))
                wing = wing + BETA[1] * fix
                mine = cond * wing_ref[f, a]
                beyond = cond * (old + BETA[1] * mine)
                beside = beside + fix + jnp.where(partner[a], beyond, 0.0)
            ahead = ALPHA[2] * direction + BETA[2] * rest
            if a in halo:
                third = halo[a][cz : 2 * cz] + BETA[2] * wide * (direction + BETA[1] * inward(mine))
                rest = rest + jnp.where(tall(partner[a], cz), wide * third, 0.0)
            out_ref[f, a] = rest
            fixed_ref[f, a, :cz] = direction
            fixed_ref[f, a, cz:] = wing
            beside_ref[f, a] = beside
            dir_ref[f, a, :cz] = ahead
            total_ref[f, a] = source_ref[f, a] * INV_CENTER + direction + ahead
    done_solution = pltpu.make_async_copy(total_ref, solution_ref, sems.at[0])
    done_solution.start()

    slots, values = panel_ref.shape
    wall = total_ref[0].reshape(ca * cz, cr)[:, cr - 1 : cr]
    wall = jnp.broadcast_to(wall, (ca * cz, values))
    wall = jnp.concatenate([wall] * (-(-slots // (ca * cz))), axis=0)[:slots]
    panel = lax.broadcasted_iota(jnp.int32, (slots, values), 0)
    fresh = emission_ref[...] * wall + reflect_ref[...] * incoming_ref[:slots]
    panel_ref[...] = jnp.where(panel < live_ref[:1], fresh, 0.0)

    def wing_emit(f, a, image):
        dir_ref[f, a, cz:] = ALPHA[2] * fixed_ref[f, a, cz:] + BETA[2] * (beside_ref[f, a] - image)

    apply_local(
        fixed_ref, lambda f, a: wing_store(wing_ref, f, a), lambda a, t: wing_ref[nf + nf // 2, a],
        cond_ref, coef_ref[...], mix_ref, (cz, cz + ROWS), wing_emit,
    )

    def emit(f, a, image):
        out_ref[f, a] = out_ref[f, a] - image

    apply_local(
        dir_ref, lambda f, a: store_ref[f, a], lambda a, t: kinds_ref[a, t * ROWS : (t + 1) * ROWS].astype(f32),
        cond_ref, coef_ref[...], mix_ref, (0, cz), emit,
    )
    done_residual = pltpu.make_async_copy(out_ref, residual_ref, sems.at[1])
    done_residual.start()
    done_solution.wait()
    done_residual.wait()


def panel_kernel(
    chunk, visible, index_ref, block_ref, rows_ref, view_ref, out_ref
):
    slots = index_ref.shape[1]
    total, values = rows_ref.shape
    index = index_ref[...].T
    block = block_ref[...].T
    types = view_ref.shape[0]
    lane = lax.broadcasted_iota(jnp.int32, (slots, chunk), 1)

    def gather(start):
        rows = rows_ref[pl.ds(start, chunk), :]
        return tuple(
            jnp.dot(
                (index[:, k : k + 1] == lane + start).astype(f32).astype(bf16),
                rows,
                preferred_element_type=f32,
            )
            for k in range(visible)
        )

    if total == chunk:
        found = gather(0)
    else:
        zero = tuple(jnp.zeros((slots, values), f32) for _ in range(visible))

        def step(i, sums):
            return tuple(s + g for s, g in zip(sums, gather(pl.multiple_of(i * chunk, chunk))))

        found = lax.fori_loop(0, total // chunk, step, zero)
    out = jnp.zeros((slots, values), f32)
    for b in range(types):
        stack = jnp.concatenate(
            [jnp.where(block[:, k : k + 1] == b, found[k], 0.0) for k in range(visible)], axis=0
        ).astype(bf16)
        moved = lax.dot_general(
            stack, view_ref[b], (((1,), (1,)), ((), ())), preferred_element_type=f32
        )
        for k in range(visible):
            out = out + moved[k * slots : (k + 1) * slots]
    out_ref[...] = out


def pairs(count, first, closed):
    swaps = []
    for i in range(first, count if closed and first else count - 1, 2):
        j = (i + 1) % count
        swaps += [(i, j), (j, i)]
    return swaps


def swap(array, axis, first, closed=False):
    return lax.ppermute(array, axis, pairs(lax.axis_size(axis), first, closed))


def body(
    source, storage, materials, conductance, mixing, counts, vis_owner, vis_slot, vis_block,
    radiosity_old, view_blocks, emission, reflect,
):
    nf, ca, cz, cr = source.shape
    mats = mixing.shape[0]
    owners = lax.axis_size("axial")
    me = lax.axis_index("axial")
    is_even = me % 2 == 0
    flags = jnp.stack([is_even, me > 0, me + 1 < owners]).astype(f32)
    flags = jnp.broadcast_to(flags[:, None, None], (3, ROWS, cr))
    azim_even = lax.axis_index("azim") % 2 == 0
    here = pltpu.VMEM

    def call(kernel, outs, args, scratch=(), far_out=False, plain_args=False):
        specs = [VMEM] * len(outs)
        if far_out:
            specs[-1] = HBM
        if not plain_args:
            args = [pltpu.with_memory_space_constraint(x, pltpu.VMEM) for x in args]
        single = len(outs) == 1
        return pl.pallas_call(
            kernel,
            out_shape=outs[0] if single else tuple(outs),
            in_specs=[VMEM] * len(args),
            out_specs=specs[0] if single else tuple(specs),
            scratch_shapes=list(scratch),
            compiler_params=PARAMS, cost_estimate=CHEAP,
        )(*args)

    def after(value, *others):
        return lax.optimization_barrier((value, *others))[0]

    plain = here((nf, ca, cz, cr), f32)
    layers = here((2, nf, cz, cr), f32)
    source, storage, materials, edges, sides = pl.pallas_call(
        ends_kernel,
        out_shape=(
            plain, plain, here((ca, cz, cr), jnp.int32), layers, here((nf + nf // 2 + 1, ca, ROWS, cr), f32)
        ),
        in_specs=[VMEM] + [HBM] * 3,
        out_specs=(VMEM,) * 5,
        scratch_shapes=[pltpu.SemaphoreType.DMA((2 * COPIES + 1,))],
        compiler_params=PARAMS, cost_estimate=CHEAP,
    )(flags, *(pltpu.with_memory_space_constraint(x, pltpu.HBM) for x in (source, storage, materials)))
    half = ROWS // 2
    to_right, to_left = sides[:, :, half:], sides[:, :, :half]
    far = jnp.where(azim_even, to_left, to_right).astype(LINK)
    near = jnp.where(azim_even, to_right, to_left).astype(LINK)
    far_in = swap(far, "azim", 1, True)
    message1 = after(edges, far)[0].astype(LINK)
    halo1 = swap(message1, "axial", 1)
    near_in = swap(after(near, message1), "azim", 0)

    slots, visible = vis_owner.shape[2:]
    values = radiosity_old.shape[3]
    tile = -(-slots // 16) * 16
    panels = jnp.pad(radiosity_old[0, 0], ((0, tile - slots), (0, 0)))
    fold = cr // values
    folded = panels.astype(f32) * RAD_SCALE
    folded = jnp.concatenate(jnp.split(folded, fold, axis=0), axis=1)
    layer0 = after(edges, message1)[1].reshape(nf * cz, cr)
    message = swap(jnp.concatenate([layer0, folded], axis=0).astype(LINK), "axial", 0)

    from_right = jnp.where(azim_even, near_in, far_in)
    from_left = jnp.where(azim_even, far_in, near_in)
    wings = jnp.concatenate([from_right, from_left], axis=2).astype(f32)

    cond = jnp.broadcast_to(conductance[:, None, None], (nf, ROWS, cr))
    mixes = mixing + 6.0 * jnp.diag(conductance)
    mixes = jnp.pad(mixes.reshape(mats * nf, nf), ((0, 0), (0, 128 - nf)))
    coef = call(coef_kernel, (here((mats * nf * ROWS, 3 * nf * ROWS), bf16),), (mixes,))
    full = here((nf, ca, cz + ROWS, cr), f32)
    rest = call(first_kernel, (full,), (source, storage, materials, wings, cond, coef), (full, full))

    def side(first, halo):
        return call(
            functools.partial(side_kernel, first),
            (here((nf, 2 * cz + ROWS, cr), f32),),
            (flags, rest, halo, source, storage, materials, wings, cond, coef),
            (here((nf, 1, cz + ROWS, cr), f32), here((nf, cz, cr), f32), here((nf, 1, cz + ROWS, cr), f32)),
        ).astype(LINK)

    halo1 = after(halo1, rest).astype(f32)
    message1 = side(True, halo1)
    second1 = swap(message1, "axial", 1).astype(f32)
    message = after(message, message1)
    halo0 = message[: nf * cz].reshape(nf, cz, cr).astype(f32)
    message0 = side(False, halo0)
    second0 = swap(message0, "axial", 0).astype(f32)

    rest2, dir2 = call(
        second_kernel,
        (plain, full),
        (flags, after(rest, message0), halo1, halo0, source, storage, materials, wings, cond, coef),
        (full,),
    )

    partner = after(message, rest2)[nf * cz :].astype(f32) * (1.0 / RAD_SCALE)
    partner = jnp.concatenate(jnp.split(partner, fold, axis=1), axis=0).astype(bf16)
    if owners <= 8 and owners & (owners - 1) == 0:
        pair = jnp.concatenate([panels, partner], axis=0)
        others = [
            lax.ppermute(pair, "axial", [(i, i ^ step) for i in range(owners)]) for step in range(2, owners, 2)
        ]
        panels = jnp.concatenate([pair, *others], axis=0)
        owner = vis_owner[0, 0].T ^ me
    else:
        pair = jnp.stack([panels, partner])
        panels = jnp.where(is_even, pair, pair[::-1]).reshape(2 * tile, values)
        groups = [list(range(k, owners, 2)) for k in range(2)]
        panels = lax.all_gather(panels, "axial", axis=0, tiled=True, axis_index_groups=groups)
        panels = panels.reshape(owners // 2, 2 * tile, values).reshape(owners * tile, values)
        owner = vis_owner[0, 0].T
    pad = ((0, -visible % ROWS), (0, -slots % 128))
    index = jnp.pad(owner * tile + vis_slot[0, 0].T, pad, constant_values=-1)
    block = jnp.pad(vis_block[0, 0].T, pad)
    chunk = tile * 8 if owners % 8 == 0 else tile * owners
    incoming = call(
        functools.partial(panel_kernel, chunk, visible),
        (here((index.shape[1], values), f32),),
        (index, block, panels, view_blocks),
        plain_args=True,
    )

    live = jnp.broadcast_to(counts, (ROWS, values))
    shape = jax.ShapeDtypeStruct
    panel_new, solution_out, residual = pl.pallas_call(
        third_kernel,
        out_shape=(shape((slots, values), f32), shape(source.shape, f32), shape(source.shape, f32)),
        in_specs=[VMEM] * 16,
        out_specs=(VMEM, HBM, HBM),
        scratch_shapes=[
            plain, plain, full, full, here((nf, ca, ROWS, cr), f32), full, pltpu.SemaphoreType.DMA((2,))
        ],
        compiler_params=PARAMS, cost_estimate=CHEAP,
    )(
        flags, rest2, second1, second0, dir2, rest, source, storage, materials, wings, cond, coef,
        live, incoming, emission[0, 0], reflect[0, 0],
    )
    return (solution_out, residual, panel_new[None, None])


def solution(mesh):
    return jax.shard_map(
        body,
        mesh=mesh,
        in_specs=(
            P(None, "axial", "azim", None),
            P(None, "axial", "azim", None),
            P("axial", "azim", None),
            P(),
            P(),
            P("axial", "azim"),
            P("axial", "azim", None, None),
            P("axial", "azim", None, None),
            P("axial", "azim", None, None),
            P("axial", "azim", None, None),
            P(),
            P("axial", "azim", None, None),
            P("axial", "azim", None, None),
        ),
        out_specs=(
            P(None, "axial", "azim", None),
            P(None, "axial", "azim", None),
            P("axial", "azim", None, None),
        ),
        check_vma=False,
    )
```

```python
import functools
import jax
import jax.numpy as jnp
from jax import lax
from jax.experimental import pallas as pl
from jax.experimental.pallas import tpu as pltpu
from jax.sharding import PartitionSpec as P

center_value = 14.2
half_width = 13.8
sigma = center_value / half_width
ratio_0 = 1.0 / sigma
ratio_1 = 1.0 / (2.0 * sigma - ratio_0)
ratio_2 = 1.0 / (2.0 * sigma - ratio_1)
ALPHA = (None, ratio_1 * ratio_0, ratio_2 * ratio_1)
BETA = (None, 2.0 * ratio_1 / half_width, 2.0 * ratio_2 / half_width)
INV_CENTER = 1.0 / center_value

GROUP = 4
COPIES = 4
ROWS = 8
LINK = jnp.float16
RAD_SCALE = 8192.0
f32, bf16 = jnp.float32, jnp.bfloat16

VMEM = pl.BlockSpec(memory_space=pltpu.VMEM)
HBM = pl.BlockSpec(memory_space=pl.ANY)
PARAMS = pltpu.CompilerParams(vmem_limit_bytes=16 * 1024 * 1024)
CHEAP = pl.CostEstimate(flops=0, bytes_accessed=0, transcendentals=0)


def each_field(count, step):
    for f in range(count):
        step(f)


def tall(tile, height):
    return jnp.concatenate([tile] * (height // ROWS), axis=0)


def mixed_part(cells, kinds, coef, out_ref, a, rows):
    nf, height, cr = cells.shape
    flat = cells.reshape(nf * height, cr)
    high = flat.astype(bf16)
    low = (flat - high.astype(f32)).astype(bf16)
    out = jnp.dot(coef, jnp.concatenate([high, high, low], axis=0), preferred_element_type=f32)
    mats = out.shape[0] // (nf * height)
    out = out.reshape(nf, mats, height, cr)
    is_kind = [kinds == m for m in range(mats - 1)]
    for f in range(nf):
        picked = out[f, mats - 1]
        for m in range(mats - 1):
            picked = jnp.where(is_kind[m], out[f, m], picked)
        out_ref[f, a, rows] = picked


def radial_sum(cells):
    cr = cells.shape[-1]
    lane = lax.broadcasted_iota(jnp.int32, cells.shape, cells.ndim - 1)
    inner = jnp.where(lane == 0, 0.0, pltpu.roll(cells, 1, cells.ndim - 1))
    outer = jnp.where(lane == cr - 1, 0.0, pltpu.roll(cells, cr - 1, cells.ndim - 1))
    return inner + outer


def azim_sum(cells):
    rows = cells.shape[0]
    return pltpu.roll(cells, 1, 0) + pltpu.roll(cells, rows - 1, 0)


def apply_local(dir_ref, store, kinds, cond_ref, coef, mix_ref, span, emit, linked=True):
    nf, ca = dir_ref.shape[:2]
    start, stop = span
    for a in range(ca):
        for t in range(start // ROWS, stop // ROWS):
            rows = slice(t * ROWS, (t + 1) * ROWS)
            mixed_part(dir_ref[:, a, rows], kinds(a, t), coef, mix_ref, a, rows)

    def step(f):
        cond = tall(cond_ref[f], stop - start)
        planes = [dir_ref[f, a] for a in range(ca)]
        for a in range(ca):
            cells = planes[a][start:stop]
            around = azim_sum(planes[a])[start:stop] + radial_sum(cells)
            if linked and a > 0:
                around = around + planes[a - 1][start:stop]
            if linked and a + 1 < ca:
                around = around + planes[a + 1][start:stop]
            emit(f, a, store(f, a) * cells + mix_ref[f, a, start:stop] - cond * around)

    each_field(nf, step)


def swapped(tile):
    place = lax.broadcasted_iota(jnp.int32, tile.shape, 0)
    return jnp.where((place // 2) % 2 == 0, pltpu.roll(tile, ROWS - 2, 0), pltpu.roll(tile, 2, 0))


def coef_rows(mixes):
    tall_rows, nf = mixes.shape
    wide, inner = tall_rows * ROWS, nf * ROWS
    high = mixes.astype(bf16)
    low = (mixes - high.astype(f32)).astype(bf16)
    row = lax.broadcasted_iota(jnp.int32, (wide, tall_rows), 0)
    col = lax.broadcasted_iota(jnp.int32, (wide, tall_rows), 1)
    down = (row // ROWS == col).astype(bf16)
    row = lax.broadcasted_iota(jnp.int32, (nf, inner), 0)
    col = lax.broadcasted_iota(jnp.int32, (nf, inner), 1)
    across = (col // ROWS == row).astype(bf16)
    row = lax.broadcasted_iota(jnp.int32, (wide, inner), 0)
    col = lax.broadcasted_iota(jnp.int32, (wide, inner), 1)
    same = row % ROWS == col % ROWS

    def spread(part):
        part = jnp.dot(down, part, preferred_element_type=f32).astype(bf16)
        full = jnp.dot(part, across, preferred_element_type=f32)
        return jnp.where(same, full, 0.0).astype(bf16)

    high = spread(high)
    return high, spread(low), high


def ends_kernel(
    flags_ref, source_hbm, store_hbm, kinds_hbm, cond_hbm, mix_hbm,
    source_ref, store_ref, kinds_ref, edge_ref, side_ref, cond_ref, coef_ref,
    cond_row, mix_rows, sems,
):
    nf, ca, cz, cr = source_ref.shape
    part = nf // COPIES
    pairs_of = [(cond_hbm, cond_row), (mix_hbm, mix_rows)] + [
        (far.at[pl.ds(i * part, part)], near.at[pl.ds(i * part, part)])
        for far, near in ((source_hbm, source_ref), (store_hbm, store_ref))
        for i in range(COPIES)
    ] + [(kinds_hbm, kinds_ref)]
    copies = [pltpu.make_async_copy(far, near, sems.at[i]) for i, (far, near) in enumerate(pairs_of)]
    for copy in copies:
        copy.start()
    even = tall(flags_ref[0], cz) > 0.5
    place = lax.broadcasted_iota(jnp.int32, (ROWS, cr), 0)

    copies[0].wait()
    copies[1].wait()
    for f in range(nf):
        cond_ref[f] = jnp.broadcast_to(cond_row[:, f : f + 1], (ROWS, cr))
    mats = mix_rows.shape[1]
    mixes = jnp.concatenate([mix_rows[f] for f in range(nf)], axis=0)
    row = lax.broadcasted_iota(jnp.int32, mixes.shape, 0)
    col = lax.broadcasted_iota(jnp.int32, mixes.shape, 1)
    mixes = mixes + jnp.where(row // mats == col, 6.0 * cond_row[...], 0.0)
    inner = nf * ROWS
    for i, rows in enumerate(coef_rows(mixes)):
        coef_ref[:, i * inner : (i + 1) * inner] = rows

    def both(ref, *lead):
        return jnp.where(place < ROWS // 2, ref[(*lead, slice(0, ROWS))], ref[(*lead, slice(cz - ROWS, cz))])

    for f in range(nf):
        if f % part == 0:
            copies[2 + f // part].wait()
        low, high = source_ref[f, 0] * INV_CENTER, source_ref[f, ca - 1] * INV_CENTER
        edge_ref[0, f] = jnp.where(even, low, high)
        edge_ref[1, f] = jnp.where(even, high, low)
        for a in range(ca):
            side_ref[f, a] = both(source_ref, f, a) * INV_CENTER
    for copy in copies[2 + COPIES :]:
        copy.wait()
    outer = (place < 2) | (place >= ROWS - 2)
    for f in range(nf // 2):
        for a in range(ca):
            side_ref[nf + f, a] = jnp.where(
                outer, both(store_ref, f, a), swapped(both(store_ref, nf // 2 + f, a))
            )
    for a in range(ca):
        side_ref[nf + nf // 2, a] = both(kinds_ref, a).astype(f32)


def wing_store(wing_ref, f, a):
    nf = wing_ref.shape[0] // 3 * 2
    if f < nf // 2:
        return wing_ref[nf + f, a]
    return swapped(wing_ref[nf // 2 + f, a])


def first_kernel(
    source_ref, store_ref, kinds_ref, wing_ref, cond_ref, coef_ref,
    rest_ref, dir_ref, mix_ref,
):
    nf, ca, cz, cr = source_ref.shape
    own = cz // ROWS
    for f in range(nf):
        for a in range(ca):
            dir_ref[f, a, :cz] = source_ref[f, a] * INV_CENTER
            dir_ref[f, a, cz:] = wing_ref[f, a]

    def store(f, a):
        return jnp.concatenate([store_ref[f, a], wing_store(wing_ref, f, a)], axis=0)

    def kinds(a, t):
        return kinds_ref[a, t * ROWS : (t + 1) * ROWS].astype(f32) if t < own else wing_ref[nf + nf // 2, a]

    def emit(f, a, image):
        origin = jnp.concatenate([source_ref[f, a], center_value * wing_ref[f, a]], axis=0)
        rest_ref[f, a] = origin - image

    apply_local(dir_ref, store, kinds, cond_ref, coef_ref[...], mix_ref, (0, cz + ROWS), emit)


def beside_rows(wing, beside):
    place = lax.broadcasted_iota(jnp.int32, wing.shape, 0)
    moved = jnp.where(place < 4, pltpu.roll(wing, 2, 0), pltpu.roll(wing, 6, 0))
    return jnp.where((place >= 2) & (place <= 5), moved, beside)


def side_kernel(
    first, flags_ref, rest_ref, halo_ref, source_ref, store_ref, kinds_ref, wing_ref, cond_ref, coef_ref,
    message_ref, dir_ref, next_ref, mix_ref,
):
    nf, ca, cz, cr = source_ref.shape
    even = flags_ref[0] > 0.5

    def choose(low, high):
        mask = tall(even, low.shape[0])
        return jnp.where(mask, low, high) if first else jnp.where(mask, high, low)

    for f in range(nf):
        rest = choose(rest_ref[f, 0], rest_ref[f, ca - 1])
        wing = choose(wing_ref[f, 0], wing_ref[f, ca - 1])
        own = rest[:cz] + tall(cond_ref[f], cz) * halo_ref[f]
        direction = (ALPHA[1] * INV_CENTER) * choose(source_ref[f, 0], source_ref[f, ca - 1]) + BETA[1] * own
        beside = ALPHA[1] * wing + BETA[1] * rest[cz:]
        next_ref[f] = (ALPHA[1] * INV_CENTER) * choose(source_ref[f, 1], source_ref[f, ca - 2]) + BETA[1] * choose(
            rest_ref[f, 1, :cz], rest_ref[f, ca - 2, :cz]
        )
        dir_ref[f, 0, :cz] = direction
        dir_ref[f, 0, cz:] = beside
        message_ref[f, :cz] = direction
        message_ref[f, cz : 2 * cz] = own
        message_ref[f, 2 * cz :] = beside_rows(wing, beside)

    def kinds(a, t):
        rows = slice(t * ROWS, (t + 1) * ROWS)
        return choose(kinds_ref[0, rows].astype(f32), kinds_ref[ca - 1, rows].astype(f32))

    def emit(f, a, image):
        rest = message_ref[f, cz : 2 * cz] - image + tall(cond_ref[f], cz) * next_ref[f]
        message_ref[f, cz : 2 * cz] = ALPHA[2] * dir_ref[f, 0, :cz] + BETA[2] * rest

    apply_local(
        dir_ref, lambda f, a: choose(store_ref[f, 0], store_ref[f, ca - 1]), kinds,
        cond_ref, coef_ref[...], mix_ref, (0, cz), emit,
    )


def second_part(
    flags_ref, rest_ref, halo1_ref, halo0_ref, source_ref, store_ref, kinds_ref, wing_ref, cond_ref, coef_ref,
    newrest_ref, dir_ref, mix_ref,
):
    nf, ca, cz, cr = store_ref.shape
    even = tall(flags_ref[0], cz) > 0.5
    for f in range(nf):
        cond = tall(cond_ref[f], cz)
        arrived = {
            0: cond * jnp.where(even, halo1_ref[f], halo0_ref[f]),
            ca - 1: cond * jnp.where(even, halo0_ref[f], halo1_ref[f]),
        }
        for a in range(ca):
            rest = rest_ref[f, a, :cz]
            if a in arrived:
                rest = rest + arrived[a]
            newrest_ref[f, a] = rest
            dir_ref[f, a, :cz] = (ALPHA[1] * INV_CENTER) * source_ref[f, a] + BETA[1] * rest
            dir_ref[f, a, cz:] = ALPHA[1] * wing_ref[f, a] + BETA[1] * rest_ref[f, a, cz:]

    def emit(f, a, image):
        newrest_ref[f, a] = newrest_ref[f, a] - image

    apply_local(
        dir_ref, lambda f, a: store_ref[f, a], lambda a, t: kinds_ref[a, t * ROWS : (t + 1) * ROWS].astype(f32),
        cond_ref, coef_ref[...], mix_ref, (0, cz), emit,
    )


def inward(beside, cz):
    place = lax.broadcasted_iota(jnp.int32, beside.shape, 0)
    ends = [jnp.where(place == 0, pltpu.roll(beside, 1, 0), 0.0)]
    ends += [jnp.zeros_like(beside)] * (cz // ROWS - 2)
    ends += [jnp.where(place == ROWS - 1, pltpu.roll(beside, ROWS - 1, 0), 0.0)]
    return jnp.concatenate(ends, axis=0)


def third_part(
    flags_ref, rest_ref, second_ref, first_rest_ref, source_ref, store_ref, kinds_ref, wing_ref, cond_ref, coef_ref,
    out_ref, total_ref, dir_ref, mix_ref,
):
    nf, ca, cz, cr = source_ref.shape
    partner = {0: flags_ref[1] > 0.5, ca - 1: flags_ref[2] > 0.5}
    for f in range(nf):
        cond = cond_ref[f]
        wide = tall(cond, cz)
        for a in range(ca):
            rest = rest_ref[f, a]
            direction = second_ref[f, a, :cz]
            ahead = ALPHA[2] * direction + BETA[2] * rest
            if a in partner:
                mine = inward(cond * wing_ref[f, a], cz)
                third = BETA[2] * wide * (direction + BETA[1] * mine)
                rest = rest + jnp.where(tall(partner[a], cz), wide * third, 0.0)
            out_ref[f, a] = rest
            dir_ref[f, a, :cz] = ahead
            total_ref[f, a] = source_ref[f, a] * INV_CENTER + direction + ahead

    def wing_emit(f, a, image):
        rest = first_rest_ref[f, a, cz:] - image
        if a in partner:
            cond = cond_ref[f]
            rest = rest + jnp.where(partner[a], BETA[1] * cond * cond * wing_ref[f, a], 0.0)
        dir_ref[f, a, cz:] = ALPHA[2] * second_ref[f, a, cz:] + BETA[2] * rest

    apply_local(
        second_ref, lambda f, a: wing_store(wing_ref, f, a), lambda a, t: wing_ref[nf + nf // 2, a],
        cond_ref, coef_ref[...], mix_ref, (cz, cz + ROWS), wing_emit,
    )

    def emit(f, a, image):
        out_ref[f, a] = out_ref[f, a] - image

    apply_local(
        dir_ref, lambda f, a: store_ref[f, a], lambda a, t: kinds_ref[a, t * ROWS : (t + 1) * ROWS].astype(f32),
        cond_ref, coef_ref[...], mix_ref, (0, cz), emit,
    )


def later_kernel(
    flags_ref, rest_ref, halo1_ref, halo0_ref, source_ref, store_ref, kinds_ref, wing_ref, cond_ref, coef_ref,
    out_ref, total_ref, second_rest_ref, second_ref, dir_ref, mix_ref,
):
    second_part(
        flags_ref, rest_ref, halo1_ref, halo0_ref, source_ref, store_ref, kinds_ref, wing_ref, cond_ref, coef_ref,
        second_rest_ref, second_ref, mix_ref,
    )
    third_part(
        flags_ref, second_rest_ref, second_ref, rest_ref, source_ref, store_ref, kinds_ref, wing_ref, cond_ref,
        coef_ref, out_ref, total_ref, dir_ref, mix_ref,
    )


def last_kernel(
    flags_ref, rest_ref, total_ref, halo1_ref, halo0_ref, store_ref, kinds_ref, wing_ref, cond_ref, coef_ref,
    live_ref, incoming_ref, emission_ref, reflect_ref,
    panel_ref, solution_ref, residual_ref,
    end_ref, out_ref, base_ref, fixed_ref, add_ref, beside_ref, mix_ref, sems,
):
    nf, ca, cz, cr = store_ref.shape
    ends = (0, ca - 1)
    beside_ends = (1, ca - 2)
    copies = []

    def send(near, far):
        copies.append(pltpu.make_async_copy(near, far, sems.at[len(copies)]))
        copies[-1].start()

    send(total_ref.at[:, 1 : ca - 1], solution_ref.at[:, 1 : ca - 1])
    even = tall(flags_ref[0], 2 * cz + ROWS) > 0.5
    place = lax.broadcasted_iota(jnp.int32, (ROWS, cr), 0)
    outer = (place <= 1) | (place >= 6)
    for f in range(nf):
        cond = cond_ref[f]
        wide = tall(cond, cz)
        h1, h0 = halo1_ref[f], halo0_ref[f]
        for e, halo in enumerate((jnp.where(even, h1, h0), jnp.where(even, h0, h1))):
            old = halo[2 * cz :]
            moved = jnp.where(place < 4, pltpu.roll(old, ROWS - 2, 0), pltpu.roll(old, 2, 0))
            fix = cond * jnp.where(outer, moved, 0.0)
            rest = wide * (halo[:cz] + BETA[1] * inward(fix, cz))
            base_ref[f, e] = rest + wide * halo[cz : 2 * cz]
            fixed_ref[f, e, :cz] = jnp.zeros_like(rest)
            fixed_ref[f, e, cz:] = BETA[1] * fix
            beside_ref[f, e] = fix + cond * old
            add_ref[f, e, :cz] = BETA[2] * rest
            end_ref[e, f] = total_ref[f, ends[e]] + BETA[2] * rest
    for e in range(2):
        send(end_ref.at[e], solution_ref.at[:, ends[e]])

    slots, values = panel_ref.shape
    wall = [end_ref[0, 0]] + [total_ref[0, a] for a in range(1, ca - 1)] + [end_ref[1, 0]]
    wall = jnp.concatenate(wall, axis=0)[:, cr - 1 : cr]
    wall = jnp.broadcast_to(wall, (ca * cz, values))
    wall = jnp.concatenate([wall] * (-(-slots // (ca * cz))), axis=0)[:slots]
    panel = lax.broadcasted_iota(jnp.int32, (slots, values), 0)
    fresh = emission_ref[...] * wall + reflect_ref[...] * incoming_ref[:slots]
    panel_ref[...] = jnp.where(panel < live_ref[:1], fresh, 0.0)

    def wing_emit(f, e, image):
        add_ref[f, e, cz:] = ALPHA[2] * fixed_ref[f, e, cz:] + BETA[2] * (beside_ref[f, e] - image)

    apply_local(
        fixed_ref, lambda f, e: wing_store(wing_ref, f, ends[e]), lambda e, t: wing_ref[nf + nf // 2, ends[e]],
        cond_ref, coef_ref[...], mix_ref, (cz, cz + ROWS), wing_emit, linked=False,
    )

    def emit(f, e, image):
        cond = cond_ref[f]
        out_ref[f, ends[e]] = rest_ref[f, ends[e]] + base_ref[f, e] - image
        inner = add_ref[f, e, :cz] + inward(BETA[2] * cond * fixed_ref[f, e, cz:], cz)
        out_ref[f, beside_ends[e]] = rest_ref[f, beside_ends[e]] + tall(cond, cz) * inner
        if e == 1:
            for a in range(2, ca - 2):
                out_ref[f, a] = rest_ref[f, a]
            if f % GROUP == GROUP - 1:
                some = pl.ds(f + 1 - GROUP, GROUP)
                send(out_ref.at[some], residual_ref.at[some])

    apply_local(
        add_ref, lambda f, e: store_ref[f, ends[e]],
        lambda e, t: kinds_ref[ends[e], t * ROWS : (t + 1) * ROWS].astype(f32),
        cond_ref, coef_ref[...], mix_ref, (0, cz), emit, linked=False,
    )
    for copy in copies:
        copy.wait()


def panel_kernel(
    chunk, visible, index_ref, block_ref, rows_ref, view_ref, out_ref
):
    slots = index_ref.shape[1]
    total, values = rows_ref.shape
    index = index_ref[...].T
    block = block_ref[...].T
    types = view_ref.shape[0]
    lane = lax.broadcasted_iota(jnp.int32, (slots, chunk), 1)

    def gather(start):
        rows = rows_ref[pl.ds(start, chunk), :]
        return tuple(
            jnp.dot(
                (index[:, k : k + 1] == lane + start).astype(f32).astype(bf16),
                rows,
                preferred_element_type=f32,
            )
            for k in range(visible)
        )

    if total == chunk:
        found = gather(0)
    else:
        zero = tuple(jnp.zeros((slots, values), f32) for _ in range(visible))

        def step(i, sums):
            return tuple(s + g for s, g in zip(sums, gather(pl.multiple_of(i * chunk, chunk))))

        found = lax.fori_loop(0, total // chunk, step, zero)
    out = jnp.zeros((slots, values), f32)
    for b in range(types):
        stack = jnp.concatenate(
            [jnp.where(block[:, k : k + 1] == b, found[k], 0.0) for k in range(visible)], axis=0
        ).astype(bf16)
        moved = lax.dot_general(
            stack, view_ref[b], (((1,), (1,)), ((), ())), preferred_element_type=f32
        )
        for k in range(visible):
            out = out + moved[k * slots : (k + 1) * slots]
    out_ref[...] = out


def relay_kernel(flags_ref, out_ref):
    out_ref[...] = flags_ref[...]


def pairs(count, first, closed):
    swaps = []
    for i in range(first, count if closed and first else count - 1, 2):
        j = (i + 1) % count
        swaps += [(i, j), (j, i)]
    return swaps


def swap(array, axis, first, closed=False):
    return lax.ppermute(array, axis, pairs(lax.axis_size(axis), first, closed))


def body(
    source, storage, materials, conductance, mixing, counts, vis_owner, vis_slot, vis_block,
    radiosity_old, view_blocks, emission, reflect,
):
    nf, ca, cz, cr = source.shape
    mats = mixing.shape[0]
    owners = lax.axis_size("axial")
    me = lax.axis_index("axial")
    is_even = me % 2 == 0
    flags = jnp.stack([is_even, me > 0, me + 1 < owners]).astype(f32)
    flags = jnp.broadcast_to(flags[:, None, None], (3, ROWS, cr))
    azim_even = lax.axis_index("azim") % 2 == 0
    here = pltpu.VMEM

    def call(kernel, outs, args, scratch=(), far_out=False, plain_args=False):
        specs = [VMEM] * len(outs)
        if far_out:
            specs[-1] = HBM
        if not plain_args:
            args = [pltpu.with_memory_space_constraint(x, pltpu.VMEM) for x in args]
        single = len(outs) == 1
        return pl.pallas_call(
            kernel,
            out_shape=outs[0] if single else tuple(outs),
            in_specs=[VMEM] * len(args),
            out_specs=specs[0] if single else tuple(specs),
            scratch_shapes=list(scratch),
            compiler_params=PARAMS, cost_estimate=CHEAP,
        )(*args)

    def after(value, *others):
        return lax.optimization_barrier((value, *others))[0]

    plain = here((nf, ca, cz, cr), f32)
    layers = here((2, nf, cz, cr), f32)
    small = (conductance[None], mixing.transpose(1, 0, 2))
    values = radiosity_old.shape[3]
    source, storage, materials, edges, sides, cond, coef = pl.pallas_call(
        ends_kernel,
        out_shape=(
            plain, plain, here((ca, cz, cr), jnp.int32), layers, here((nf + nf // 2 + 1, ca, ROWS, cr), f32),
            here((nf, ROWS, cr), f32), here((mats * nf * ROWS, 3 * nf * ROWS), bf16),
        ),
        in_specs=[VMEM] + [HBM] * 5,
        out_specs=(VMEM,) * 7,
        scratch_shapes=[here(x.shape, x.dtype) for x in small] + [pltpu.SemaphoreType.DMA((2 * COPIES + 3,))],
        compiler_params=PARAMS, cost_estimate=CHEAP,
    )(flags, *(pltpu.with_memory_space_constraint(x, pltpu.HBM) for x in (source, storage, materials, *small)))
    half = ROWS // 2
    to_right, to_left = sides[:, :, half:], sides[:, :, :half]
    far = jnp.where(azim_even, to_left, to_right).astype(LINK)
    near = jnp.where(azim_even, to_right, to_left).astype(LINK)
    far_in = swap(far, "azim", 1, True)
    message1 = after(edges, far)[0].astype(LINK)
    halo1 = swap(message1, "axial", 1)
    near_in = swap(after(near, message1), "azim", 0)

    slots, visible = vis_owner.shape[2:]
    tile = -(-slots // 16) * 16
    panels = jnp.pad(radiosity_old[0, 0], ((0, tile - slots), (0, 0)))
    fold = cr // values
    folded = panels.astype(f32) * RAD_SCALE
    folded = jnp.concatenate(jnp.split(folded, fold, axis=0), axis=1)
    layer0 = after(edges, message1)[1].reshape(nf * cz, cr)
    message = swap(jnp.concatenate([layer0, folded], axis=0).astype(LINK), "axial", 0)

    from_right = jnp.where(azim_even, near_in, far_in)
    from_left = jnp.where(azim_even, far_in, near_in)
    wings = jnp.concatenate([from_right, from_left], axis=2).astype(f32)

    full = here((nf, ca, cz + ROWS, cr), f32)
    rest = call(first_kernel, (full,), (source, storage, materials, wings, cond, coef), (full, full))

    def side(first, halo):
        one = here((nf, 1, cz + ROWS, cr), f32)
        return call(
            functools.partial(side_kernel, first),
            (here((nf, 2 * cz + ROWS, cr), f32),),
            (flags, rest, halo, source, storage, materials, wings, cond, coef),
            (one, here((nf, cz, cr), f32), one),
        ).astype(LINK)

    halo1 = after(halo1, rest).astype(f32)
    message1 = side(True, halo1)
    second1 = swap(message1, "axial", 1).astype(f32)
    message = after(message, message1)
    halo0 = message[: nf * cz].reshape(nf, cz, cr).astype(f32)
    message0 = side(False, halo0)
    second0 = swap(message0, "axial", 0).astype(f32)
    rest3, total = call(
        later_kernel,
        (plain, plain),
        (flags, after(rest, message0), halo1, halo0, source, storage, materials, wings, cond, coef),
        (plain, full, full, full),
    )

    partner = after(message, message0)[nf * cz :].astype(f32) * (1.0 / RAD_SCALE)
    partner = jnp.concatenate(jnp.split(partner, fold, axis=1), axis=0).astype(bf16)
    if owners <= 8 and owners & (owners - 1) == 0:
        pair = jnp.concatenate([panels, partner], axis=0)
        others = [
            lax.ppermute(pair, "axial", [(i, i ^ step) for i in range(owners)]) for step in range(2, owners, 2)
        ]
        panels = jnp.concatenate([after(pair, second1), *others], axis=0)
        owner = vis_owner[0, 0].T ^ me
    else:
        pair = jnp.stack([panels, partner])
        panels = jnp.where(is_even, pair, pair[::-1]).reshape(2 * tile, values)
        groups = [list(range(k, owners, 2)) for k in range(2)]
        panels = lax.all_gather(panels, "axial", axis=0, tiled=True, axis_index_groups=groups)
        panels = panels.reshape(owners // 2, 2 * tile, values).reshape(owners * tile, values)
        owner = vis_owner[0, 0].T
    pad = ((0, -visible % ROWS), (0, -slots % 128))
    index = jnp.pad(owner * tile + vis_slot[0, 0].T, pad, constant_values=-1)
    block = jnp.pad(vis_block[0, 0].T, pad)
    chunk = tile * 8 if owners % 8 == 0 else tile * owners
    incoming = call(
        functools.partial(panel_kernel, chunk, visible),
        (here((index.shape[1], values), f32),),
        (index, block, panels, view_blocks),
        plain_args=True,
    )

    live = jnp.broadcast_to(after(counts, rest3), (ROWS, values))
    checked = call(relay_kernel, (here(flags.shape, f32),), (after(flags, second0),))
    shape = jax.ShapeDtypeStruct
    pair_full = here((nf, 2, cz + ROWS, cr), f32)
    panel_new, solution_out, residual = pl.pallas_call(
        last_kernel,
        out_shape=(shape((slots, values), f32), shape(plain.shape, f32), shape(plain.shape, f32)),
        in_specs=[VMEM] * 14,
        out_specs=(VMEM, HBM, HBM),
        scratch_shapes=[
            layers, plain, here((nf, 2, cz, cr), f32), pair_full, pair_full, here((nf, 2, ROWS, cr), f32), pair_full,
            pltpu.SemaphoreType.DMA((3 + nf // GROUP,)),
        ],
        compiler_params=PARAMS, cost_estimate=CHEAP,
    )(
        checked, rest3, total, second1, second0, storage, materials, wings, cond, coef,
        live, incoming, emission[0, 0], reflect[0, 0],
    )
    return (solution_out, residual, panel_new[None, None])


def solution(mesh):
    return jax.shard_map(
        body,
        mesh=mesh,
        in_specs=(
            P(None, "axial", "azim", None),
            P(None, "axial", "azim", None),
            P("axial", "azim", None),
            P(),
            P(),
            P("axial", "azim"),
            P("axial", "azim", None, None),
            P("axial", "azim", None, None),
            P("axial", "azim", None, None),
            P("axial", "azim", None, None),
            P(),
            P("axial", "azim", None, None),
            P("axial", "azim", None, None),
        ),
        out_specs=(
            P(None, "axial", "azim", None),
            P(None, "axial", "azim", None),
            P("axial", "azim", None, None),
        ),
        check_vma=False,
    )
```

```python
import functools
import jax
import jax.numpy as jnp
from jax import lax
from jax.experimental import pallas as pl
from jax.experimental.pallas import tpu as pltpu
from jax.sharding import PartitionSpec as P

center_value = 14.2
half_width = 13.8
sigma = center_value / half_width
ratio_0 = 1.0 / sigma
ratio_1 = 1.0 / (2.0 * sigma - ratio_0)
ratio_2 = 1.0 / (2.0 * sigma - ratio_1)
ALPHA = (None, ratio_1 * ratio_0, ratio_2 * ratio_1)
BETA = (None, 2.0 * ratio_1 / half_width, 2.0 * ratio_2 / half_width)
INV_CENTER = 1.0 / center_value

GROUP = 4
COPIES = 4
ROWS = 8
LINK = jnp.float16
RAD_SCALE = 8192.0
f32, bf16 = jnp.float32, jnp.bfloat16

VMEM = pl.BlockSpec(memory_space=pltpu.VMEM)
HBM = pl.BlockSpec(memory_space=pl.ANY)
PARAMS = pltpu.CompilerParams(vmem_limit_bytes=16 * 1024 * 1024)
CHEAP = pl.CostEstimate(flops=0, bytes_accessed=0, transcendentals=0)


def each_field(count, step):
    for f in range(count):
        step(f)


def tall(tile, height):
    return jnp.concatenate([tile] * (height // ROWS), axis=0)


def mixed_part(cells, kinds, coef, out_ref, a, rows):
    nf, height, cr = cells.shape
    flat = cells.reshape(nf * height, cr)
    high = flat.astype(bf16)
    low = (flat - high.astype(f32)).astype(bf16)
    out = jnp.dot(coef, jnp.concatenate([high, high, low], axis=0), preferred_element_type=f32)
    mats = out.shape[0] // (nf * height)
    out = out.reshape(nf, mats, height, cr)
    is_kind = [kinds == m for m in range(mats - 1)]
    for f in range(nf):
        picked = out[f, mats - 1]
        for m in range(mats - 1):
            picked = jnp.where(is_kind[m], out[f, m], picked)
        out_ref[f, a, rows] = picked


def radial_sum(cells):
    cr = cells.shape[-1]
    lane = lax.broadcasted_iota(jnp.int32, cells.shape, cells.ndim - 1)
    inner = jnp.where(lane == 0, 0.0, pltpu.roll(cells, 1, cells.ndim - 1))
    outer = jnp.where(lane == cr - 1, 0.0, pltpu.roll(cells, cr - 1, cells.ndim - 1))
    return inner + outer


def azim_sum(cells):
    rows = cells.shape[0]
    return pltpu.roll(cells, 1, 0) + pltpu.roll(cells, rows - 1, 0)


def apply_local(dir_ref, store, kinds, cond_ref, coef, mix_ref, span, emit, linked=True):
    nf, ca = dir_ref.shape[:2]
    start, stop = span
    for a in range(ca):
        for t in range(start // ROWS, stop // ROWS):
            rows = slice(t * ROWS, (t + 1) * ROWS)
            mixed_part(dir_ref[:, a, rows], kinds(a, t), coef, mix_ref, a, rows)

    def step(f):
        cond = tall(cond_ref[f], stop - start)
        planes = [dir_ref[f, a] for a in range(ca)]
        for a in range(ca):
            cells = planes[a][start:stop]
            around = azim_sum(planes[a])[start:stop] + radial_sum(cells)
            if linked and a > 0:
                around = around + planes[a - 1][start:stop]
            if linked and a + 1 < ca:
                around = around + planes[a + 1][start:stop]
            emit(f, a, store(f, a) * cells + mix_ref[f, a, start:stop] - cond * around)

    each_field(nf, step)


def swapped(tile):
    place = lax.broadcasted_iota(jnp.int32, tile.shape, 0)
    return jnp.where((place // 2) % 2 == 0, pltpu.roll(tile, ROWS - 2, 0), pltpu.roll(tile, 2, 0))


def coef_rows(mixes):
    tall_rows, nf = mixes.shape
    wide, inner = tall_rows * ROWS, nf * ROWS
    high = mixes.astype(bf16)
    low = (mixes - high.astype(f32)).astype(bf16)
    row = lax.broadcasted_iota(jnp.int32, (wide, tall_rows), 0)
    col = lax.broadcasted_iota(jnp.int32, (wide, tall_rows), 1)
    down = (row // ROWS == col).astype(bf16)
    row = lax.broadcasted_iota(jnp.int32, (nf, inner), 0)
    col = lax.broadcasted_iota(jnp.int32, (nf, inner), 1)
    across = (col // ROWS == row).astype(bf16)
    row = lax.broadcasted_iota(jnp.int32, (wide, inner), 0)
    col = lax.broadcasted_iota(jnp.int32, (wide, inner), 1)
    same = row % ROWS == col % ROWS

    def spread(part):
        part = jnp.dot(down, part, preferred_element_type=f32).astype(bf16)
        full = jnp.dot(part, across, preferred_element_type=f32)
        return jnp.where(same, full, 0.0).astype(bf16)

    high = spread(high)
    return high, spread(low), high


def ends_kernel(
    flags_ref, source_hbm, store_hbm, kinds_hbm, cond_hbm, mix_hbm,
    source_ref, store_ref, kinds_ref, edge_ref, side_ref, cond_ref, coef_ref,
    cond_row, mix_rows, sems,
):
    nf, ca, cz, cr = source_ref.shape
    part = nf // COPIES
    pairs_of = [(cond_hbm, cond_row), (mix_hbm, mix_rows)] + [
        (far.at[pl.ds(i * part, part)], near.at[pl.ds(i * part, part)])
        for far, near in ((source_hbm, source_ref), (store_hbm, store_ref))
        for i in range(COPIES)
    ] + [(kinds_hbm, kinds_ref)]
    copies = [pltpu.make_async_copy(far, near, sems.at[i]) for i, (far, near) in enumerate(pairs_of)]
    for copy in copies:
        copy.start()
    even = tall(flags_ref[0], cz) > 0.5
    place = lax.broadcasted_iota(jnp.int32, (ROWS, cr), 0)

    copies[0].wait()
    copies[1].wait()
    for f in range(nf):
        cond_ref[f] = jnp.broadcast_to(cond_row[:, f : f + 1], (ROWS, cr))
    mats = mix_rows.shape[1]
    mixes = jnp.concatenate([mix_rows[f] for f in range(nf)], axis=0)
    row = lax.broadcasted_iota(jnp.int32, mixes.shape, 0)
    col = lax.broadcasted_iota(jnp.int32, mixes.shape, 1)
    mixes = mixes + jnp.where(row // mats == col, 6.0 * cond_row[...], 0.0)
    inner = nf * ROWS
    for i, rows in enumerate(coef_rows(mixes)):
        coef_ref[:, i * inner : (i + 1) * inner] = rows

    def both(ref, *lead):
        return jnp.where(place < ROWS // 2, ref[(*lead, slice(0, ROWS))], ref[(*lead, slice(cz - ROWS, cz))])

    for f in range(nf):
        if f % part == 0:
            copies[2 + f // part].wait()
        low, high = source_ref[f, 0] * INV_CENTER, source_ref[f, ca - 1] * INV_CENTER
        edge_ref[0, f] = jnp.where(even, low, high)
        edge_ref[1, f] = jnp.where(even, high, low)
        for a in range(ca):
            side_ref[f, a] = both(source_ref, f, a) * INV_CENTER
    for copy in copies[2 + COPIES :]:
        copy.wait()
    outer = (place < 2) | (place >= ROWS - 2)
    for f in range(nf // 2):
        for a in range(ca):
            side_ref[nf + f, a] = jnp.where(
                outer, both(store_ref, f, a), swapped(both(store_ref, nf // 2 + f, a))
            )
    for a in range(ca):
        side_ref[nf + nf // 2, a] = both(kinds_ref, a).astype(f32)


def wing_store(wing_ref, f, a):
    nf = wing_ref.shape[0] // 3 * 2
    if f < nf // 2:
        return wing_ref[nf + f, a]
    return swapped(wing_ref[nf // 2 + f, a])


def first_kernel(
    source_ref, store_ref, kinds_ref, wing_ref, cond_ref, coef_ref,
    rest_ref, dir_ref, mix_ref,
):
    nf, ca, cz, cr = source_ref.shape
    own = cz // ROWS
    for f in range(nf):
        for a in range(ca):
            dir_ref[f, a, :cz] = source_ref[f, a] * INV_CENTER
            dir_ref[f, a, cz:] = wing_ref[f, a]

    def store(f, a):
        return jnp.concatenate([store_ref[f, a], wing_store(wing_ref, f, a)], axis=0)

    def kinds(a, t):
        return kinds_ref[a, t * ROWS : (t + 1) * ROWS].astype(f32) if t < own else wing_ref[nf + nf // 2, a]

    def emit(f, a, image):
        origin = jnp.concatenate([source_ref[f, a], center_value * wing_ref[f, a]], axis=0)
        rest_ref[f, a] = origin - image

    apply_local(dir_ref, store, kinds, cond_ref, coef_ref[...], mix_ref, (0, cz + ROWS), emit)


def beside_rows(wing, beside):
    place = lax.broadcasted_iota(jnp.int32, wing.shape, 0)
    moved = jnp.where(place < 4, pltpu.roll(wing, 2, 0), pltpu.roll(wing, 6, 0))
    return jnp.where((place >= 2) & (place <= 5), moved, beside)


def side_kernel(
    first, flags_ref, rest_ref, halo_ref, source_ref, store_ref, kinds_ref, wing_ref, cond_ref, coef_ref,
    message_ref, dir_ref, next_ref, mix_ref,
):
    nf, ca, cz, cr = source_ref.shape
    even = flags_ref[0] > 0.5

    def choose(low, high):
        mask = tall(even, low.shape[0])
        return jnp.where(mask, low, high) if first else jnp.where(mask, high, low)

    for f in range(nf):
        rest = choose(rest_ref[f, 0], rest_ref[f, ca - 1])
        wing = choose(wing_ref[f, 0], wing_ref[f, ca - 1])
        own = rest[:cz] + tall(cond_ref[f], cz) * halo_ref[f]
        direction = (ALPHA[1] * INV_CENTER) * choose(source_ref[f, 0], source_ref[f, ca - 1]) + BETA[1] * own
        beside = ALPHA[1] * wing + BETA[1] * rest[cz:]
        next_ref[f] = (ALPHA[1] * INV_CENTER) * choose(source_ref[f, 1], source_ref[f, ca - 2]) + BETA[1] * choose(
            rest_ref[f, 1, :cz], rest_ref[f, ca - 2, :cz]
        )
        dir_ref[f, 0, :cz] = direction
        dir_ref[f, 0, cz:] = beside
        message_ref[f, :cz] = direction
        message_ref[f, cz : 2 * cz] = own
        message_ref[f, 2 * cz :] = beside_rows(wing, beside)

    def kinds(a, t):
        rows = slice(t * ROWS, (t + 1) * ROWS)
        return choose(kinds_ref[0, rows].astype(f32), kinds_ref[ca - 1, rows].astype(f32))

    def emit(f, a, image):
        rest = message_ref[f, cz : 2 * cz] - image + tall(cond_ref[f], cz) * next_ref[f]
        message_ref[f, cz : 2 * cz] = ALPHA[2] * dir_ref[f, 0, :cz] + BETA[2] * rest

    apply_local(
        dir_ref, lambda f, a: choose(store_ref[f, 0], store_ref[f, ca - 1]), kinds,
        cond_ref, coef_ref[...], mix_ref, (0, cz), emit,
    )


def second_part(
    flags_ref, rest_ref, halo1_ref, halo0_ref, source_ref, store_ref, kinds_ref, wing_ref, cond_ref, coef_ref,
    newrest_ref, dir_ref, mix_ref,
):
    nf, ca, cz, cr = store_ref.shape
    even = tall(flags_ref[0], cz) > 0.5
    for f in range(nf):
        cond = tall(cond_ref[f], cz)
        arrived = {
            0: cond * jnp.where(even, halo1_ref[f], halo0_ref[f]),
            ca - 1: cond * jnp.where(even, halo0_ref[f], halo1_ref[f]),
        }
        for a in range(ca):
            rest = rest_ref[f, a, :cz]
            if a in arrived:
                rest = rest + arrived[a]
            newrest_ref[f, a] = rest
            dir_ref[f, a, :cz] = (ALPHA[1] * INV_CENTER) * source_ref[f, a] + BETA[1] * rest
            dir_ref[f, a, cz:] = ALPHA[1] * wing_ref[f, a] + BETA[1] * rest_ref[f, a, cz:]

    def emit(f, a, image):
        newrest_ref[f, a] = newrest_ref[f, a] - image

    apply_local(
        dir_ref, lambda f, a: store_ref[f, a], lambda a, t: kinds_ref[a, t * ROWS : (t + 1) * ROWS].astype(f32),
        cond_ref, coef_ref[...], mix_ref, (0, cz), emit,
    )


def inward(beside, cz):
    place = lax.broadcasted_iota(jnp.int32, beside.shape, 0)
    ends = [jnp.where(place == 0, pltpu.roll(beside, 1, 0), 0.0)]
    ends += [jnp.zeros_like(beside)] * (cz // ROWS - 2)
    ends += [jnp.where(place == ROWS - 1, pltpu.roll(beside, ROWS - 1, 0), 0.0)]
    return jnp.concatenate(ends, axis=0)


def third_part(
    flags_ref, rest_ref, second_ref, first_rest_ref, source_ref, store_ref, kinds_ref, wing_ref, cond_ref, coef_ref,
    out_ref, total_ref, dir_ref, mix_ref,
):
    nf, ca, cz, cr = source_ref.shape
    partner = {0: flags_ref[1] > 0.5, ca - 1: flags_ref[2] > 0.5}
    for f in range(nf):
        cond = cond_ref[f]
        wide = tall(cond, cz)
        for a in range(ca):
            rest = rest_ref[f, a]
            direction = second_ref[f, a, :cz]
            ahead = ALPHA[2] * direction + BETA[2] * rest
            if a in partner:
                mine = inward(cond * wing_ref[f, a], cz)
                third = BETA[2] * wide * (direction + BETA[1] * mine)
                rest = rest + jnp.where(tall(partner[a], cz), wide * third, 0.0)
            out_ref[f, a] = rest
            dir_ref[f, a, :cz] = ahead
            total_ref[f, a] = source_ref[f, a] * INV_CENTER + direction + ahead

    def wing_emit(f, a, image):
        rest = first_rest_ref[f, a, cz:] - image
        if a in partner:
            cond = cond_ref[f]
            rest = rest + jnp.where(partner[a], BETA[1] * cond * cond * wing_ref[f, a], 0.0)
        dir_ref[f, a, cz:] = ALPHA[2] * second_ref[f, a, cz:] + BETA[2] * rest

    apply_local(
        second_ref, lambda f, a: wing_store(wing_ref, f, a), lambda a, t: wing_ref[nf + nf // 2, a],
        cond_ref, coef_ref[...], mix_ref, (cz, cz + ROWS), wing_emit,
    )

    def emit(f, a, image):
        out_ref[f, a] = out_ref[f, a] - image

    apply_local(
        dir_ref, lambda f, a: store_ref[f, a], lambda a, t: kinds_ref[a, t * ROWS : (t + 1) * ROWS].astype(f32),
        cond_ref, coef_ref[...], mix_ref, (0, cz), emit,
    )


def later_kernel(
    flags_ref, rest_ref, halo1_ref, halo0_ref, source_ref, store_ref, kinds_ref, wing_ref, cond_ref, coef_ref,
    out_ref, total_ref, second_rest_ref, second_ref, dir_ref, mix_ref,
):
    second_part(
        flags_ref, rest_ref, halo1_ref, halo0_ref, source_ref, store_ref, kinds_ref, wing_ref, cond_ref, coef_ref,
        second_rest_ref, second_ref, mix_ref,
    )
    third_part(
        flags_ref, second_rest_ref, second_ref, rest_ref, source_ref, store_ref, kinds_ref, wing_ref, cond_ref,
        coef_ref, out_ref, total_ref, dir_ref, mix_ref,
    )


def end_part(
    first, flags_ref, halo_ref, store_ref, kinds_ref, wing_ref, cond_ref, coef_ref,
    delta_ref, base_ref, fixed_ref, add_ref, beside_ref, mix_ref, early, emit,
):
    nf, ca, cz, cr = store_ref.shape
    even = flags_ref[0] > 0.5

    def choose(low, high):
        mask = tall(even, low.shape[0])
        return jnp.where(mask, low, high) if first else jnp.where(mask, high, low)

    place = lax.broadcasted_iota(jnp.int32, (ROWS, cr), 0)
    outer = (place <= 1) | (place >= 6)
    for f in range(nf):
        cond = cond_ref[f]
        wide = tall(cond, cz)
        old = halo_ref[f, 2 * cz :]
        moved = jnp.where(place < 4, pltpu.roll(old, ROWS - 2, 0), pltpu.roll(old, 2, 0))
        fix = cond * jnp.where(outer, moved, 0.0)
        rest = wide * (halo_ref[f, :cz] + BETA[1] * inward(fix, cz))
        base_ref[f] = rest + wide * halo_ref[f, cz : 2 * cz]
        fixed_ref[f, 0, :cz] = jnp.zeros_like(rest)
        fixed_ref[f, 0, cz:] = BETA[1] * fix
        beside_ref[f] = fix + cond * old
        add_ref[f, 0, :cz] = BETA[2] * rest
        delta_ref[0, f] = BETA[2] * rest
    early()

    def wing_emit(f, a, image):
        add_ref[f, 0, cz:] = ALPHA[2] * fixed_ref[f, 0, cz:] + BETA[2] * (beside_ref[f] - image)

    def wing_choice(f, a):
        return choose(wing_store(wing_ref, f, 0), wing_store(wing_ref, f, ca - 1))

    def wing_kinds(a, t):
        return choose(wing_ref[nf + nf // 2, 0], wing_ref[nf + nf // 2, ca - 1])

    apply_local(
        fixed_ref, wing_choice, wing_kinds, cond_ref, coef_ref[...], mix_ref, (cz, cz + ROWS), wing_emit, linked=False
    )

    def own_emit(f, a, image):
        cond = cond_ref[f]
        delta_ref[1, f] = base_ref[f] - image
        inner = add_ref[f, 0, :cz] + inward(BETA[2] * cond * fixed_ref[f, 0, cz:], cz)
        delta_ref[2, f] = tall(cond, cz) * inner
        emit(f)

    def kinds(a, t):
        rows = slice(t * ROWS, (t + 1) * ROWS)
        return choose(kinds_ref[0, rows].astype(f32), kinds_ref[ca - 1, rows].astype(f32))

    apply_local(
        add_ref, lambda f, a: choose(store_ref[f, 0], store_ref[f, ca - 1]), kinds,
        cond_ref, coef_ref[...], mix_ref, (0, cz), own_emit, linked=False,
    )


def end_kernel(
    flags_ref, halo_ref, store_ref, kinds_ref, wing_ref, cond_ref, coef_ref,
    delta_ref, base_ref, fixed_ref, add_ref, beside_ref, mix_ref,
):
    end_part(
        False, flags_ref, halo_ref, store_ref, kinds_ref, wing_ref, cond_ref, coef_ref,
        delta_ref, base_ref, fixed_ref, add_ref, beside_ref, mix_ref, lambda: None, lambda f: None,
    )


def last_kernel(
    flags_ref, rest_ref, total_ref, halo_ref, other_ref, store_ref, kinds_ref, wing_ref, cond_ref, coef_ref,
    live_ref, incoming_ref, emission_ref, reflect_ref,
    panel_hbm, solution_ref, residual_ref,
    panel_ref, end_ref, out_ref, delta_ref, base_ref, fixed_ref, add_ref, beside_ref, mix_ref, sems,
):
    nf, ca, cz, cr = store_ref.shape
    even = tall(flags_ref[0], cz) > 0.5
    copies = []

    def send(near, far):
        copies.append(pltpu.make_async_copy(near, far, sems.at[len(copies)]))
        copies[-1].start()

    send(total_ref.at[:, 1 : ca - 1], solution_ref.at[:, 1 : ca - 1])

    def both(i, f):
        one, other = delta_ref[i, f], other_ref[i, f]
        return jnp.where(even, one, other), jnp.where(even, other, one)

    def early():
        for f in range(nf):
            low, high = both(0, f)
            end_ref[0, f] = total_ref[f, 0] + low
            end_ref[1, f] = total_ref[f, ca - 1] + high
        send(end_ref.at[0], solution_ref.at[:, 0])
        send(end_ref.at[1], solution_ref.at[:, ca - 1])
        slots, values = panel_ref.shape
        wall = [end_ref[0, 0]] + [total_ref[0, a] for a in range(1, ca - 1)] + [end_ref[1, 0]]
        wall = jnp.concatenate(wall, axis=0)[:, cr - 1 : cr]
        wall = jnp.broadcast_to(wall, (ca * cz, values))
        wall = jnp.concatenate([wall] * (-(-slots // (ca * cz))), axis=0)[:slots]
        panel = lax.broadcasted_iota(jnp.int32, (slots, values), 0)
        fresh = emission_ref[...] * wall + reflect_ref[...] * incoming_ref[:slots]
        panel_ref[...] = jnp.where(panel < live_ref[:1], fresh, 0.0)
        send(panel_ref, panel_hbm)

    def emit(f):
        low, high = both(1, f)
        out_ref[f, 0] = rest_ref[f, 0] + low
        out_ref[f, ca - 1] = rest_ref[f, ca - 1] + high
        low, high = both(2, f)
        out_ref[f, 1] = rest_ref[f, 1] + low
        for a in range(2, ca - 2):
            out_ref[f, a] = rest_ref[f, a]
        out_ref[f, ca - 2] = rest_ref[f, ca - 2] + high
        if f % GROUP == GROUP - 1:
            some = pl.ds(f + 1 - GROUP, GROUP)
            send(out_ref.at[some], residual_ref.at[some])

    end_part(
        True, flags_ref, halo_ref, store_ref, kinds_ref, wing_ref, cond_ref, coef_ref,
        delta_ref, base_ref, fixed_ref, add_ref, beside_ref, mix_ref, early, emit,
    )
    for copy in copies:
        copy.wait()


def panel_kernel(
    chunk, visible, index_ref, block_ref, rows_ref, view_ref, out_ref
):
    slots = index_ref.shape[1]
    total, values = rows_ref.shape
    index = index_ref[...].T
    block = block_ref[...].T
    types = view_ref.shape[0]
    lane = lax.broadcasted_iota(jnp.int32, (slots, chunk), 1)

    def gather(start):
        rows = rows_ref[pl.ds(start, chunk), :]
        return tuple(
            jnp.dot(
                (index[:, k : k + 1] == lane + start).astype(f32).astype(bf16),
                rows,
                preferred_element_type=f32,
            )
            for k in range(visible)
        )

    if total == chunk:
        found = gather(0)
    else:
        zero = tuple(jnp.zeros((slots, values), f32) for _ in range(visible))

        def step(i, sums):
            return tuple(s + g for s, g in zip(sums, gather(pl.multiple_of(i * chunk, chunk))))

        found = lax.fori_loop(0, total // chunk, step, zero)
    out = jnp.zeros((slots, values), f32)
    for b in range(types):
        stack = jnp.concatenate(
            [jnp.where(block[:, k : k + 1] == b, found[k], 0.0) for k in range(visible)], axis=0
        ).astype(bf16)
        moved = lax.dot_general(
            stack, view_ref[b], (((1,), (1,)), ((), ())), preferred_element_type=f32
        )
        for k in range(visible):
            out = out + moved[k * slots : (k + 1) * slots]
    out_ref[...] = out


def pairs(count, first, closed):
    swaps = []
    for i in range(first, count if closed and first else count - 1, 2):
        j = (i + 1) % count
        swaps += [(i, j), (j, i)]
    return swaps


def swap(array, axis, first, closed=False):
    return lax.ppermute(array, axis, pairs(lax.axis_size(axis), first, closed))


def body(
    source, storage, materials, conductance, mixing, counts, vis_owner, vis_slot, vis_block,
    radiosity_old, view_blocks, emission, reflect,
):
    nf, ca, cz, cr = source.shape
    mats = mixing.shape[0]
    owners = lax.axis_size("axial")
    me = lax.axis_index("axial")
    is_even = me % 2 == 0
    flags = jnp.stack([is_even, me > 0, me + 1 < owners]).astype(f32)
    flags = jnp.broadcast_to(flags[:, None, None], (3, ROWS, cr))
    azim_even = lax.axis_index("azim") % 2 == 0
    here = pltpu.VMEM

    def call(kernel, outs, args, scratch=(), far_out=False, plain_args=False):
        specs = [VMEM] * len(outs)
        if far_out:
            specs[-1] = HBM
        if not plain_args:
            args = [pltpu.with_memory_space_constraint(x, pltpu.VMEM) for x in args]
        single = len(outs) == 1
        return pl.pallas_call(
            kernel,
            out_shape=outs[0] if single else tuple(outs),
            in_specs=[VMEM] * len(args),
            out_specs=specs[0] if single else tuple(specs),
            scratch_shapes=list(scratch),
            compiler_params=PARAMS, cost_estimate=CHEAP,
        )(*args)

    def after(value, *others):
        return lax.optimization_barrier((value, *others))[0]

    plain = here((nf, ca, cz, cr), f32)
    layers = here((2, nf, cz, cr), f32)
    small = (conductance[None], mixing.transpose(1, 0, 2))
    values = radiosity_old.shape[3]
    source, storage, materials, edges, sides, cond, coef = pl.pallas_call(
        ends_kernel,
        out_shape=(
            plain, plain, here((ca, cz, cr), jnp.int32), layers, here((nf + nf // 2 + 1, ca, ROWS, cr), f32),
            here((nf, ROWS, cr), f32), here((mats * nf * ROWS, 3 * nf * ROWS), bf16),
        ),
        in_specs=[VMEM] + [HBM] * 5,
        out_specs=(VMEM,) * 7,
        scratch_shapes=[here(x.shape, x.dtype) for x in small] + [pltpu.SemaphoreType.DMA((2 * COPIES + 3,))],
        compiler_params=PARAMS, cost_estimate=CHEAP,
    )(flags, *(pltpu.with_memory_space_constraint(x, pltpu.HBM) for x in (source, storage, materials, *small)))
    half = ROWS // 2
    to_right, to_left = sides[:, :, half:], sides[:, :, :half]
    far = jnp.where(azim_even, to_left, to_right).astype(LINK)
    near = jnp.where(azim_even, to_right, to_left).astype(LINK)
    slots, visible = vis_owner.shape[2:]
    tile = -(-slots // 16) * 16
    panels = jnp.pad(radiosity_old[0, 0], ((0, tile - slots), (0, 0)))
    fold = cr // values
    folded = panels.astype(f32) * RAD_SCALE
    folded = jnp.concatenate(jnp.split(folded, fold, axis=0), axis=1)
    far = far
    far_in = swap(far, "azim", 1, True)
    layer0 = after(edges, far)[1].reshape(nf * cz, cr)
    message0 = jnp.concatenate([layer0, folded], axis=0).astype(LINK)
    message = swap(message0, "axial", 0)
    near = after(near, message0)
    near_in = swap(near, "azim", 0)
    message1 = after(edges, near)[0].astype(LINK)
    halo1 = swap(message1, "axial", 1)

    from_right = jnp.where(azim_even, near_in, far_in)
    from_left = jnp.where(azim_even, far_in, near_in)
    wings = jnp.concatenate([from_right, from_left], axis=2).astype(f32)

    full = here((nf, ca, cz + ROWS, cr), f32)
    rest = call(first_kernel, (full,), (source, storage, materials, wings, cond, coef), (full, full))

    def side(first, halo):
        one = here((nf, 1, cz + ROWS, cr), f32)
        return call(
            functools.partial(side_kernel, first),
            (here((nf, 2 * cz + ROWS, cr), f32),),
            (flags, rest, halo, source, storage, materials, wings, cond, coef),
            (one, here((nf, cz, cr), f32), one),
        ).astype(LINK)

    message = after(message, rest)
    halo0 = message[: nf * cz].reshape(nf, cz, cr).astype(f32)
    message0 = side(False, halo0)
    second0 = swap(message0, "axial", 0).astype(f32)
    halo1 = after(halo1, message0).astype(f32)
    message1 = side(True, halo1)
    second1 = swap(message1, "axial", 1).astype(f32)
    rest3, total = call(
        later_kernel,
        (plain, plain),
        (flags, after(rest, message1), halo1, halo0, source, storage, materials, wings, cond, coef),
        (plain, full, full, full),
    )

    partner = after(message, message1)[nf * cz :].astype(f32) * (1.0 / RAD_SCALE)
    partner = jnp.concatenate(jnp.split(partner, fold, axis=1), axis=0).astype(bf16)
    if owners <= 8 and owners & (owners - 1) == 0:
        pair = jnp.concatenate([panels, partner], axis=0)
        others = [
            lax.ppermute(pair, "axial", [(i, i ^ step) for i in range(owners)]) for step in range(2, owners, 2)
        ]
        panels = jnp.concatenate([after(pair, second0), *others], axis=0)
        owner = vis_owner[0, 0].T ^ me
    else:
        pair = jnp.stack([panels, partner])
        panels = jnp.where(is_even, pair, pair[::-1]).reshape(2 * tile, values)
        groups = [list(range(k, owners, 2)) for k in range(2)]
        panels = lax.all_gather(panels, "axial", axis=0, tiled=True, axis_index_groups=groups)
        panels = panels.reshape(owners // 2, 2 * tile, values).reshape(owners * tile, values)
        owner = vis_owner[0, 0].T
    pad = ((0, -visible % ROWS), (0, -slots % 128))
    index = jnp.pad(owner * tile + vis_slot[0, 0].T, pad, constant_values=-1)
    block = jnp.pad(vis_block[0, 0].T, pad)
    chunk = tile * 8 if owners % 8 == 0 else tile * owners
    incoming = call(
        functools.partial(panel_kernel, chunk, visible),
        (here((index.shape[1], values), f32),),
        (index, block, panels, view_blocks),
        plain_args=True,
    )

    live = jnp.broadcast_to(after(counts, rest3), (ROWS, values))
    shape = jax.ShapeDtypeStruct
    one = here((nf, 1, cz + ROWS, cr), f32)
    deltas = here((3, nf, cz, cr), f32)
    parts = (here((nf, cz, cr), f32), one, one, here((nf, ROWS, cr), f32), one)
    delta0 = call(
        end_kernel, (deltas,), (flags, second0, storage, materials, wings, cond, coef), parts
    )
    panel_new, solution_out, residual = pl.pallas_call(
        last_kernel,
        out_shape=(shape((slots, values), f32), shape(plain.shape, f32), shape(plain.shape, f32)),
        in_specs=[VMEM] * 14,
        out_specs=(HBM, HBM, HBM),
        scratch_shapes=[
            here((slots, values), f32), layers, plain, deltas, *parts, pltpu.SemaphoreType.DMA((4 + nf // GROUP,))
        ],
        compiler_params=PARAMS, cost_estimate=CHEAP,
    )(
        flags, rest3, total, second1, delta0, storage, materials, wings, cond, coef,
        live, incoming, emission[0, 0], reflect[0, 0],
    )
    return (solution_out, residual, panel_new[None, None])


def solution(mesh):
    return jax.shard_map(
        body,
        mesh=mesh,
        in_specs=(
            P(None, "axial", "azim", None),
            P(None, "axial", "azim", None),
            P("axial", "azim", None),
            P(),
            P(),
            P("axial", "azim"),
            P("axial", "azim", None, None),
            P("axial", "azim", None, None),
            P("axial", "azim", None, None),
            P("axial", "azim", None, None),
            P(),
            P("axial", "azim", None, None),
            P("axial", "azim", None, None),
        ),
        out_specs=(
            P(None, "axial", "azim", None),
            P(None, "axial", "azim", None),
            P("axial", "azim", None, None),
        ),
        check_vma=False,
    )
```

```python
import functools
import jax
import jax.numpy as jnp
from jax import lax
from jax.experimental import pallas as pl
from jax.experimental.pallas import tpu as pltpu
from jax.sharding import PartitionSpec as P

center_value = 14.2
half_width = 13.8
sigma = center_value / half_width
ratio_0 = 1.0 / sigma
ratio_1 = 1.0 / (2.0 * sigma - ratio_0)
ratio_2 = 1.0 / (2.0 * sigma - ratio_1)
ALPHA = (None, ratio_1 * ratio_0, ratio_2 * ratio_1)
BETA = (None, 2.0 * ratio_1 / half_width, 2.0 * ratio_2 / half_width)
INV_CENTER = 1.0 / center_value

GROUP = 4
COPIES = 4
ROWS = 8
LINK = jnp.float16
RAD_SCALE = 8192.0
f32, bf16 = jnp.float32, jnp.bfloat16

VMEM = pl.BlockSpec(memory_space=pltpu.VMEM)
HBM = pl.BlockSpec(memory_space=pl.ANY)
PARAMS = pltpu.CompilerParams(vmem_limit_bytes=16 * 1024 * 1024)
CHEAP = pl.CostEstimate(flops=0, bytes_accessed=0, transcendentals=0)


def each_field(count, step):
    for f in range(count):
        step(f)


def tall(tile, height):
    return jnp.concatenate([tile] * (height // ROWS), axis=0)


def mixed_part(cells, kinds, coef, out_ref, a, rows):
    nf, height, cr = cells.shape
    flat = cells.reshape(nf * height, cr)
    high = flat.astype(bf16)
    low = (flat - high.astype(f32)).astype(bf16)
    out = jnp.dot(coef, jnp.concatenate([high, high, low], axis=0), preferred_element_type=f32)
    mats = out.shape[0] // (nf * height)
    out = out.reshape(nf, mats, height, cr)
    is_kind = [kinds == m for m in range(mats - 1)]
    for f in range(nf):
        picked = out[f, mats - 1]
        for m in range(mats - 1):
            picked = jnp.where(is_kind[m], out[f, m], picked)
        out_ref[f, a, rows] = picked


def radial_sum(cells):
    cr = cells.shape[-1]
    lane = lax.broadcasted_iota(jnp.int32, cells.shape, cells.ndim - 1)
    inner = jnp.where(lane == 0, 0.0, pltpu.roll(cells, 1, cells.ndim - 1))
    outer = jnp.where(lane == cr - 1, 0.0, pltpu.roll(cells, cr - 1, cells.ndim - 1))
    return inner + outer


def azim_sum(cells):
    rows = cells.shape[0]
    return pltpu.roll(cells, 1, 0) + pltpu.roll(cells, rows - 1, 0)


def apply_local(dir_ref, store, kinds, cond_ref, coef, mix_ref, span, emit, linked=True):
    nf, ca = dir_ref.shape[:2]
    start, stop = span
    for a in range(ca):
        for t in range(start // ROWS, stop // ROWS):
            rows = slice(t * ROWS, (t + 1) * ROWS)
            mixed_part(dir_ref[:, a, rows], kinds(a, t), coef, mix_ref, a, rows)

    def step(f):
        cond = tall(cond_ref[f], stop - start)
        planes = [dir_ref[f, a] for a in range(ca)]
        for a in range(ca):
            cells = planes[a][start:stop]
            around = azim_sum(planes[a])[start:stop] + radial_sum(cells)
            if linked and a > 0:
                around = around + planes[a - 1][start:stop]
            if linked and a + 1 < ca:
                around = around + planes[a + 1][start:stop]
            emit(f, a, store(f, a) * cells + mix_ref[f, a, start:stop] - cond * around)

    each_field(nf, step)


def swapped(tile):
    place = lax.broadcasted_iota(jnp.int32, tile.shape, 0)
    return jnp.where((place // 2) % 2 == 0, pltpu.roll(tile, ROWS - 2, 0), pltpu.roll(tile, 2, 0))


def coef_rows(mixes):
    tall_rows, nf = mixes.shape
    wide, inner = tall_rows * ROWS, nf * ROWS
    high = mixes.astype(bf16)
    low = (mixes - high.astype(f32)).astype(bf16)
    row = lax.broadcasted_iota(jnp.int32, (wide, tall_rows), 0)
    col = lax.broadcasted_iota(jnp.int32, (wide, tall_rows), 1)
    down = (row // ROWS == col).astype(bf16)
    row = lax.broadcasted_iota(jnp.int32, (nf, inner), 0)
    col = lax.broadcasted_iota(jnp.int32, (nf, inner), 1)
    across = (col // ROWS == row).astype(bf16)
    row = lax.broadcasted_iota(jnp.int32, (wide, inner), 0)
    col = lax.broadcasted_iota(jnp.int32, (wide, inner), 1)
    same = row % ROWS == col % ROWS

    def spread(part):
        part = jnp.dot(down, part, preferred_element_type=f32).astype(bf16)
        full = jnp.dot(part, across, preferred_element_type=f32)
        return jnp.where(same, full, 0.0).astype(bf16)

    high = spread(high)
    return high, spread(low), high


def ends_kernel(
    source_hbm, store_hbm, kinds_hbm, cond_hbm, mix_hbm,
    source_ref, store_ref, kinds_ref, edge_ref, side_ref, cond_ref, coef_ref,
    cond_row, mix_rows, sems,
):
    nf, ca, cz, cr = source_ref.shape
    part = nf // COPIES
    pairs_of = [(cond_hbm, cond_row), (mix_hbm, mix_rows)] + [
        (far.at[pl.ds(i * part, part)], near.at[pl.ds(i * part, part)])
        for far, near in ((source_hbm, source_ref), (store_hbm, store_ref))
        for i in range(COPIES)
    ] + [(kinds_hbm, kinds_ref)]
    copies = [pltpu.make_async_copy(far, near, sems.at[i]) for i, (far, near) in enumerate(pairs_of)]
    for copy in copies:
        copy.start()
    place = lax.broadcasted_iota(jnp.int32, (ROWS, cr), 0)

    copies[0].wait()
    copies[1].wait()
    for f in range(nf):
        cond_ref[f] = jnp.broadcast_to(cond_row[:, f : f + 1], (ROWS, cr))
    mats = mix_rows.shape[1]
    mixes = jnp.concatenate([mix_rows[f] for f in range(nf)], axis=0)
    row = lax.broadcasted_iota(jnp.int32, mixes.shape, 0)
    col = lax.broadcasted_iota(jnp.int32, mixes.shape, 1)
    mixes = mixes + jnp.where(row // mats == col, 6.0 * cond_row[...], 0.0)
    inner = nf * ROWS
    for i, rows in enumerate(coef_rows(mixes)):
        coef_ref[:, i * inner : (i + 1) * inner] = rows

    def both(ref, *lead):
        return jnp.where(place < ROWS // 2, ref[(*lead, slice(0, ROWS))], ref[(*lead, slice(cz - ROWS, cz))])

    for f in range(nf):
        if f % part == 0:
            copies[2 + f // part].wait()
        edge_ref[0, f] = source_ref[f, 0] * INV_CENTER
        edge_ref[1, f] = source_ref[f, ca - 1] * INV_CENTER
        for a in range(ca):
            side_ref[f, a] = both(source_ref, f, a) * INV_CENTER
    for copy in copies[2 + COPIES :]:
        copy.wait()
    outer = (place < 2) | (place >= ROWS - 2)
    for f in range(nf // 2):
        for a in range(ca):
            side_ref[nf + f, a] = jnp.where(
                outer, both(store_ref, f, a), swapped(both(store_ref, nf // 2 + f, a))
            )
    for a in range(ca):
        side_ref[nf + nf // 2, a] = both(kinds_ref, a).astype(f32)


def wing_store(wing_ref, f, a):
    nf = wing_ref.shape[0] // 3 * 2
    if f < nf // 2:
        return wing_ref[nf + f, a]
    return swapped(wing_ref[nf // 2 + f, a])


def first_kernel(
    source_ref, store_ref, kinds_ref, wing_ref, cond_ref, coef_ref,
    rest_ref, dir_ref, mix_ref,
):
    nf, ca, cz, cr = source_ref.shape
    own = cz // ROWS
    for f in range(nf):
        for a in range(ca):
            dir_ref[f, a, :cz] = source_ref[f, a] * INV_CENTER
            dir_ref[f, a, cz:] = wing_ref[f, a]

    def store(f, a):
        return jnp.concatenate([store_ref[f, a], wing_store(wing_ref, f, a)], axis=0)

    def kinds(a, t):
        return kinds_ref[a, t * ROWS : (t + 1) * ROWS].astype(f32) if t < own else wing_ref[nf + nf // 2, a]

    def emit(f, a, image):
        origin = jnp.concatenate([source_ref[f, a], center_value * wing_ref[f, a]], axis=0)
        rest_ref[f, a] = origin - image

    apply_local(dir_ref, store, kinds, cond_ref, coef_ref[...], mix_ref, (0, cz + ROWS), emit)


def beside_rows(wing, beside):
    place = lax.broadcasted_iota(jnp.int32, wing.shape, 0)
    moved = jnp.where(place < 4, pltpu.roll(wing, 2, 0), pltpu.roll(wing, 6, 0))
    return jnp.where((place >= 2) & (place <= 5), moved, beside)


KEPT = 6


def put_beside(message_ref, start, rows):
    message_ref[start : start + 1] = rows[:1]
    message_ref[start + 1 : start + 5] = rows[2:6]
    message_ref[start + 5 : start + 6] = rows[7:]


def get_beside(message_ref, start):
    first, inner, last = (message_ref[start + a : start + b] for a, b in ((0, 1), (1, 5), (5, 6)))
    return jnp.concatenate([first, first, inner, last, last], axis=0)


def side_kernel(
    first, flags_ref, rest_ref, halo_ref, source_ref, store_ref, kinds_ref, wing_ref, cond_ref, coef_ref,
    message_ref, dir_ref, next_ref, mix_ref,
):
    nf, ca, cz, cr = source_ref.shape
    even = flags_ref[0] > 0.5

    def choose(low, high):
        mask = tall(even, low.shape[0])
        return jnp.where(mask, low, high) if first else jnp.where(mask, high, low)

    for f in range(nf):
        rest = choose(rest_ref[f, 0], rest_ref[f, ca - 1])
        wing = choose(wing_ref[f, 0], wing_ref[f, ca - 1])
        own = rest[:cz] + tall(cond_ref[f], cz) * halo_ref[f]
        direction = (ALPHA[1] * INV_CENTER) * choose(source_ref[f, 0], source_ref[f, ca - 1]) + BETA[1] * own
        beside = ALPHA[1] * wing + BETA[1] * rest[cz:]
        next_ref[f] = (ALPHA[1] * INV_CENTER) * choose(source_ref[f, 1], source_ref[f, ca - 2]) + BETA[1] * choose(
            rest_ref[f, 1, :cz], rest_ref[f, ca - 2, :cz]
        )
        dir_ref[f, 0, :cz] = direction
        dir_ref[f, 0, cz:] = beside
        message_ref[2 * f * cz : (2 * f + 1) * cz] = direction
        message_ref[(2 * f + 1) * cz : 2 * (f + 1) * cz] = own
        put_beside(message_ref, 2 * nf * cz + KEPT * f, beside_rows(wing, beside))

    def kinds(a, t):
        rows = slice(t * ROWS, (t + 1) * ROWS)
        return choose(kinds_ref[0, rows].astype(f32), kinds_ref[ca - 1, rows].astype(f32))

    def emit(f, a, image):
        third = pl.ds((2 * f + 1) * cz, cz)
        rest = message_ref[third] - image + tall(cond_ref[f], cz) * next_ref[f]
        message_ref[third] = ALPHA[2] * dir_ref[f, 0, :cz] + BETA[2] * rest

    apply_local(
        dir_ref, lambda f, a: choose(store_ref[f, 0], store_ref[f, ca - 1]), kinds,
        cond_ref, coef_ref[...], mix_ref, (0, cz), emit,
    )


def second_part(
    flags_ref, rest_ref, halo1_ref, halo0_ref, source_ref, store_ref, kinds_ref, wing_ref, cond_ref, coef_ref,
    newrest_ref, dir_ref, mix_ref,
):
    nf, ca, cz, cr = store_ref.shape
    even = tall(flags_ref[0], cz) > 0.5
    for f in range(nf):
        cond = tall(cond_ref[f], cz)
        arrived = {
            0: cond * jnp.where(even, halo1_ref[f], halo0_ref[f]),
            ca - 1: cond * jnp.where(even, halo0_ref[f], halo1_ref[f]),
        }
        for a in range(ca):
            rest = rest_ref[f, a, :cz]
            if a in arrived:
                rest = rest + arrived[a]
            newrest_ref[f, a] = rest
            dir_ref[f, a, :cz] = (ALPHA[1] * INV_CENTER) * source_ref[f, a] + BETA[1] * rest
            dir_ref[f, a, cz:] = ALPHA[1] * wing_ref[f, a] + BETA[1] * rest_ref[f, a, cz:]

    def emit(f, a, image):
        newrest_ref[f, a] = newrest_ref[f, a] - image

    apply_local(
        dir_ref, lambda f, a: store_ref[f, a], lambda a, t: kinds_ref[a, t * ROWS : (t + 1) * ROWS].astype(f32),
        cond_ref, coef_ref[...], mix_ref, (0, cz), emit,
    )


def inward(beside, cz):
    place = lax.broadcasted_iota(jnp.int32, beside.shape, 0)
    ends = [jnp.where(place == 0, pltpu.roll(beside, 1, 0), 0.0)]
    ends += [jnp.zeros_like(beside)] * (cz // ROWS - 2)
    ends += [jnp.where(place == ROWS - 1, pltpu.roll(beside, ROWS - 1, 0), 0.0)]
    return jnp.concatenate(ends, axis=0)


def third_part(
    flags_ref, rest_ref, second_ref, first_rest_ref, source_ref, store_ref, kinds_ref, wing_ref, cond_ref, coef_ref,
    out_ref, total_ref, dir_ref, mix_ref,
):
    nf, ca, cz, cr = source_ref.shape
    partner = {0: flags_ref[1] > 0.5, ca - 1: flags_ref[2] > 0.5}
    for f in range(nf):
        cond = cond_ref[f]
        wide = tall(cond, cz)
        for a in range(ca):
            rest = rest_ref[f, a]
            direction = second_ref[f, a, :cz]
            ahead = ALPHA[2] * direction + BETA[2] * rest
            if a in partner:
                mine = inward(cond * wing_ref[f, a], cz)
                third = BETA[2] * wide * (direction + BETA[1] * mine)
                rest = rest + jnp.where(tall(partner[a], cz), wide * third, 0.0)
            out_ref[f, a] = rest
            dir_ref[f, a, :cz] = ahead
            total_ref[f, a] = source_ref[f, a] * INV_CENTER + direction + ahead

    def wing_emit(f, a, image):
        rest = first_rest_ref[f, a, cz:] - image
        if a in partner:
            cond = cond_ref[f]
            rest = rest + jnp.where(partner[a], BETA[1] * cond * cond * wing_ref[f, a], 0.0)
        dir_ref[f, a, cz:] = ALPHA[2] * second_ref[f, a, cz:] + BETA[2] * rest

    apply_local(
        second_ref, lambda f, a: wing_store(wing_ref, f, a), lambda a, t: wing_ref[nf + nf // 2, a],
        cond_ref, coef_ref[...], mix_ref, (cz, cz + ROWS), wing_emit,
    )

    def emit(f, a, image):
        out_ref[f, a] = out_ref[f, a] - image

    apply_local(
        dir_ref, lambda f, a: store_ref[f, a], lambda a, t: kinds_ref[a, t * ROWS : (t + 1) * ROWS].astype(f32),
        cond_ref, coef_ref[...], mix_ref, (0, cz), emit,
    )


def later_kernel(
    flags_ref, rest_ref, halo1_ref, halo0_ref, source_ref, store_ref, kinds_ref, wing_ref, cond_ref, coef_ref,
    out_ref, total_ref, second_rest_ref, second_ref, dir_ref, mix_ref,
):
    second_part(
        flags_ref, rest_ref, halo1_ref, halo0_ref, source_ref, store_ref, kinds_ref, wing_ref, cond_ref, coef_ref,
        second_rest_ref, second_ref, mix_ref,
    )
    third_part(
        flags_ref, second_rest_ref, second_ref, rest_ref, source_ref, store_ref, kinds_ref, wing_ref, cond_ref,
        coef_ref, out_ref, total_ref, dir_ref, mix_ref,
    )


def end_part(
    first, flags_ref, halo_ref, store_ref, kinds_ref, wing_ref, cond_ref, coef_ref,
    delta_ref, base_ref, fixed_ref, add_ref, beside_ref, mix_ref, early, emit,
):
    nf, ca, cz, cr = store_ref.shape
    even = flags_ref[0] > 0.5

    def choose(low, high):
        mask = tall(even, low.shape[0])
        return jnp.where(mask, low, high) if first else jnp.where(mask, high, low)

    place = lax.broadcasted_iota(jnp.int32, (ROWS, cr), 0)
    outer = (place <= 1) | (place >= 6)
    for f in range(nf):
        cond = cond_ref[f]
        wide = tall(cond, cz)
        old = get_beside(halo_ref, 2 * nf * cz + KEPT * f)
        moved = jnp.where(place < 4, pltpu.roll(old, ROWS - 2, 0), pltpu.roll(old, 2, 0))
        fix = cond * jnp.where(outer, moved, 0.0)
        rest = wide * (halo_ref[2 * f * cz : (2 * f + 1) * cz] + BETA[1] * inward(fix, cz))
        base_ref[f] = rest + wide * halo_ref[(2 * f + 1) * cz : 2 * (f + 1) * cz]
        fixed_ref[f, 0, :cz] = jnp.zeros_like(rest)
        fixed_ref[f, 0, cz:] = BETA[1] * fix
        beside_ref[f] = fix + cond * old
        add_ref[f, 0, :cz] = BETA[2] * rest
        delta_ref[0, f] = BETA[2] * rest
    early()

    def wing_emit(f, a, image):
        add_ref[f, 0, cz:] = ALPHA[2] * fixed_ref[f, 0, cz:] + BETA[2] * (beside_ref[f] - image)

    def wing_choice(f, a):
        return choose(wing_store(wing_ref, f, 0), wing_store(wing_ref, f, ca - 1))

    def wing_kinds(a, t):
        return choose(wing_ref[nf + nf // 2, 0], wing_ref[nf + nf // 2, ca - 1])

    apply_local(
        fixed_ref, wing_choice, wing_kinds, cond_ref, coef_ref[...], mix_ref, (cz, cz + ROWS), wing_emit, linked=False
    )

    def own_emit(f, a, image):
        cond = cond_ref[f]
        delta_ref[1, f] = base_ref[f] - image
        inner = add_ref[f, 0, :cz] + inward(BETA[2] * cond * fixed_ref[f, 0, cz:], cz)
        delta_ref[2, f] = tall(cond, cz) * inner
        emit(f)

    def kinds(a, t):
        rows = slice(t * ROWS, (t + 1) * ROWS)
        return choose(kinds_ref[0, rows].astype(f32), kinds_ref[ca - 1, rows].astype(f32))

    apply_local(
        add_ref, lambda f, a: choose(store_ref[f, 0], store_ref[f, ca - 1]), kinds,
        cond_ref, coef_ref[...], mix_ref, (0, cz), own_emit, linked=False,
    )


def end_kernel(
    flags_ref, halo_ref, store_ref, kinds_ref, wing_ref, cond_ref, coef_ref,
    delta_ref, base_ref, fixed_ref, add_ref, beside_ref, mix_ref,
):
    end_part(
        False, flags_ref, halo_ref, store_ref, kinds_ref, wing_ref, cond_ref, coef_ref,
        delta_ref, base_ref, fixed_ref, add_ref, beside_ref, mix_ref, lambda: None, lambda f: None,
    )


def last_kernel(
    flags_ref, rest_ref, total_ref, halo_ref, other_ref, store_ref, kinds_ref, wing_ref, cond_ref, coef_ref,
    live_ref, incoming_ref, emission_ref, reflect_ref,
    panel_hbm, solution_ref, residual_ref,
    panel_ref, end_ref, out_ref, delta_ref, base_ref, fixed_ref, add_ref, beside_ref, mix_ref, sems,
):
    nf, ca, cz, cr = store_ref.shape
    even = tall(flags_ref[0], cz) > 0.5
    copies = []

    def send(near, far):
        copies.append(pltpu.make_async_copy(near, far, sems.at[len(copies)]))
        copies[-1].start()

    send(total_ref.at[:, 1 : ca - 1], solution_ref.at[:, 1 : ca - 1])

    def both(i, f):
        one, other = delta_ref[i, f], other_ref[i, f]
        return jnp.where(even, one, other), jnp.where(even, other, one)

    def early():
        for f in range(nf):
            low, high = both(0, f)
            end_ref[0, f] = total_ref[f, 0] + low
            end_ref[1, f] = total_ref[f, ca - 1] + high
        send(end_ref.at[0], solution_ref.at[:, 0])
        send(end_ref.at[1], solution_ref.at[:, ca - 1])
        slots, values = panel_ref.shape
        wall = [end_ref[0, 0]] + [total_ref[0, a] for a in range(1, ca - 1)] + [end_ref[1, 0]]
        wall = jnp.concatenate(wall, axis=0)[:, cr - 1 : cr]
        wall = jnp.broadcast_to(wall, (ca * cz, values))
        wall = jnp.concatenate([wall] * (-(-slots // (ca * cz))), axis=0)[:slots]
        panel = lax.broadcasted_iota(jnp.int32, (slots, values), 0)
        fresh = emission_ref[...] * wall + reflect_ref[...] * incoming_ref[:slots]
        panel_ref[...] = jnp.where(panel < live_ref[:1], fresh, 0.0)
        send(panel_ref, panel_hbm)

    def emit(f):
        low, high = both(1, f)
        out_ref[f, 0] = rest_ref[f, 0] + low
        out_ref[f, ca - 1] = rest_ref[f, ca - 1] + high
        low, high = both(2, f)
        out_ref[f, 1] = rest_ref[f, 1] + low
        for a in range(2, ca - 2):
            out_ref[f, a] = rest_ref[f, a]
        out_ref[f, ca - 2] = rest_ref[f, ca - 2] + high
        if f % GROUP == GROUP - 1:
            some = pl.ds(f + 1 - GROUP, GROUP)
            send(out_ref.at[some], residual_ref.at[some])

    end_part(
        True, flags_ref, halo_ref, store_ref, kinds_ref, wing_ref, cond_ref, coef_ref,
        delta_ref, base_ref, fixed_ref, add_ref, beside_ref, mix_ref, early, emit,
    )
    for copy in copies:
        copy.wait()


def panel_kernel(
    chunk, visible, index_ref, block_ref, rows_ref, view_ref, out_ref
):
    slots = index_ref.shape[1]
    total, values = rows_ref.shape
    index = index_ref[...].T
    block = block_ref[...].T
    types = view_ref.shape[0]
    lane = lax.broadcasted_iota(jnp.int32, (slots, chunk), 1)

    def gather(start):
        rows = rows_ref[pl.ds(start, chunk), :]
        return tuple(
            jnp.dot(
                (index[:, k : k + 1] == lane + start).astype(f32).astype(bf16),
                rows,
                preferred_element_type=f32,
            )
            for k in range(visible)
        )

    if total == chunk:
        found = gather(0)
    else:
        zero = tuple(jnp.zeros((slots, values), f32) for _ in range(visible))

        def step(i, sums):
            return tuple(s + g for s, g in zip(sums, gather(pl.multiple_of(i * chunk, chunk))))

        found = lax.fori_loop(0, total // chunk, step, zero)
    out = jnp.zeros((slots, values), f32)
    for b in range(types):
        stack = jnp.concatenate(
            [jnp.where(block[:, k : k + 1] == b, found[k], 0.0) for k in range(visible)], axis=0
        ).astype(bf16)
        moved = lax.dot_general(
            stack, view_ref[b], (((1,), (1,)), ((), ())), preferred_element_type=f32
        )
        for k in range(visible):
            out = out + moved[k * slots : (k + 1) * slots]
    out_ref[...] = out


def pairs(count, first, closed):
    swaps = []
    for i in range(first, count if closed and first else count - 1, 2):
        j = (i + 1) % count
        swaps += [(i, j), (j, i)]
    return swaps


def swap(array, axis, first, closed=False):
    return lax.ppermute(array, axis, pairs(lax.axis_size(axis), first, closed))


def body(
    source, storage, materials, conductance, mixing, counts, vis_owner, vis_slot, vis_block,
    radiosity_old, view_blocks, emission, reflect,
):
    nf, ca, cz, cr = source.shape
    mats = mixing.shape[0]
    owners = lax.axis_size("axial")
    me = lax.axis_index("axial")
    is_even = me % 2 == 0
    flags = jnp.stack([is_even, me > 0, me + 1 < owners]).astype(f32)
    flags = jnp.broadcast_to(flags[:, None, None], (3, ROWS, cr))
    azim_even = lax.axis_index("azim") % 2 == 0
    here = pltpu.VMEM

    def call(kernel, outs, args, scratch=(), far_out=False, plain_args=False):
        specs = [VMEM] * len(outs)
        if far_out:
            specs[-1] = HBM
        if not plain_args:
            args = [pltpu.with_memory_space_constraint(x, pltpu.VMEM) for x in args]
        single = len(outs) == 1
        return pl.pallas_call(
            kernel,
            out_shape=outs[0] if single else tuple(outs),
            in_specs=[VMEM] * len(args),
            out_specs=specs[0] if single else tuple(specs),
            scratch_shapes=list(scratch),
            compiler_params=PARAMS, cost_estimate=CHEAP,
        )(*args)

    def after(value, *others):
        return lax.optimization_barrier((value, *others))[0]

    plain = here((nf, ca, cz, cr), f32)
    layers = here((2, nf, cz, cr), f32)
    small = (conductance[None], mixing.transpose(1, 0, 2))
    values = radiosity_old.shape[3]
    source, storage, materials, edges, sides, cond, coef = pl.pallas_call(
        ends_kernel,
        out_shape=(
            plain, plain, here((ca, cz, cr), jnp.int32), layers, here((nf + nf // 2 + 1, ca, ROWS, cr), f32),
            here((nf, ROWS, cr), f32), here((mats * nf * ROWS, 3 * nf * ROWS), bf16),
        ),
        in_specs=[HBM] * 5,
        out_specs=(VMEM,) * 7,
        scratch_shapes=[here(x.shape, x.dtype) for x in small] + [pltpu.SemaphoreType.DMA((2 * COPIES + 3,))],
        compiler_params=PARAMS, cost_estimate=CHEAP,
    )(*(pltpu.with_memory_space_constraint(x, pltpu.HBM) for x in (source, storage, materials, *small)))
    edges = jnp.where(is_even, edges, edges[::-1])
    half = ROWS // 2
    to_right, to_left = sides[:, :, half:], sides[:, :, :half]
    far = jnp.where(azim_even, to_left, to_right).astype(LINK)
    near = jnp.where(azim_even, to_right, to_left).astype(LINK)
    slots, visible = vis_owner.shape[2:]
    tile = -(-slots // 16) * 16
    panels = jnp.pad(radiosity_old[0, 0], ((0, tile - slots), (0, 0)))
    fold = cr // values
    folded = panels.astype(f32) * RAD_SCALE
    folded = jnp.concatenate(jnp.split(folded, fold, axis=0), axis=1)
    far = far
    far_in = swap(far, "azim", 1, True)
    layer0 = after(edges, far)[1].reshape(nf * cz, cr)
    message0 = jnp.concatenate([layer0, folded], axis=0).astype(LINK)
    message = swap(message0, "axial", 0)
    near = after(near, message0)
    near_in = swap(near, "azim", 0)
    message1 = after(edges, near)[0].astype(LINK)
    halo1 = swap(message1, "axial", 1)

    from_right = jnp.where(azim_even, near_in, far_in)
    from_left = jnp.where(azim_even, far_in, near_in)
    wings = jnp.concatenate([from_right, from_left], axis=2).astype(f32)

    full = here((nf, ca, cz + ROWS, cr), f32)
    rest = call(first_kernel, (full,), (source, storage, materials, wings, cond, coef), (full, full))

    def side(first, halo):
        one = here((nf, 1, cz + ROWS, cr), f32)
        return call(
            functools.partial(side_kernel, first),
            (here((nf * (2 * cz + KEPT), cr), f32),),
            (flags, rest, halo, source, storage, materials, wings, cond, coef),
            (one, here((nf, cz, cr), f32), one),
        ).astype(LINK)

    message = after(message, rest)
    halo0 = message[: nf * cz].reshape(nf, cz, cr).astype(f32)
    message0 = side(False, halo0)
    second0 = swap(message0, "axial", 0).astype(f32)
    halo1 = after(halo1, message0).astype(f32)
    message1 = side(True, halo1)
    second1 = swap(message1, "axial", 1).astype(f32)
    rest3, total = call(
        later_kernel,
        (plain, plain),
        (flags, after(rest, message1), halo1, halo0, source, storage, materials, wings, cond, coef),
        (plain, full, full, full),
    )

    partner = after(message, message1)[nf * cz :].astype(f32) * (1.0 / RAD_SCALE)
    partner = jnp.concatenate(jnp.split(partner, fold, axis=1), axis=0).astype(bf16)
    if owners <= 8 and owners & (owners - 1) == 0:
        pair = jnp.concatenate([panels, partner], axis=0)
        others = [
            lax.ppermute(pair, "axial", [(i, i ^ step) for i in range(owners)]) for step in range(2, owners, 2)
        ]
        panels = jnp.concatenate([after(pair, second0), *others], axis=0)
        owner = vis_owner[0, 0].T ^ me
    else:
        pair = jnp.stack([panels, partner])
        panels = jnp.where(is_even, pair, pair[::-1]).reshape(2 * tile, values)
        groups = [list(range(k, owners, 2)) for k in range(2)]
        panels = lax.all_gather(panels, "axial", axis=0, tiled=True, axis_index_groups=groups)
        panels = panels.reshape(owners // 2, 2 * tile, values).reshape(owners * tile, values)
        owner = vis_owner[0, 0].T
    pad = ((0, -visible % ROWS), (0, -slots % 128))
    index = jnp.pad(owner * tile + vis_slot[0, 0].T, pad, constant_values=-1)
    block = jnp.pad(vis_block[0, 0].T, pad)
    chunk = tile * 8 if owners % 8 == 0 else tile * owners
    incoming = call(
        functools.partial(panel_kernel, chunk, visible),
        (here((index.shape[1], values), f32),),
        (index, block, panels, view_blocks),
        plain_args=True,
    )

    live = jnp.broadcast_to(after(counts, rest3), (ROWS, values))
    shape = jax.ShapeDtypeStruct
    one = here((nf, 1, cz + ROWS, cr), f32)
    deltas = here((3, nf, cz, cr), f32)
    parts = (here((nf, cz, cr), f32), one, one, here((nf, ROWS, cr), f32), one)
    delta0 = call(
        end_kernel, (deltas,), (flags, second0, storage, materials, wings, cond, coef), parts
    )
    panel_new, solution_out, residual = pl.pallas_call(
        last_kernel,
        out_shape=(shape((slots, values), f32), shape(plain.shape, f32), shape(plain.shape, f32)),
        in_specs=[VMEM] * 14,
        out_specs=(HBM, HBM, HBM),
        scratch_shapes=[
            here((slots, values), f32), layers, plain, deltas, *parts, pltpu.SemaphoreType.DMA((4 + nf // GROUP,))
        ],
        compiler_params=PARAMS, cost_estimate=CHEAP,
    )(
        flags, rest3, total, second1, delta0, storage, materials, wings, cond, coef,
        live, incoming, emission[0, 0], reflect[0, 0],
    )
    return (solution_out, residual, panel_new[None, None])


def solution(mesh):
    return jax.shard_map(
        body,
        mesh=mesh,
        in_specs=(
            P(None, "axial", "azim", None),
            P(None, "axial", "azim", None),
            P("axial", "azim", None),
            P(),
            P(),
            P("axial", "azim"),
            P("axial", "azim", None, None),
            P("axial", "azim", None, None),
            P("axial", "azim", None, None),
            P("axial", "azim", None, None),
            P(),
            P("axial", "azim", None, None),
            P("axial", "azim", None, None),
        ),
        out_specs=(
            P(None, "axial", "azim", None),
            P(None, "axial", "azim", None),
            P("axial", "azim", None, None),
        ),
        check_vma=False,
    )
```

```python
import functools
import jax
import jax.numpy as jnp
from jax import lax
from jax.experimental import pallas as pl
from jax.experimental.pallas import tpu as pltpu
from jax.sharding import PartitionSpec as P

center_value = 14.2
half_width = 13.8
sigma = center_value / half_width
ratio_0 = 1.0 / sigma
ratio_1 = 1.0 / (2.0 * sigma - ratio_0)
ratio_2 = 1.0 / (2.0 * sigma - ratio_1)
ALPHA = (None, ratio_1 * ratio_0, ratio_2 * ratio_1)
BETA = (None, 2.0 * ratio_1 / half_width, 2.0 * ratio_2 / half_width)
INV_CENTER = 1.0 / center_value

GROUP = 4
COPIES = 4
ROWS = 8
LINK = jnp.float16
SIDE_SCALE = 2.0**14
FIRST_SCALE = 2.0**15
SECOND_SCALE = 2.0**9
RAD_SCALE = 8192.0
f32, bf16 = jnp.float32, jnp.bfloat16

VMEM = pl.BlockSpec(memory_space=pltpu.VMEM)
HBM = pl.BlockSpec(memory_space=pl.ANY)
PARAMS = pltpu.CompilerParams(vmem_limit_bytes=16 * 1024 * 1024)
CHEAP = pl.CostEstimate(flops=0, bytes_accessed=0, transcendentals=0)


def each_field(count, step):
    for f in range(count):
        step(f)


def tall(tile, height):
    return jnp.concatenate([tile] * (height // ROWS), axis=0)


def mixed_part(cells, kinds, coef, out_ref, a, rows):
    nf, height, cr = cells.shape
    flat = cells.reshape(nf * height, cr)
    high = flat.astype(bf16)
    low = (flat - high.astype(f32)).astype(bf16)
    out = jnp.dot(coef, jnp.concatenate([high, high, low], axis=0), preferred_element_type=f32)
    mats = out.shape[0] // (nf * height)
    out = out.reshape(nf, mats, height, cr)
    is_kind = [kinds == m for m in range(mats - 1)]
    for f in range(nf):
        picked = out[f, mats - 1]
        for m in range(mats - 1):
            picked = jnp.where(is_kind[m], out[f, m], picked)
        out_ref[f, a, rows] = picked


def radial_sum(cells):
    cr = cells.shape[-1]
    lane = lax.broadcasted_iota(jnp.int32, cells.shape, cells.ndim - 1)
    inner = jnp.where(lane == 0, 0.0, pltpu.roll(cells, 1, cells.ndim - 1))
    outer = jnp.where(lane == cr - 1, 0.0, pltpu.roll(cells, cr - 1, cells.ndim - 1))
    return inner + outer


def azim_sum(cells):
    rows = cells.shape[0]
    return pltpu.roll(cells, 1, 0) + pltpu.roll(cells, rows - 1, 0)


def apply_local(dir_ref, store, kinds, cond_ref, coef, mix_ref, span, emit, linked=True):
    nf, ca = dir_ref.shape[:2]
    start, stop = span
    for a in range(ca):
        for t in range(start // ROWS, stop // ROWS):
            rows = slice(t * ROWS, (t + 1) * ROWS)
            mixed_part(dir_ref[:, a, rows], kinds(a, t), coef, mix_ref, a, rows)

    def step(f):
        cond = tall(cond_ref[f], stop - start)
        planes = [dir_ref[f, a] for a in range(ca)]
        for a in range(ca):
            cells = planes[a][start:stop]
            around = azim_sum(planes[a])[start:stop] + radial_sum(cells)
            if linked and a > 0:
                around = around + planes[a - 1][start:stop]
            if linked and a + 1 < ca:
                around = around + planes[a + 1][start:stop]
            emit(f, a, store(f, a) * cells + mix_ref[f, a, start:stop] - cond * around)

    each_field(nf, step)


def swapped(tile):
    place = lax.broadcasted_iota(jnp.int32, tile.shape, 0)
    return jnp.where((place // 2) % 2 == 0, pltpu.roll(tile, ROWS - 2, 0), pltpu.roll(tile, 2, 0))


def coef_rows(mixes):
    tall_rows, nf = mixes.shape
    wide, inner = tall_rows * ROWS, nf * ROWS
    high = mixes.astype(bf16)
    low = (mixes - high.astype(f32)).astype(bf16)
    row = lax.broadcasted_iota(jnp.int32, (wide, tall_rows), 0)
    col = lax.broadcasted_iota(jnp.int32, (wide, tall_rows), 1)
    down = (row // ROWS == col).astype(bf16)
    row = lax.broadcasted_iota(jnp.int32, (nf, inner), 0)
    col = lax.broadcasted_iota(jnp.int32, (nf, inner), 1)
    across = (col // ROWS == row).astype(bf16)
    row = lax.broadcasted_iota(jnp.int32, (wide, inner), 0)
    col = lax.broadcasted_iota(jnp.int32, (wide, inner), 1)
    same = row % ROWS == col % ROWS

    def spread(part):
        part = jnp.dot(down, part, preferred_element_type=f32).astype(bf16)
        full = jnp.dot(part, across, preferred_element_type=f32)
        return jnp.where(same, full, 0.0).astype(bf16)

    high = spread(high)
    return high, spread(low), high


def ends_kernel(
    source_hbm, store_hbm, kinds_hbm, cond_hbm, mix_hbm,
    source_ref, store_ref, kinds_ref, edge_ref, side_ref, cond_ref, coef_ref,
    cond_row, mix_rows, sems,
):
    nf, ca, cz, cr = source_ref.shape
    part = nf // COPIES
    pairs_of = [(cond_hbm, cond_row), (mix_hbm, mix_rows)] + [
        (far.at[pl.ds(i * part, part)], near.at[pl.ds(i * part, part)])
        for far, near in ((source_hbm, source_ref), (store_hbm, store_ref))
        for i in range(COPIES)
    ] + [(kinds_hbm, kinds_ref)]
    copies = [pltpu.make_async_copy(far, near, sems.at[i]) for i, (far, near) in enumerate(pairs_of)]
    for copy in copies:
        copy.start()
    place = lax.broadcasted_iota(jnp.int32, (ROWS, cr), 0)

    copies[0].wait()
    copies[1].wait()
    for f in range(nf):
        cond_ref[f] = jnp.broadcast_to(cond_row[:, f : f + 1], (ROWS, cr))
    mats = mix_rows.shape[1]
    mixes = jnp.concatenate([mix_rows[f] for f in range(nf)], axis=0)
    row = lax.broadcasted_iota(jnp.int32, mixes.shape, 0)
    col = lax.broadcasted_iota(jnp.int32, mixes.shape, 1)
    mixes = mixes + jnp.where(row // mats == col, 6.0 * cond_row[...], 0.0)
    inner = nf * ROWS
    for i, rows in enumerate(coef_rows(mixes)):
        coef_ref[:, i * inner : (i + 1) * inner] = rows

    def both(ref, *lead):
        return jnp.where(place < ROWS // 2, ref[(*lead, slice(0, ROWS))], ref[(*lead, slice(cz - ROWS, cz))])

    for f in range(nf):
        if f % part == 0:
            copies[2 + f // part].wait()
        edge_ref[0, f] = source_ref[f, 0] * (INV_CENTER * FIRST_SCALE)
        edge_ref[1, f] = source_ref[f, ca - 1] * (INV_CENTER * FIRST_SCALE)
        for a in range(ca):
            side_ref[f, a] = both(source_ref, f, a) * (INV_CENTER * SIDE_SCALE)
    for copy in copies[2 + COPIES :]:
        copy.wait()
    outer = (place < 2) | (place >= ROWS - 2)
    for f in range(nf // 2):
        for a in range(ca):
            side_ref[nf + f, a] = jnp.where(
                outer, both(store_ref, f, a), swapped(both(store_ref, nf // 2 + f, a))
            ) * SIDE_SCALE
    for a in range(ca):
        side_ref[nf + nf // 2, a] = both(kinds_ref, a).astype(f32) * SIDE_SCALE


def wing_store(wing_ref, f, a):
    nf = wing_ref.shape[0] // 3 * 2
    if f < nf // 2:
        return wing_ref[nf + f, a]
    return swapped(wing_ref[nf // 2 + f, a])


def first_kernel(
    source_ref, store_ref, kinds_ref, wing_ref, cond_ref, coef_ref,
    rest_ref, dir_ref, mix_ref,
):
    nf, ca, cz, cr = source_ref.shape
    own = cz // ROWS
    for f in range(nf):
        for a in range(ca):
            dir_ref[f, a, :cz] = source_ref[f, a] * INV_CENTER
            dir_ref[f, a, cz:] = wing_ref[f, a]

    def store(f, a):
        return jnp.concatenate([store_ref[f, a], wing_store(wing_ref, f, a)], axis=0)

    def kinds(a, t):
        return kinds_ref[a, t * ROWS : (t + 1) * ROWS].astype(f32) if t < own else wing_ref[nf + nf // 2, a]

    def emit(f, a, image):
        origin = jnp.concatenate([source_ref[f, a], center_value * wing_ref[f, a]], axis=0)
        rest_ref[f, a] = origin - image

    apply_local(dir_ref, store, kinds, cond_ref, coef_ref[...], mix_ref, (0, cz + ROWS), emit)


def beside_rows(wing, beside):
    place = lax.broadcasted_iota(jnp.int32, wing.shape, 0)
    moved = jnp.where(place < 4, pltpu.roll(wing, 2, 0), pltpu.roll(wing, 6, 0))
    return jnp.where((place >= 2) & (place <= 5), moved, beside)


KEPT = 6


def put_beside(message_ref, start, rows):
    message_ref[start : start + 1] = rows[:1]
    message_ref[start + 1 : start + 5] = rows[2:6]
    message_ref[start + 5 : start + 6] = rows[7:]


def get_beside(message_ref, start):
    first, inner, last = (message_ref[start + a : start + b] for a, b in ((0, 1), (1, 5), (5, 6)))
    return jnp.concatenate([first, first, inner, last, last], axis=0)


def side_kernel(
    first, flags_ref, rest_ref, halo_ref, source_ref, store_ref, kinds_ref, wing_ref, cond_ref, coef_ref,
    message_ref, dir_ref, next_ref, mix_ref,
):
    nf, ca, cz, cr = source_ref.shape
    even = flags_ref[0] > 0.5

    def choose(low, high):
        mask = tall(even, low.shape[0])
        return jnp.where(mask, low, high) if first else jnp.where(mask, high, low)

    for f in range(nf):
        rest = choose(rest_ref[f, 0], rest_ref[f, ca - 1])
        wing = choose(wing_ref[f, 0], wing_ref[f, ca - 1])
        own = rest[:cz] + tall(cond_ref[f] * (1.0 / FIRST_SCALE), cz) * halo_ref[f]
        direction = (ALPHA[1] * INV_CENTER) * choose(source_ref[f, 0], source_ref[f, ca - 1]) + BETA[1] * own
        beside = ALPHA[1] * wing + BETA[1] * rest[cz:]
        next_ref[f] = (ALPHA[1] * INV_CENTER) * choose(source_ref[f, 1], source_ref[f, ca - 2]) + BETA[1] * choose(
            rest_ref[f, 1, :cz], rest_ref[f, ca - 2, :cz]
        )
        dir_ref[f, 0, :cz] = direction
        dir_ref[f, 0, cz:] = beside
        message_ref[2 * f * cz : (2 * f + 1) * cz] = direction * SECOND_SCALE
        message_ref[(2 * f + 1) * cz : 2 * (f + 1) * cz] = own
        put_beside(message_ref, 2 * nf * cz + KEPT * f, beside_rows(wing, beside) * SECOND_SCALE)

    def kinds(a, t):
        rows = slice(t * ROWS, (t + 1) * ROWS)
        return choose(kinds_ref[0, rows].astype(f32), kinds_ref[ca - 1, rows].astype(f32))

    def emit(f, a, image):
        third = pl.ds((2 * f + 1) * cz, cz)
        rest = message_ref[third] - image + tall(cond_ref[f], cz) * next_ref[f]
        message_ref[third] = (ALPHA[2] * SECOND_SCALE) * dir_ref[f, 0, :cz] + (BETA[2] * SECOND_SCALE) * rest

    apply_local(
        dir_ref, lambda f, a: choose(store_ref[f, 0], store_ref[f, ca - 1]), kinds,
        cond_ref, coef_ref[...], mix_ref, (0, cz), emit,
    )


def second_part(
    flags_ref, rest_ref, halo1_ref, halo0_ref, source_ref, store_ref, kinds_ref, wing_ref, cond_ref, coef_ref,
    newrest_ref, dir_ref, mix_ref,
):
    nf, ca, cz, cr = store_ref.shape
    even = tall(flags_ref[0], cz) > 0.5
    for f in range(nf):
        cond = tall(cond_ref[f] * (1.0 / FIRST_SCALE), cz)
        arrived = {
            0: cond * jnp.where(even, halo1_ref[f], halo0_ref[f]),
            ca - 1: cond * jnp.where(even, halo0_ref[f], halo1_ref[f]),
        }
        for a in range(ca):
            rest = rest_ref[f, a, :cz]
            if a in arrived:
                rest = rest + arrived[a]
            newrest_ref[f, a] = rest
            dir_ref[f, a, :cz] = (ALPHA[1] * INV_CENTER) * source_ref[f, a] + BETA[1] * rest
            dir_ref[f, a, cz:] = ALPHA[1] * wing_ref[f, a] + BETA[1] * rest_ref[f, a, cz:]

    def emit(f, a, image):
        newrest_ref[f, a] = newrest_ref[f, a] - image

    apply_local(
        dir_ref, lambda f, a: store_ref[f, a], lambda a, t: kinds_ref[a, t * ROWS : (t + 1) * ROWS].astype(f32),
        cond_ref, coef_ref[...], mix_ref, (0, cz), emit,
    )


def inward(beside, cz):
    place = lax.broadcasted_iota(jnp.int32, beside.shape, 0)
    ends = [jnp.where(place == 0, pltpu.roll(beside, 1, 0), 0.0)]
    ends += [jnp.zeros_like(beside)] * (cz // ROWS - 2)
    ends += [jnp.where(place == ROWS - 1, pltpu.roll(beside, ROWS - 1, 0), 0.0)]
    return jnp.concatenate(ends, axis=0)


def third_part(
    flags_ref, rest_ref, second_ref, first_rest_ref, source_ref, store_ref, kinds_ref, wing_ref, cond_ref, coef_ref,
    out_ref, total_ref, dir_ref, mix_ref,
):
    nf, ca, cz, cr = source_ref.shape
    partner = {0: flags_ref[1] > 0.5, ca - 1: flags_ref[2] > 0.5}
    for f in range(nf):
        cond = cond_ref[f]
        wide = tall(cond, cz)
        for a in range(ca):
            rest = rest_ref[f, a]
            direction = second_ref[f, a, :cz]
            ahead = ALPHA[2] * direction + BETA[2] * rest
            if a in partner:
                mine = inward(cond * wing_ref[f, a], cz)
                third = BETA[2] * wide * (direction + BETA[1] * mine)
                rest = rest + jnp.where(tall(partner[a], cz), wide * third, 0.0)
            out_ref[f, a] = rest
            dir_ref[f, a, :cz] = ahead
            total_ref[f, a] = source_ref[f, a] * INV_CENTER + direction + ahead

    def wing_emit(f, a, image):
        rest = first_rest_ref[f, a, cz:] - image
        if a in partner:
            cond = cond_ref[f]
            rest = rest + jnp.where(partner[a], BETA[1] * cond * cond * wing_ref[f, a], 0.0)
        dir_ref[f, a, cz:] = ALPHA[2] * second_ref[f, a, cz:] + BETA[2] * rest

    apply_local(
        second_ref, lambda f, a: wing_store(wing_ref, f, a), lambda a, t: wing_ref[nf + nf // 2, a],
        cond_ref, coef_ref[...], mix_ref, (cz, cz + ROWS), wing_emit,
    )

    def emit(f, a, image):
        out_ref[f, a] = out_ref[f, a] - image

    apply_local(
        dir_ref, lambda f, a: store_ref[f, a], lambda a, t: kinds_ref[a, t * ROWS : (t + 1) * ROWS].astype(f32),
        cond_ref, coef_ref[...], mix_ref, (0, cz), emit,
    )


def later_kernel(
    flags_ref, rest_ref, halo1_ref, halo0_ref, source_ref, store_ref, kinds_ref, wing_ref, cond_ref, coef_ref,
    out_ref, total_ref, second_rest_ref, second_ref, dir_ref, mix_ref,
):
    second_part(
        flags_ref, rest_ref, halo1_ref, halo0_ref, source_ref, store_ref, kinds_ref, wing_ref, cond_ref, coef_ref,
        second_rest_ref, second_ref, mix_ref,
    )
    third_part(
        flags_ref, second_rest_ref, second_ref, rest_ref, source_ref, store_ref, kinds_ref, wing_ref, cond_ref,
        coef_ref, out_ref, total_ref, dir_ref, mix_ref,
    )


def end_part(
    first, flags_ref, halo_ref, store_ref, kinds_ref, wing_ref, cond_ref, coef_ref,
    delta_ref, base_ref, fixed_ref, add_ref, beside_ref, mix_ref, early, emit,
):
    nf, ca, cz, cr = store_ref.shape
    even = flags_ref[0] > 0.5

    def choose(low, high):
        mask = tall(even, low.shape[0])
        return jnp.where(mask, low, high) if first else jnp.where(mask, high, low)

    place = lax.broadcasted_iota(jnp.int32, (ROWS, cr), 0)
    outer = (place <= 1) | (place >= 6)
    for f in range(nf):
        cond = cond_ref[f]
        wide = tall(cond, cz)
        scaled = wide * (1.0 / SECOND_SCALE)
        old = get_beside(halo_ref, 2 * nf * cz + KEPT * f) * (1.0 / SECOND_SCALE)
        moved = jnp.where(place < 4, pltpu.roll(old, ROWS - 2, 0), pltpu.roll(old, 2, 0))
        fix = cond * jnp.where(outer, moved, 0.0)
        rest = scaled * halo_ref[2 * f * cz : (2 * f + 1) * cz] + BETA[1] * wide * inward(fix, cz)
        base_ref[f] = rest + scaled * halo_ref[(2 * f + 1) * cz : 2 * (f + 1) * cz]
        fixed_ref[f, 0, :cz] = jnp.zeros_like(rest)
        fixed_ref[f, 0, cz:] = BETA[1] * fix
        beside_ref[f] = fix + cond * old
        add_ref[f, 0, :cz] = BETA[2] * rest
        delta_ref[0, f] = BETA[2] * rest
    early()

    def wing_emit(f, a, image):
        add_ref[f, 0, cz:] = ALPHA[2] * fixed_ref[f, 0, cz:] + BETA[2] * (beside_ref[f] - image)

    def wing_choice(f, a):
        return choose(wing_store(wing_ref, f, 0), wing_store(wing_ref, f, ca - 1))

    def wing_kinds(a, t):
        return choose(wing_ref[nf + nf // 2, 0], wing_ref[nf + nf // 2, ca - 1])

    apply_local(
        fixed_ref, wing_choice, wing_kinds, cond_ref, coef_ref[...], mix_ref, (cz, cz + ROWS), wing_emit, linked=False
    )

    def own_emit(f, a, image):
        cond = cond_ref[f]
        delta_ref[1, f] = base_ref[f] - image
        inner = add_ref[f, 0, :cz] + inward(BETA[2] * cond * fixed_ref[f, 0, cz:], cz)
        delta_ref[2, f] = tall(cond, cz) * inner
        emit(f)

    def kinds(a, t):
        rows = slice(t * ROWS, (t + 1) * ROWS)
        return choose(kinds_ref[0, rows].astype(f32), kinds_ref[ca - 1, rows].astype(f32))

    apply_local(
        add_ref, lambda f, a: choose(store_ref[f, 0], store_ref[f, ca - 1]), kinds,
        cond_ref, coef_ref[...], mix_ref, (0, cz), own_emit, linked=False,
    )


def end_kernel(
    flags_ref, halo_ref, store_ref, kinds_ref, wing_ref, cond_ref, coef_ref,
    delta_ref, base_ref, fixed_ref, add_ref, beside_ref, mix_ref,
):
    end_part(
        False, flags_ref, halo_ref, store_ref, kinds_ref, wing_ref, cond_ref, coef_ref,
        delta_ref, base_ref, fixed_ref, add_ref, beside_ref, mix_ref, lambda: None, lambda f: None,
    )


def last_kernel(
    flags_ref, rest_ref, total_ref, halo_ref, other_ref, store_ref, kinds_ref, wing_ref, cond_ref, coef_ref,
    live_ref, incoming_ref, emission_ref, reflect_ref,
    panel_hbm, solution_ref, residual_ref,
    panel_ref, end_ref, out_ref, delta_ref, base_ref, fixed_ref, add_ref, beside_ref, mix_ref, sems,
):
    nf, ca, cz, cr = store_ref.shape
    even = tall(flags_ref[0], cz) > 0.5
    copies = []

    def send(near, far):
        copies.append(pltpu.make_async_copy(near, far, sems.at[len(copies)]))
        copies[-1].start()

    send(total_ref.at[:, 1 : ca - 1], solution_ref.at[:, 1 : ca - 1])

    def both(i, f):
        one, other = delta_ref[i, f], other_ref[i, f]
        return jnp.where(even, one, other), jnp.where(even, other, one)

    def early():
        for f in range(nf):
            low, high = both(0, f)
            end_ref[0, f] = total_ref[f, 0] + low
            end_ref[1, f] = total_ref[f, ca - 1] + high
        send(end_ref.at[0], solution_ref.at[:, 0])
        send(end_ref.at[1], solution_ref.at[:, ca - 1])
        slots, values = panel_ref.shape
        wall = [end_ref[0, 0]] + [total_ref[0, a] for a in range(1, ca - 1)] + [end_ref[1, 0]]
        wall = jnp.concatenate(wall, axis=0)[:, cr - 1 : cr]
        wall = jnp.broadcast_to(wall, (ca * cz, values))
        wall = jnp.concatenate([wall] * (-(-slots // (ca * cz))), axis=0)[:slots]
        panel = lax.broadcasted_iota(jnp.int32, (slots, values), 0)
        fresh = emission_ref[...] * wall + reflect_ref[...] * incoming_ref[:slots]
        panel_ref[...] = jnp.where(panel < live_ref[:1], fresh, 0.0)
        send(panel_ref, panel_hbm)

    def emit(f):
        low, high = both(1, f)
        out_ref[f, 0] = rest_ref[f, 0] + low
        out_ref[f, ca - 1] = rest_ref[f, ca - 1] + high
        low, high = both(2, f)
        out_ref[f, 1] = rest_ref[f, 1] + low
        for a in range(2, ca - 2):
            out_ref[f, a] = rest_ref[f, a]
        out_ref[f, ca - 2] = rest_ref[f, ca - 2] + high
        if f % GROUP == GROUP - 1:
            some = pl.ds(f + 1 - GROUP, GROUP)
            send(out_ref.at[some], residual_ref.at[some])

    end_part(
        True, flags_ref, halo_ref, store_ref, kinds_ref, wing_ref, cond_ref, coef_ref,
        delta_ref, base_ref, fixed_ref, add_ref, beside_ref, mix_ref, early, emit,
    )
    for copy in copies:
        copy.wait()


def panel_kernel(
    chunk, visible, index_ref, block_ref, rows_ref, view_ref, out_ref
):
    slots = index_ref.shape[1]
    total, values = rows_ref.shape
    index = index_ref[...].T
    block = block_ref[...].T
    types = view_ref.shape[0]
    lane = lax.broadcasted_iota(jnp.int32, (slots, chunk), 1)

    def gather(start):
        rows = rows_ref[pl.ds(start, chunk), :]
        return tuple(
            jnp.dot(
                (index[:, k : k + 1] == lane + start).astype(f32).astype(bf16),
                rows,
                preferred_element_type=f32,
            )
            for k in range(visible)
        )

    if total == chunk:
        found = gather(0)
    else:
        zero = tuple(jnp.zeros((slots, values), f32) for _ in range(visible))

        def step(i, sums):
            return tuple(s + g for s, g in zip(sums, gather(pl.multiple_of(i * chunk, chunk))))

        found = lax.fori_loop(0, total // chunk, step, zero)
    out = jnp.zeros((slots, values), f32)
    for b in range(types):
        stack = jnp.concatenate(
            [jnp.where(block[:, k : k + 1] == b, found[k], 0.0) for k in range(visible)], axis=0
        ).astype(bf16)
        moved = lax.dot_general(
            stack, view_ref[b], (((1,), (1,)), ((), ())), preferred_element_type=f32
        )
        for k in range(visible):
            out = out + moved[k * slots : (k + 1) * slots]
    out_ref[...] = out


def pairs(count, first, closed):
    swaps = []
    for i in range(first, count if closed and first else count - 1, 2):
        j = (i + 1) % count
        swaps += [(i, j), (j, i)]
    return swaps


def swap(array, axis, first, closed=False):
    return lax.ppermute(array, axis, pairs(lax.axis_size(axis), first, closed))


def body(
    source, storage, materials, conductance, mixing, counts, vis_owner, vis_slot, vis_block,
    radiosity_old, view_blocks, emission, reflect,
):
    nf, ca, cz, cr = source.shape
    mats = mixing.shape[0]
    owners = lax.axis_size("axial")
    me = lax.axis_index("axial")
    is_even = me % 2 == 0
    flags = jnp.stack([is_even, me > 0, me + 1 < owners]).astype(f32)
    flags = jnp.broadcast_to(flags[:, None, None], (3, ROWS, cr))
    azim_even = lax.axis_index("azim") % 2 == 0
    here = pltpu.VMEM

    def call(kernel, outs, args, scratch=(), far_out=False, plain_args=False):
        specs = [VMEM] * len(outs)
        if far_out:
            specs[-1] = HBM
        if not plain_args:
            args = [pltpu.with_memory_space_constraint(x, pltpu.VMEM) for x in args]
        single = len(outs) == 1
        return pl.pallas_call(
            kernel,
            out_shape=outs[0] if single else tuple(outs),
            in_specs=[VMEM] * len(args),
            out_specs=specs[0] if single else tuple(specs),
            scratch_shapes=list(scratch),
            compiler_params=PARAMS, cost_estimate=CHEAP,
        )(*args)

    def after(value, *others):
        return lax.optimization_barrier((value, *others))[0]

    plain = here((nf, ca, cz, cr), f32)
    layers = here((2, nf, cz, cr), f32)
    small = (conductance[None], mixing.transpose(1, 0, 2))
    values = radiosity_old.shape[3]
    source, storage, materials, edges, sides, cond, coef = pl.pallas_call(
        ends_kernel,
        out_shape=(
            plain, plain, here((ca, cz, cr), jnp.int32), layers, here((nf + nf // 2 + 1, ca, ROWS, cr), f32),
            here((nf, ROWS, cr), f32), here((mats * nf * ROWS, 3 * nf * ROWS), bf16),
        ),
        in_specs=[HBM] * 5,
        out_specs=(VMEM,) * 7,
        scratch_shapes=[here(x.shape, x.dtype) for x in small] + [pltpu.SemaphoreType.DMA((2 * COPIES + 3,))],
        compiler_params=PARAMS, cost_estimate=CHEAP,
    )(*(pltpu.with_memory_space_constraint(x, pltpu.HBM) for x in (source, storage, materials, *small)))
    edges = jnp.where(is_even, edges, edges[::-1])
    half = ROWS // 2
    to_right, to_left = sides[:, :, half:], sides[:, :, :half]
    far = jnp.where(azim_even, to_left, to_right).astype(LINK)
    near = jnp.where(azim_even, to_right, to_left).astype(LINK)
    slots, visible = vis_owner.shape[2:]
    tile = -(-slots // 16) * 16
    panels = jnp.pad(radiosity_old[0, 0], ((0, tile - slots), (0, 0)))
    fold = cr // values
    folded = panels.astype(f32) * RAD_SCALE
    folded = jnp.concatenate(jnp.split(folded, fold, axis=0), axis=1)
    far = far
    far_in = swap(far, "azim", 1, True)
    layer0 = after(edges, far)[1].reshape(nf * cz, cr)
    message0 = jnp.concatenate([layer0, folded], axis=0).astype(LINK)
    message = swap(message0, "axial", 0)
    near = after(near, message0)
    near_in = swap(near, "azim", 0)
    message1 = after(edges, near)[0].astype(LINK)
    halo1 = swap(message1, "axial", 1)

    from_right = jnp.where(azim_even, near_in, far_in)
    from_left = jnp.where(azim_even, far_in, near_in)
    wings = jnp.concatenate([from_right, from_left], axis=2).astype(f32) * (1.0 / SIDE_SCALE)

    full = here((nf, ca, cz + ROWS, cr), f32)
    rest = call(first_kernel, (full,), (source, storage, materials, wings, cond, coef), (full, full))

    def side(first, halo):
        one = here((nf, 1, cz + ROWS, cr), f32)
        return call(
            functools.partial(side_kernel, first),
            (here((nf * (2 * cz + KEPT), cr), f32),),
            (flags, rest, halo, source, storage, materials, wings, cond, coef),
            (one, here((nf, cz, cr), f32), one),
        ).astype(LINK)

    message = after(message, rest)
    halo0 = message[: nf * cz].reshape(nf, cz, cr).astype(f32)
    message0 = side(False, halo0)
    second0 = swap(message0, "axial", 0).astype(f32)
    halo1 = after(halo1, message0).astype(f32)
    message1 = side(True, halo1)
    second1 = swap(message1, "axial", 1).astype(f32)
    rest3, total = call(
        later_kernel,
        (plain, plain),
        (flags, after(rest, message1), halo1, halo0, source, storage, materials, wings, cond, coef),
        (plain, full, full, full),
    )

    partner = after(message, message1)[nf * cz :].astype(f32) * (1.0 / RAD_SCALE)
    partner = jnp.concatenate(jnp.split(partner, fold, axis=1), axis=0).astype(bf16)
    if owners <= 8 and owners & (owners - 1) == 0:
        pair = jnp.concatenate([panels, partner], axis=0)
        others = [
            lax.ppermute(pair, "axial", [(i, i ^ step) for i in range(owners)]) for step in range(2, owners, 2)
        ]
        panels = jnp.concatenate([after(pair, second0), *others], axis=0)
        owner = vis_owner[0, 0].T ^ me
    else:
        pair = jnp.stack([panels, partner])
        panels = jnp.where(is_even, pair, pair[::-1]).reshape(2 * tile, values)
        groups = [list(range(k, owners, 2)) for k in range(2)]
        panels = lax.all_gather(panels, "axial", axis=0, tiled=True, axis_index_groups=groups)
        panels = panels.reshape(owners // 2, 2 * tile, values).reshape(owners * tile, values)
        owner = vis_owner[0, 0].T
    pad = ((0, -visible % ROWS), (0, -slots % 128))
    index = jnp.pad(owner * tile + vis_slot[0, 0].T, pad, constant_values=-1)
    block = jnp.pad(vis_block[0, 0].T, pad)
    chunk = tile * 8 if owners % 8 == 0 else tile * owners
    incoming = call(
        functools.partial(panel_kernel, chunk, visible),
        (here((index.shape[1], values), f32),),
        (index, block, panels, view_blocks),
        plain_args=True,
    )

    live = jnp.broadcast_to(after(counts, rest3), (ROWS, values))
    shape = jax.ShapeDtypeStruct
    one = here((nf, 1, cz + ROWS, cr), f32)
    deltas = here((3, nf, cz, cr), f32)
    parts = (here((nf, cz, cr), f32), one, one, here((nf, ROWS, cr), f32), one)
    delta0 = call(
        end_kernel, (deltas,), (flags, second0, storage, materials, wings, cond, coef), parts
    )
    panel_new, solution_out, residual = pl.pallas_call(
        last_kernel,
        out_shape=(shape((slots, values), f32), shape(plain.shape, f32), shape(plain.shape, f32)),
        in_specs=[VMEM] * 14,
        out_specs=(HBM, HBM, HBM),
        scratch_shapes=[
            here((slots, values), f32), layers, plain, deltas, *parts, pltpu.SemaphoreType.DMA((4 + nf // GROUP,))
        ],
        compiler_params=PARAMS, cost_estimate=CHEAP,
    )(
        flags, rest3, total, second1, delta0, storage, materials, wings, cond, coef,
        live, incoming, emission[0, 0], reflect[0, 0],
    )
    return (solution_out, residual, panel_new[None, None])


def solution(mesh):
    return jax.shard_map(
        body,
        mesh=mesh,
        in_specs=(
            P(None, "axial", "azim", None),
            P(None, "axial", "azim", None),
            P("axial", "azim", None),
            P(),
            P(),
            P("axial", "azim"),
            P("axial", "azim", None, None),
            P("axial", "azim", None, None),
            P("axial", "azim", None, None),
            P("axial", "azim", None, None),
            P(),
            P("axial", "azim", None, None),
            P("axial", "azim", None, None),
        ),
        out_specs=(
            P(None, "axial", "azim", None),
            P(None, "axial", "azim", None),
            P("axial", "azim", None, None),
        ),
        check_vma=False,
    )
```

```python
import functools
import jax
import jax.numpy as jnp
from jax import lax
from jax.experimental import pallas as pl
from jax.experimental.pallas import tpu as pltpu
from jax.sharding import PartitionSpec as P

center_value = 14.2
half_width = 13.8
sigma = center_value / half_width
ratio_0 = 1.0 / sigma
ratio_1 = 1.0 / (2.0 * sigma - ratio_0)
ratio_2 = 1.0 / (2.0 * sigma - ratio_1)
ALPHA = (None, ratio_1 * ratio_0, ratio_2 * ratio_1)
BETA = (None, 2.0 * ratio_1 / half_width, 2.0 * ratio_2 / half_width)
INV_CENTER = 1.0 / center_value

GROUP = 4
COPIES = 4
ROWS = 8
LINK = jnp.float16
SIDE_SCALE = 2.0**14
FIRST_SCALE = 2.0**15
SECOND_SCALE = 2.0**9
RAD_SCALE = 8192.0
f32, bf16 = jnp.float32, jnp.bfloat16

VMEM = pl.BlockSpec(memory_space=pltpu.VMEM)
HBM = pl.BlockSpec(memory_space=pl.ANY)
PARAMS = pltpu.CompilerParams(vmem_limit_bytes=16 * 1024 * 1024)
CHEAP = pl.CostEstimate(flops=0, bytes_accessed=0, transcendentals=0)


def each_field(count, step):
    for f in range(count):
        step(f)


def tall(tile, height):
    return jnp.concatenate([tile] * (height // ROWS), axis=0)


def mixed_part(cells, kinds, coef, out_ref, a, rows):
    nf, height, cr = cells.shape
    flat = cells.reshape(nf * height, cr)
    high = flat.astype(bf16)
    low = (flat - high.astype(f32)).astype(bf16)
    out = jnp.dot(coef, jnp.concatenate([high, high, low], axis=0), preferred_element_type=f32)
    mats = out.shape[0] // (nf * height)
    out = out.reshape(nf, mats, height, cr)
    is_kind = [kinds == m for m in range(mats - 1)]
    for f in range(nf):
        picked = out[f, mats - 1]
        for m in range(mats - 1):
            picked = jnp.where(is_kind[m], out[f, m], picked)
        out_ref[f, a, rows] = picked


def radial_sum(cells):
    cr = cells.shape[-1]
    lane = lax.broadcasted_iota(jnp.int32, cells.shape, cells.ndim - 1)
    inner = jnp.where(lane == 0, 0.0, pltpu.roll(cells, 1, cells.ndim - 1))
    outer = jnp.where(lane == cr - 1, 0.0, pltpu.roll(cells, cr - 1, cells.ndim - 1))
    return inner + outer


def azim_sum(cells):
    rows = cells.shape[0]
    return pltpu.roll(cells, 1, 0) + pltpu.roll(cells, rows - 1, 0)


def apply_local(dir_ref, store, kinds, cond_ref, coef, mix_ref, span, emit, linked=True):
    nf, ca = dir_ref.shape[:2]
    start, stop = span
    for a in range(ca):
        for t in range(start // ROWS, stop // ROWS):
            rows = slice(t * ROWS, (t + 1) * ROWS)
            mixed_part(dir_ref[:, a, rows], kinds(a, t), coef, mix_ref, a, rows)

    def step(f):
        cond = tall(cond_ref[f], stop - start)
        planes = [dir_ref[f, a] for a in range(ca)]
        for a in range(ca):
            cells = planes[a][start:stop]
            around = azim_sum(planes[a])[start:stop] + radial_sum(cells)
            if linked and a > 0:
                around = around + planes[a - 1][start:stop]
            if linked and a + 1 < ca:
                around = around + planes[a + 1][start:stop]
            emit(f, a, store(f, a) * cells + mix_ref[f, a, start:stop] - cond * around)

    each_field(nf, step)


def swapped(tile):
    place = lax.broadcasted_iota(jnp.int32, tile.shape, 0)
    return jnp.where((place // 2) % 2 == 0, pltpu.roll(tile, ROWS - 2, 0), pltpu.roll(tile, 2, 0))


def coef_rows(mixes):
    tall_rows, nf = mixes.shape
    wide, inner = tall_rows * ROWS, nf * ROWS
    high = mixes.astype(bf16)
    low = (mixes - high.astype(f32)).astype(bf16)
    row = lax.broadcasted_iota(jnp.int32, (wide, tall_rows), 0)
    col = lax.broadcasted_iota(jnp.int32, (wide, tall_rows), 1)
    down = (row // ROWS == col).astype(bf16)
    row = lax.broadcasted_iota(jnp.int32, (nf, inner), 0)
    col = lax.broadcasted_iota(jnp.int32, (nf, inner), 1)
    across = (col // ROWS == row).astype(bf16)
    row = lax.broadcasted_iota(jnp.int32, (wide, inner), 0)
    col = lax.broadcasted_iota(jnp.int32, (wide, inner), 1)
    same = row % ROWS == col % ROWS

    def spread(part):
        part = jnp.dot(down, part, preferred_element_type=f32).astype(bf16)
        full = jnp.dot(part, across, preferred_element_type=f32)
        return jnp.where(same, full, 0.0).astype(bf16)

    high = spread(high)
    return high, spread(low), high


def ends_kernel(
    source_hbm, store_hbm, kinds_hbm, cond_hbm, mix_hbm,
    source_ref, store_ref, kinds_ref, edge_ref, side_ref, cond_ref, coef_ref,
    cond_row, mix_rows, sems,
):
    nf, ca, cz, cr = source_ref.shape
    part = nf // COPIES
    pairs_of = [(cond_hbm, cond_row), (mix_hbm, mix_rows)] + [
        (far.at[pl.ds(i * part, part)], near.at[pl.ds(i * part, part)])
        for far, near in ((source_hbm, source_ref), (store_hbm, store_ref))
        for i in range(COPIES)
    ] + [(kinds_hbm, kinds_ref)]
    copies = [pltpu.make_async_copy(far, near, sems.at[i]) for i, (far, near) in enumerate(pairs_of)]
    for copy in copies:
        copy.start()
    place = lax.broadcasted_iota(jnp.int32, (ROWS, cr), 0)

    copies[0].wait()
    copies[1].wait()
    for f in range(nf):
        cond_ref[f] = jnp.broadcast_to(cond_row[:, f : f + 1], (ROWS, cr))
    mats = mix_rows.shape[1]
    mixes = jnp.concatenate([mix_rows[f] for f in range(nf)], axis=0)
    row = lax.broadcasted_iota(jnp.int32, mixes.shape, 0)
    col = lax.broadcasted_iota(jnp.int32, mixes.shape, 1)
    mixes = mixes + jnp.where(row // mats == col, 6.0 * cond_row[...], 0.0)
    inner = nf * ROWS
    for i, rows in enumerate(coef_rows(mixes)):
        coef_ref[:, i * inner : (i + 1) * inner] = rows

    def both(ref, *lead):
        return jnp.where(place < ROWS // 2, ref[(*lead, slice(0, ROWS))], ref[(*lead, slice(cz - ROWS, cz))])

    for f in range(nf):
        if f % part == 0:
            copies[2 + f // part].wait()
        edge_ref[0, f] = source_ref[f, 0] * (INV_CENTER * FIRST_SCALE)
        edge_ref[1, f] = source_ref[f, ca - 1] * (INV_CENTER * FIRST_SCALE)
        for a in range(ca):
            side_ref[f, a] = both(source_ref, f, a) * (INV_CENTER * SIDE_SCALE)
    for copy in copies[2 + COPIES :]:
        copy.wait()
    outer = (place < 2) | (place >= ROWS - 2)
    for f in range(nf // 2):
        for a in range(ca):
            side_ref[nf + f, a] = jnp.where(
                outer, both(store_ref, f, a), swapped(both(store_ref, nf // 2 + f, a))
            ) * SIDE_SCALE
    for a in range(ca):
        side_ref[nf + nf // 2, a] = both(kinds_ref, a).astype(f32) * SIDE_SCALE


def wing_store(wing_ref, f, a):
    nf = wing_ref.shape[0] // 3 * 2
    if f < nf // 2:
        return wing_ref[nf + f, a]
    return swapped(wing_ref[nf // 2 + f, a])


def first_kernel(
    source_ref, store_ref, kinds_ref, wing_ref, cond_ref, coef_ref,
    rest_ref, dir_ref, mix_ref,
):
    nf, ca, cz, cr = source_ref.shape
    own = cz // ROWS
    for f in range(nf):
        for a in range(ca):
            dir_ref[f, a, :cz] = source_ref[f, a] * INV_CENTER
            dir_ref[f, a, cz:] = wing_ref[f, a]

    def store(f, a):
        return jnp.concatenate([store_ref[f, a], wing_store(wing_ref, f, a)], axis=0)

    def kinds(a, t):
        return kinds_ref[a, t * ROWS : (t + 1) * ROWS].astype(f32) if t < own else wing_ref[nf + nf // 2, a]

    def emit(f, a, image):
        origin = jnp.concatenate([source_ref[f, a], center_value * wing_ref[f, a]], axis=0)
        rest_ref[f, a] = origin - image

    apply_local(dir_ref, store, kinds, cond_ref, coef_ref[...], mix_ref, (0, cz + ROWS), emit)


def beside_rows(wing, beside):
    place = lax.broadcasted_iota(jnp.int32, wing.shape, 0)
    moved = jnp.where(place < 4, pltpu.roll(wing, 2, 0), pltpu.roll(wing, 6, 0))
    return jnp.where((place >= 2) & (place <= 5), moved, beside)


KEPT = 6


def put_beside(message_ref, start, rows):
    message_ref[start : start + 1] = rows[:1]
    message_ref[start + 1 : start + 5] = rows[2:6]
    message_ref[start + 5 : start + 6] = rows[7:]


def get_beside(message_ref, start):
    first, inner, last = (message_ref[start + a : start + b] for a, b in ((0, 1), (1, 5), (5, 6)))
    return jnp.concatenate([first, first, inner, last, last], axis=0)


def side_kernel(
    first, flags_ref, rest_ref, halo_ref, source_ref, store_ref, kinds_ref, wing_ref, cond_ref, coef_ref,
    message_ref, dir_ref, next_ref, mix_ref,
):
    nf, ca, cz, cr = source_ref.shape
    even = flags_ref[0] > 0.5

    def choose(low, high):
        mask = tall(even, low.shape[0])
        return jnp.where(mask, low, high) if first else jnp.where(mask, high, low)

    for f in range(nf):
        rest = choose(rest_ref[f, 0], rest_ref[f, ca - 1])
        wing = choose(wing_ref[f, 0], wing_ref[f, ca - 1])
        own = rest[:cz] + tall(cond_ref[f] * (1.0 / FIRST_SCALE), cz) * halo_ref[f]
        direction = (ALPHA[1] * INV_CENTER) * choose(source_ref[f, 0], source_ref[f, ca - 1]) + BETA[1] * own
        beside = ALPHA[1] * wing + BETA[1] * rest[cz:]
        next_ref[f] = (ALPHA[1] * INV_CENTER) * choose(source_ref[f, 1], source_ref[f, ca - 2]) + BETA[1] * choose(
            rest_ref[f, 1, :cz], rest_ref[f, ca - 2, :cz]
        )
        dir_ref[f, 0, :cz] = direction
        dir_ref[f, 0, cz:] = beside
        message_ref[2 * f * cz : (2 * f + 1) * cz] = direction * SECOND_SCALE
        message_ref[(2 * f + 1) * cz : 2 * (f + 1) * cz] = own
        put_beside(message_ref, 2 * nf * cz + KEPT * f, beside_rows(wing, beside) * SECOND_SCALE)

    def kinds(a, t):
        rows = slice(t * ROWS, (t + 1) * ROWS)
        return choose(kinds_ref[0, rows].astype(f32), kinds_ref[ca - 1, rows].astype(f32))

    def emit(f, a, image):
        third = pl.ds((2 * f + 1) * cz, cz)
        rest = message_ref[third] - image + tall(cond_ref[f], cz) * next_ref[f]
        message_ref[third] = (ALPHA[2] * SECOND_SCALE) * dir_ref[f, 0, :cz] + (BETA[2] * SECOND_SCALE) * rest

    apply_local(
        dir_ref, lambda f, a: choose(store_ref[f, 0], store_ref[f, ca - 1]), kinds,
        cond_ref, coef_ref[...], mix_ref, (0, cz), emit,
    )


def second_part(
    flags_ref, rest_ref, halo1_ref, halo0_ref, source_ref, store_ref, kinds_ref, wing_ref, cond_ref, coef_ref,
    newrest_ref, dir_ref, mix_ref,
):
    nf, ca, cz, cr = store_ref.shape
    even = tall(flags_ref[0], cz) > 0.5
    for f in range(nf):
        cond = tall(cond_ref[f] * (1.0 / FIRST_SCALE), cz)
        arrived = {
            0: cond * jnp.where(even, halo1_ref[f], halo0_ref[f]),
            ca - 1: cond * jnp.where(even, halo0_ref[f], halo1_ref[f]),
        }
        for a in range(ca):
            rest = rest_ref[f, a, :cz]
            if a in arrived:
                rest = rest + arrived[a]
            newrest_ref[f, a] = rest
            dir_ref[f, a, :cz] = (ALPHA[1] * INV_CENTER) * source_ref[f, a] + BETA[1] * rest
            dir_ref[f, a, cz:] = ALPHA[1] * wing_ref[f, a] + BETA[1] * rest_ref[f, a, cz:]

    def emit(f, a, image):
        newrest_ref[f, a] = newrest_ref[f, a] - image

    apply_local(
        dir_ref, lambda f, a: store_ref[f, a], lambda a, t: kinds_ref[a, t * ROWS : (t + 1) * ROWS].astype(f32),
        cond_ref, coef_ref[...], mix_ref, (0, cz), emit,
    )


def inward(beside, cz):
    place = lax.broadcasted_iota(jnp.int32, beside.shape, 0)
    ends = [jnp.where(place == 0, pltpu.roll(beside, 1, 0), 0.0)]
    ends += [jnp.zeros_like(beside)] * (cz // ROWS - 2)
    ends += [jnp.where(place == ROWS - 1, pltpu.roll(beside, ROWS - 1, 0), 0.0)]
    return jnp.concatenate(ends, axis=0)


def third_part(
    flags_ref, rest_ref, second_ref, first_rest_ref, source_ref, store_ref, kinds_ref, wing_ref, cond_ref, coef_ref,
    out_ref, total_ref, dir_ref, mix_ref,
):
    nf, ca, cz, cr = source_ref.shape
    partner = {0: flags_ref[1] > 0.5, ca - 1: flags_ref[2] > 0.5}
    for f in range(nf):
        cond = cond_ref[f]
        wide = tall(cond, cz)
        for a in range(ca):
            rest = rest_ref[f, a]
            direction = second_ref[f, a, :cz]
            ahead = ALPHA[2] * direction + BETA[2] * rest
            if a in partner:
                mine = inward(cond * wing_ref[f, a], cz)
                third = BETA[2] * wide * (direction + BETA[1] * mine)
                rest = rest + jnp.where(tall(partner[a], cz), wide * third, 0.0)
            out_ref[f, a] = rest
            dir_ref[f, a, :cz] = ahead
            total_ref[f, a] = source_ref[f, a] * INV_CENTER + direction + ahead

    def wing_emit(f, a, image):
        rest = first_rest_ref[f, a, cz:] - image
        if a in partner:
            cond = cond_ref[f]
            rest = rest + jnp.where(partner[a], BETA[1] * cond * cond * wing_ref[f, a], 0.0)
        dir_ref[f, a, cz:] = ALPHA[2] * second_ref[f, a, cz:] + BETA[2] * rest

    apply_local(
        second_ref, lambda f, a: wing_store(wing_ref, f, a), lambda a, t: wing_ref[nf + nf // 2, a],
        cond_ref, coef_ref[...], mix_ref, (cz, cz + ROWS), wing_emit,
    )

    def emit(f, a, image):
        out_ref[f, a] = out_ref[f, a] - image

    apply_local(
        dir_ref, lambda f, a: store_ref[f, a], lambda a, t: kinds_ref[a, t * ROWS : (t + 1) * ROWS].astype(f32),
        cond_ref, coef_ref[...], mix_ref, (0, cz), emit,
    )


def later_kernel(
    flags_ref, rest_ref, halo1_ref, halo0_ref, source_ref, store_ref, kinds_ref, wing_ref, cond_ref, coef_ref,
    out_ref, total_ref, second_rest_ref, second_ref, dir_ref, mix_ref,
):
    second_part(
        flags_ref, rest_ref, halo1_ref, halo0_ref, source_ref, store_ref, kinds_ref, wing_ref, cond_ref, coef_ref,
        second_rest_ref, second_ref, mix_ref,
    )
    third_part(
        flags_ref, second_rest_ref, second_ref, rest_ref, source_ref, store_ref, kinds_ref, wing_ref, cond_ref,
        coef_ref, out_ref, total_ref, dir_ref, mix_ref,
    )


def end_part(
    first, flags_ref, halo_ref, store_ref, kinds_ref, wing_ref, cond_ref, coef_ref,
    delta_ref, base_ref, fixed_ref, add_ref, beside_ref, mix_ref, early, emit,
):
    nf, ca, cz, cr = store_ref.shape
    even = flags_ref[0] > 0.5

    def choose(low, high):
        mask = tall(even, low.shape[0])
        return jnp.where(mask, low, high) if first else jnp.where(mask, high, low)

    place = lax.broadcasted_iota(jnp.int32, (ROWS, cr), 0)
    outer = (place <= 1) | (place >= 6)
    for f in range(nf):
        cond = cond_ref[f]
        wide = tall(cond, cz)
        scaled = wide * (1.0 / SECOND_SCALE)
        old = get_beside(halo_ref, 2 * nf * cz + KEPT * f) * (1.0 / SECOND_SCALE)
        moved = jnp.where(place < 4, pltpu.roll(old, ROWS - 2, 0), pltpu.roll(old, 2, 0))
        fix = cond * jnp.where(outer, moved, 0.0)
        rest = scaled * halo_ref[2 * f * cz : (2 * f + 1) * cz] + BETA[1] * wide * inward(fix, cz)
        base_ref[f] = rest + scaled * halo_ref[(2 * f + 1) * cz : 2 * (f + 1) * cz]
        fixed_ref[f, 0, :cz] = jnp.zeros_like(rest)
        fixed_ref[f, 0, cz:] = BETA[1] * fix
        beside_ref[f] = fix + cond * old
        add_ref[f, 0, :cz] = BETA[2] * rest
        delta_ref[0, f] = BETA[2] * rest
    early()

    def wing_emit(f, a, image):
        add_ref[f, 0, cz:] = ALPHA[2] * fixed_ref[f, 0, cz:] + BETA[2] * (beside_ref[f] - image)

    def wing_choice(f, a):
        return choose(wing_store(wing_ref, f, 0), wing_store(wing_ref, f, ca - 1))

    def wing_kinds(a, t):
        return choose(wing_ref[nf + nf // 2, 0], wing_ref[nf + nf // 2, ca - 1])

    apply_local(
        fixed_ref, wing_choice, wing_kinds, cond_ref, coef_ref[...], mix_ref, (cz, cz + ROWS), wing_emit, linked=False
    )

    def own_emit(f, a, image):
        cond = cond_ref[f]
        delta_ref[1, f] = base_ref[f] - image
        inner = add_ref[f, 0, :cz] + inward(BETA[2] * cond * fixed_ref[f, 0, cz:], cz)
        delta_ref[2, f] = tall(cond, cz) * inner
        emit(f)

    def kinds(a, t):
        rows = slice(t * ROWS, (t + 1) * ROWS)
        return choose(kinds_ref[0, rows].astype(f32), kinds_ref[ca - 1, rows].astype(f32))

    apply_local(
        add_ref, lambda f, a: choose(store_ref[f, 0], store_ref[f, ca - 1]), kinds,
        cond_ref, coef_ref[...], mix_ref, (0, cz), own_emit, linked=False,
    )


def end_kernel(
    flags_ref, halo_ref, store_ref, kinds_ref, wing_ref, cond_ref, coef_ref,
    delta_ref, base_ref, fixed_ref, add_ref, beside_ref, mix_ref,
):
    end_part(
        False, flags_ref, halo_ref, store_ref, kinds_ref, wing_ref, cond_ref, coef_ref,
        delta_ref, base_ref, fixed_ref, add_ref, beside_ref, mix_ref, lambda: None, lambda f: None,
    )


def last_kernel(
    flags_ref, rest_ref, total_ref, halo_ref, other_ref, store_ref, kinds_ref, wing_ref, cond_ref, coef_ref,
    live_ref, incoming_ref, emission_ref, reflect_ref,
    panel_hbm, solution_ref, residual_ref,
    panel_ref, end_ref, out_ref, delta_ref, base_ref, fixed_ref, add_ref, beside_ref, mix_ref, sems,
):
    nf, ca, cz, cr = store_ref.shape
    even = tall(flags_ref[0], cz) > 0.5
    copies = []

    def send(near, far):
        copies.append(pltpu.make_async_copy(near, far, sems.at[len(copies)]))
        copies[-1].start()

    send(total_ref.at[:, 1 : ca - 1], solution_ref.at[:, 1 : ca - 1])

    def both(i, f):
        one, other = delta_ref[i, f], other_ref[i, f]
        return jnp.where(even, one, other), jnp.where(even, other, one)

    def early():
        for f in range(nf):
            low, high = both(0, f)
            end_ref[0, f] = total_ref[f, 0] + low
            end_ref[1, f] = total_ref[f, ca - 1] + high
        send(end_ref.at[0], solution_ref.at[:, 0])
        send(end_ref.at[1], solution_ref.at[:, ca - 1])
        slots, values = panel_ref.shape
        wall = [end_ref[0, 0]] + [total_ref[0, a] for a in range(1, ca - 1)] + [end_ref[1, 0]]
        wall = jnp.concatenate(wall, axis=0)[:, cr - 1 : cr]
        wall = jnp.broadcast_to(wall, (ca * cz, values))
        wall = jnp.concatenate([wall] * (-(-slots // (ca * cz))), axis=0)[:slots]
        panel = lax.broadcasted_iota(jnp.int32, (slots, values), 0)
        fresh = emission_ref[...] * wall + reflect_ref[...] * incoming_ref[:slots]
        panel_ref[...] = jnp.where(panel < live_ref[:1], fresh, 0.0)
        send(panel_ref, panel_hbm)

    def emit(f):
        low, high = both(1, f)
        out_ref[f, 0] = rest_ref[f, 0] + low
        out_ref[f, ca - 1] = rest_ref[f, ca - 1] + high
        low, high = both(2, f)
        out_ref[f, 1] = rest_ref[f, 1] + low
        for a in range(2, ca - 2):
            out_ref[f, a] = rest_ref[f, a]
        out_ref[f, ca - 2] = rest_ref[f, ca - 2] + high
        if f % GROUP == GROUP - 1:
            some = pl.ds(f + 1 - GROUP, GROUP)
            send(out_ref.at[some], residual_ref.at[some])

    end_part(
        True, flags_ref, halo_ref, store_ref, kinds_ref, wing_ref, cond_ref, coef_ref,
        delta_ref, base_ref, fixed_ref, add_ref, beside_ref, mix_ref, early, emit,
    )
    for copy in copies:
        copy.wait()


def panel_kernel(
    chunk, visible, index_ref, block_ref, rows_ref, view_ref, out_ref
):
    slots = index_ref.shape[1]
    total, values = rows_ref.shape
    index = index_ref[...].T
    block = block_ref[...].T
    types = view_ref.shape[0]
    lane = lax.broadcasted_iota(jnp.int32, (slots, chunk), 1)

    def gather(start):
        rows = rows_ref[pl.ds(start, chunk), :]
        return tuple(
            jnp.dot(
                (index[:, k : k + 1] == lane + start).astype(f32).astype(bf16),
                rows,
                preferred_element_type=f32,
            )
            for k in range(visible)
        )

    if total == chunk:
        found = gather(0)
    else:
        zero = tuple(jnp.zeros((slots, values), f32) for _ in range(visible))

        def step(i, sums):
            return tuple(s + g for s, g in zip(sums, gather(pl.multiple_of(i * chunk, chunk))))

        found = lax.fori_loop(0, total // chunk, step, zero)
    out = jnp.zeros((slots, values), f32)
    for b in range(types):
        stack = jnp.concatenate(
            [jnp.where(block[:, k : k + 1] == b, found[k], 0.0) for k in range(visible)], axis=0
        ).astype(bf16)
        moved = lax.dot_general(
            stack, view_ref[b], (((1,), (1,)), ((), ())), preferred_element_type=f32
        )
        for k in range(visible):
            out = out + moved[k * slots : (k + 1) * slots]
    out_ref[...] = out


def pairs(count, first, closed):
    swaps = []
    for i in range(first, count if closed and first else count - 1, 2):
        j = (i + 1) % count
        swaps += [(i, j), (j, i)]
    return swaps


def swap(array, axis, first, closed=False):
    return lax.ppermute(array, axis, pairs(lax.axis_size(axis), first, closed))


def body(
    source, storage, materials, conductance, mixing, counts, vis_owner, vis_slot, vis_block,
    radiosity_old, view_blocks, emission, reflect,
):
    nf, ca, cz, cr = source.shape
    mats = mixing.shape[0]
    owners = lax.axis_size("axial")
    me = lax.axis_index("axial")
    is_even = me % 2 == 0
    flags = jnp.stack([is_even, me > 0, me + 1 < owners]).astype(f32)
    flags = jnp.broadcast_to(flags[:, None, None], (3, ROWS, cr))
    azim_even = lax.axis_index("azim") % 2 == 0
    here = pltpu.VMEM

    def call(kernel, outs, args, scratch=(), far_out=False, plain_args=False):
        specs = [VMEM] * len(outs)
        if far_out:
            specs[-1] = HBM
        if not plain_args:
            args = [pltpu.with_memory_space_constraint(x, pltpu.VMEM) for x in args]
        single = len(outs) == 1
        return pl.pallas_call(
            kernel,
            out_shape=outs[0] if single else tuple(outs),
            in_specs=[VMEM] * len(args),
            out_specs=specs[0] if single else tuple(specs),
            scratch_shapes=list(scratch),
            compiler_params=PARAMS, cost_estimate=CHEAP,
        )(*args)

    def after(value, *others):
        return lax.optimization_barrier((value, *others))[0]

    plain = here((nf, ca, cz, cr), f32)
    layers = here((2, nf, cz, cr), f32)
    small = (conductance[None], mixing.transpose(1, 0, 2))
    values = radiosity_old.shape[3]
    source, storage, materials, edges, sides, cond, coef = pl.pallas_call(
        ends_kernel,
        out_shape=(
            plain, plain, here((ca, cz, cr), jnp.int32), layers, here((nf + nf // 2 + 1, ca, ROWS, cr), f32),
            here((nf, ROWS, cr), f32), here((mats * nf * ROWS, 3 * nf * ROWS), bf16),
        ),
        in_specs=[HBM] * 5,
        out_specs=(VMEM,) * 7,
        scratch_shapes=[here(x.shape, x.dtype) for x in small] + [pltpu.SemaphoreType.DMA((2 * COPIES + 3,))],
        compiler_params=PARAMS, cost_estimate=CHEAP,
    )(*(pltpu.with_memory_space_constraint(x, pltpu.HBM) for x in (source, storage, materials, *small)))
    edges = jnp.where(is_even, edges, edges[::-1])
    half = ROWS // 2
    to_right, to_left = sides[:, :, half:], sides[:, :, :half]
    far = jnp.where(azim_even, to_left, to_right).astype(LINK)
    near = jnp.where(azim_even, to_right, to_left).astype(LINK)
    slots, visible = vis_owner.shape[2:]
    tile = -(-slots // 16) * 16
    panels = jnp.pad(radiosity_old[0, 0], ((0, tile - slots), (0, 0)))
    fold = cr // values
    folded = panels.astype(f32) * RAD_SCALE
    folded = jnp.concatenate(jnp.split(folded, fold, axis=0), axis=1)
    far_in = swap(far, "azim", 1, True)
    layer0 = after(edges, far)[1].reshape(nf * cz, cr)
    message0 = jnp.concatenate([layer0, folded], axis=0).astype(LINK)
    message = swap(message0, "axial", 0)
    near = after(near, message0)
    near_in = swap(near, "azim", 0)
    message1 = after(edges, near)[0].astype(LINK)
    halo1 = swap(message1, "axial", 1)

    from_right = jnp.where(azim_even, near_in, far_in)
    from_left = jnp.where(azim_even, far_in, near_in)
    wings = jnp.concatenate([from_right, from_left], axis=2).astype(f32) * (1.0 / SIDE_SCALE)

    full = here((nf, ca, cz + ROWS, cr), f32)
    rest = call(first_kernel, (full,), (source, storage, materials, wings, cond, coef), (full, full))

    def side(first, halo):
        one = here((nf, 1, cz + ROWS, cr), f32)
        return call(
            functools.partial(side_kernel, first),
            (here((nf * (2 * cz + KEPT), cr), f32),),
            (flags, rest, halo, source, storage, materials, wings, cond, coef),
            (one, here((nf, cz, cr), f32), one),
        ).astype(LINK)

    message = after(message, rest)
    halo0 = message[: nf * cz].reshape(nf, cz, cr).astype(f32)
    message0 = side(False, halo0)
    second0 = swap(message0, "axial", 0).astype(f32)
    halo1 = after(halo1, message0).astype(f32)
    message1 = side(True, halo1)
    second1 = swap(message1, "axial", 1).astype(f32)
    rest3, total = call(
        later_kernel,
        (plain, plain),
        (flags, after(rest, message1), halo1, halo0, source, storage, materials, wings, cond, coef),
        (plain, full, full, full),
    )

    partner = after(message, message1)[nf * cz :].astype(f32) * (1.0 / RAD_SCALE)
    partner = jnp.concatenate(jnp.split(partner, fold, axis=1), axis=0).astype(bf16)[:slots]
    panels = panels[:slots]
    if owners <= 8 and owners & (owners - 1) == 0:
        pair = jnp.concatenate([panels, partner], axis=0)
        others = [
            lax.ppermute(pair, "axial", [(i, i ^ step) for i in range(owners)]) for step in range(2, owners, 2)
        ]
        panels = jnp.concatenate([after(pair, second0), *others], axis=0)
        owner = vis_owner[0, 0].T ^ me
    else:
        pair = jnp.stack([panels, partner])
        panels = jnp.where(is_even, pair, pair[::-1]).reshape(2 * slots, values)
        groups = [list(range(k, owners, 2)) for k in range(2)]
        panels = lax.all_gather(panels, "axial", axis=0, tiled=True, axis_index_groups=groups)
        owner = vis_owner[0, 0].T
    pad = ((0, -visible % ROWS), (0, -slots % 128))
    index = jnp.pad(owner * slots + vis_slot[0, 0].T, pad, constant_values=-1)
    block = jnp.pad(vis_block[0, 0].T, pad)
    chunk = slots * 8 if owners % 8 == 0 else slots * owners
    incoming = call(
        functools.partial(panel_kernel, chunk, visible),
        (here((index.shape[1], values), f32),),
        (index, block, panels, view_blocks),
        plain_args=True,
    )

    live = jnp.broadcast_to(after(counts, rest3), (ROWS, values))
    shape = jax.ShapeDtypeStruct
    one = here((nf, 1, cz + ROWS, cr), f32)
    deltas = here((3, nf, cz, cr), f32)
    parts = (here((nf, cz, cr), f32), one, one, here((nf, ROWS, cr), f32), one)
    delta0 = call(
        end_kernel, (deltas,), (flags, second0, storage, materials, wings, cond, coef), parts
    )
    panel_new, solution_out, residual = pl.pallas_call(
        last_kernel,
        out_shape=(shape((slots, values), f32), shape(plain.shape, f32), shape(plain.shape, f32)),
        in_specs=[VMEM] * 14,
        out_specs=(HBM, HBM, HBM),
        scratch_shapes=[
            here((slots, values), f32), layers, plain, deltas, *parts, pltpu.SemaphoreType.DMA((4 + nf // GROUP,))
        ],
        compiler_params=PARAMS, cost_estimate=CHEAP,
    )(
        flags, rest3, total, second1, delta0, storage, materials, wings, cond, coef,
        live, incoming, emission[0, 0], reflect[0, 0],
    )
    return (solution_out, residual, panel_new[None, None])


def solution(mesh):
    return jax.shard_map(
        body,
        mesh=mesh,
        in_specs=(
            P(None, "axial", "azim", None),
            P(None, "axial", "azim", None),
            P("axial", "azim", None),
            P(),
            P(),
            P("axial", "azim"),
            P("axial", "azim", None, None),
            P("axial", "azim", None, None),
            P("axial", "azim", None, None),
            P("axial", "azim", None, None),
            P(),
            P("axial", "azim", None, None),
            P("axial", "azim", None, None),
        ),
        out_specs=(
            P(None, "axial", "azim", None),
            P(None, "axial", "azim", None),
            P("axial", "azim", None, None),
        ),
        check_vma=False,
    )
```
